256 devices in a mesh: ctx: 32 (over z, x), head: 8 (over y, core).
Axes of the slice: x: 4, y: 4, z: 8, core: 2. Of those that a mesh axis runs over, the one named last changes fastest.
Arguments:
- hidden: bfloat16 [8192, 2304], P('ctx', 'head'), may hold values from -10 to 10
- qkv_weight: bfloat16 [3, 2304, 4096], P(None, None, 'head'), may hold values from -0.125 to 0.125
- conv_weight: float32 [4, 3, 4096], P(None, None, 'head'), may hold values from -2 to 2
- w_beta: bfloat16 [2304, 32], P(None, 'head'), may hold values from -1 to 1
- gate_down: bfloat16 [2304, 128], replicated, may hold values from -0.125 to 0.125
- gate_up: bfloat16 [128, 4096], P(None, 'head'), may hold values from -0.5 to 0.5
- a_log: float32 [32], P('head'), may hold values from -30 to -2
- dt_bias: float32 [4096], P('head'), may hold values from -3 to 3
- norm_gain: float32 [128], replicated, may hold values from 0.25 to 1.75
- prompt_lengths: int32 [4], replicated, may hold values from 1 to 7424, 8192 in all
- send_slot: int32 [8192], P('ctx'), may hold values from 0 to 511, as said below
- gather_src: int32 [8192], P('ctx'), may hold values from 0 to 511, as said below
Outputs:
- attention: bfloat16 [8192, 4096], P('ctx', 'head')
The draws below stay inside these ranges and needn't reach their ends.
Inputs may be any that keep to these rules, and one draw needn't show every extreme that they name: `send_slot`: slot d * 16 + place of the row's context device d; the rows of one owner name distinct slots, at most 16 rows of one owner go to one context device, every context device receives 256 rows in all, and some owner fills all 16 slots for some context device. `gather_src`: received slot o * 16 + place, o the sending owner; the entries of one context device are distinct and name exactly the slots that owners filled for it.
All inputs are finite; a program needn't handle non-finite values.
Results may differ from the reference program's by a relative error of at most 0.0045.
Values may be sent and summed in bfloat16 or wider, within the bound.
A program may use at most 128 MiB of HBM per device.

```python
import math
import jax
import jax.numpy as jnp
import numpy as np
from jax import lax

D = 2304
HEADS = 32
HEAD_DIM = 128
GATE_RANK = 128
CONV = 4
SPAN = 64
TOK_DEV = 256
PROMPTS = 4
TOKENS = 8192
CAP = 16
LONGEST = 7424
N_CTX = 32


def placement_tables(key):
    ctx_count = N_CTX
    owned_rows = TOK_DEV
    even_share = owned_rows // ctx_count
    capacity = 2 * even_share
    subkeys = jax.random.split(key, 6)
    pairing = jax.random.permutation(subkeys[0], ctx_count)
    excess = jax.random.randint(subkeys[1], (ctx_count // 2,), 0, even_share + 1).at[0].set(even_share)
    shifts = jnp.zeros((ctx_count,), jnp.int32).at[pairing[0::2]].set(excess).at[pairing[1::2]].set(-excess)
    slot_weights = even_share + shifts
    owner_turn = jax.random.permutation(subkeys[2], ctx_count)
    target_turn = jax.random.permutation(subkeys[3], ctx_count)
    pair_counts = slot_weights[(target_turn[None, :] - owner_turn[:, None]) % ctx_count]
    slot_rank = jnp.arange(owned_rows, dtype=jnp.int32)
    owner_index = jnp.arange(ctx_count)[:, None]
    send_ends = jnp.cumsum(pair_counts, axis=1)
    send_starts = send_ends - pair_counts
    destination = jnp.sum((send_ends[:, None, :] <= slot_rank[None, :, None]).astype(jnp.int32), axis=2)
    slot_place = slot_rank[None, :] - jnp.take_along_axis(send_starts, destination, axis=1)
    encoded = destination * capacity + slot_place
    owner_orders = jax.vmap(lambda subkey: jax.random.permutation(subkey, owned_rows))(jax.random.split(subkeys[4], ctx_count))
    send_table = jnp.zeros((ctx_count, owned_rows), jnp.int32).at[owner_index, owner_orders].set(encoded)
    recv_ends = jnp.cumsum(pair_counts, axis=0).T
    recv_starts = recv_ends - pair_counts.T
    sender = jnp.sum((recv_ends[:, None, :] <= slot_rank[None, :, None]).astype(jnp.int32), axis=2)
    place_in = slot_rank[None, :] - jnp.take_along_axis(recv_starts, sender, axis=1)
    received = sender * capacity + place_in
    packed_orders = jax.vmap(lambda subkey: jax.random.permutation(subkey, owned_rows))(jax.random.split(subkeys[5], ctx_count))
    gather_table = jnp.zeros((ctx_count, owned_rows), jnp.int32).at[owner_index, packed_orders].set(received)
    return (send_table.reshape(TOKENS).astype(jnp.int32), gather_table.reshape(TOKENS).astype(jnp.int32))


def head_slowness(key, cut):
    subkeys = jax.random.split(jax.random.fold_in(key, 101), 2)
    head_order = jax.random.permutation(subkeys[0], HEADS)
    head_ranks = jnp.zeros((HEADS,), jnp.int32).at[head_order].set(jnp.arange(HEADS, dtype=jnp.int32))
    spread = (head_ranks.astype(jnp.float32) + jax.random.uniform(subkeys[1], (HEADS,), jnp.float32)) / HEADS
    return jnp.minimum(spread / cut, 1.0).astype(jnp.float32)


def outlier_mean(key, amplitude):
    subkeys = jax.random.split(jax.random.fold_in(key, 202), 2)
    chosen = jax.random.permutation(subkeys[0], D)[:8]
    signs = jnp.where(jax.random.randint(subkeys[1], (8,), 0, 2) == 0, -1.0, 1.0).astype(jnp.float32)
    return jnp.zeros((D,), jnp.float32).at[chosen].set(signs * amplitude)


def draw_send_slot(key, part):
    tables = placement_tables(key)
    return tables[0]


def draw_gather_src(key, part):
    tables = placement_tables(key)
    return tables[1]


def draw_hidden(key, part):
    shared = outlier_mean(key, 4.0)
    key = jax.random.fold_in(key, 13)
    noise = jax.random.truncated_normal(key, -6.0, 6.0, (TOKENS, D), jnp.float32)
    return (noise + shared[None, :]).astype(jnp.bfloat16)


def draw_w_beta(key, part):
    shared = outlier_mean(key, 4.0)
    slowness = head_slowness(key, 0.5)
    key = jax.random.fold_in(key, 17)
    noise = jax.random.truncated_normal(key, -6.0, 6.0, (D, HEADS), jnp.float32)
    target = -5.5 * slowness
    offset = shared[:, None] * target[None, :] / (8.0 * 16.0)
    return (noise * D ** (-0.5) + offset).astype(jnp.bfloat16)


def draw_a_log(key, part):
    slowness = head_slowness(key, 0.5)
    key = jax.random.fold_in(key, 11)
    subkeys = jax.random.split(key, 3)
    slow_rate = jnp.log(0.5 / TOKENS) + jax.random.uniform(subkeys[1], (HEADS,), jnp.float32, -1.0, 1.0)
    fast_rate = jnp.log(0.04) + jax.random.uniform(subkeys[2], (HEADS,), jnp.float32, -0.5, 0.5)
    return (fast_rate + slowness * (slow_rate - fast_rate)).astype(jnp.float32)


def shard_levels(rng, extent, cuts, least, top_value):
    factor_of, own = 1.0, jax.random.fold_in(rng, 6)
    for position, blocks in cuts:
        heights = jnp.exp(jax.random.uniform(jax.random.fold_in(own, position), (blocks,), jnp.float32, least / len(cuts), top_value / len(cuts)))
        factor_of = factor_of * jnp.repeat(heights, extent[position] // blocks).reshape([-1 if axis == position else 1 for axis in range(len(extent))])
    return factor_of


def split_up(number_of, total, bound, slope):
    weights = [(1 << 20) // math.isqrt(rank ** slope) + 1 for rank in range(2, number_of + 1)]
    rest, counts = total - bound - (number_of - 1), [1] * (number_of - 1)
    while rest > 0:
        candidates = [i for i in range(number_of - 1) if counts[i] < bound]
        whole, left = sum([weights[i] for i in candidates]), rest
        for i in candidates:
            extra = min(bound - counts[i], max(1, left * weights[i] // whole), rest)
            counts[i] = counts[i] + extra
            rest = rest - extra
    return np.array([bound] + counts)


def ragged_sizes(own_key, number_of, total, limit, slope):
    if number_of == 2:
        one = jax.random.randint(own_key, (), max(1, total - limit), min(limit, total - 1) + 1)
        return jnp.stack([one, total - one])
    sizes = jnp.asarray(split_up(number_of, total, limit, slope), jnp.int32)
    twos = (number_of - 1) // 2
    donor, sink = sizes[1:1 + 2 * twos:2], sizes[2:2 + 2 * twos:2]
    slack = jnp.minimum(donor - 1, limit - sink)
    moved = jax.random.randint(jax.random.fold_in(own_key, 1), (twos,), 0, 1 << 20) % (slack + 1)
    sizes = sizes.at[1:1 + 2 * twos:2].set(donor - moved).at[2:2 + 2 * twos:2].set(sink + moved)
    return sizes[jax.random.permutation(jax.random.fold_in(own_key, 2), number_of)]


def bell_draw(stream_key, shape, scale, limit, shards=(), held_as=jnp.bfloat16):
    gain = shard_levels(stream_key, shape, shards, -0.22, 0.18) if shards else 1.0
    values = jax.random.normal(stream_key, shape, jnp.float32) * scale * gain
    return jnp.minimum(jnp.maximum(values, -limit), limit).astype(held_as)


def setup_inputs(seed: int = 0) -> dict:
    streams_of = jax.random.split(jax.random.key(seed), 13)
    return {
        "hidden": draw_hidden(jax.random.fold_in(streams_of[12], 71), 0),
        "qkv_weight": bell_draw(streams_of[1], (3, D, HEADS * HEAD_DIM), D ** -0.5, 0.125, ((2, 8),)),
        "conv_weight": bell_draw(streams_of[2], (CONV, 3, HEADS * HEAD_DIM), 0.5, 2.0, ((2, 8),), jnp.float32),
        "w_beta": draw_w_beta(jax.random.fold_in(streams_of[12], 71), 0),
        "gate_down": bell_draw(streams_of[4], (D, GATE_RANK), D ** -0.5, 0.125),
        "gate_up": bell_draw(streams_of[5], (GATE_RANK, HEADS * HEAD_DIM), GATE_RANK ** -0.5, 0.5, ((1, 8),)),
        "a_log": draw_a_log(jax.random.fold_in(streams_of[12], 71), 0),
        "dt_bias": bell_draw(streams_of[7], (HEADS * HEAD_DIM,), 1.0, 3.0, ((0, 8),), jnp.float32),
        "norm_gain": jnp.clip(1.0 + 0.15 * jax.random.normal(streams_of[8], (HEAD_DIM,), jnp.float32), 0.25, 1.75),
        "prompt_lengths": ragged_sizes(streams_of[9], PROMPTS, TOKENS, LONGEST, 2).astype(jnp.int32),
        "send_slot": draw_send_slot(jax.random.fold_in(streams_of[12], 71), 0),
        "gather_src": draw_gather_src(jax.random.fold_in(streams_of[12], 71), 0),
    }


def doc_ids(lengths, positions):
    prompt_ends = jnp.cumsum(lengths).astype(jnp.int32)
    ended = lax.optimization_barrier(jnp.sum((prompt_ends[None, :] <= positions[:, None]).astype(jnp.int32), axis=1))
    return jnp.where(positions < 0, -1, ended).astype(jnp.int32)

def unit_norm(values):
    return values / jnp.sqrt(lax.optimization_barrier(jnp.sum(values * values, axis=-1, keepdims=True)) + 1e-06)

def span_pieces(query, key_rows, value_rows, decay_log, strength, segments, seg_before):
    highest = lax.Precision.HIGHEST
    block_len = query.shape[-2]
    channels = query.shape[-1]
    cumulative = jnp.cumsum(decay_log, axis=-2)
    last_cum = cumulative[..., -1:, :]
    key_up = key_rows * jnp.exp(cumulative)
    key_down = key_rows * jnp.exp(-cumulative)
    query_up = query * jnp.exp(cumulative)
    same_doc = segments[..., :, None] == segments[..., None, :]
    row_ids = jnp.arange(block_len)
    strict_mask = (row_ids[:, None] > row_ids[None, :]) & same_doc
    incl_mask = (row_ids[:, None] >= row_ids[None, :]) & same_doc
    first_doc = (segments == seg_before[..., None]).astype(jnp.float32)[..., None]
    last_doc = (segments == segments[..., -1:]).astype(jnp.float32)[..., None]
    carry_flag = (segments[..., -1] == seg_before).astype(jnp.float32)
    key_mix = jnp.einsum('...td,...sd->...ts', key_up, key_down, precision=highest)
    strict_part = jnp.where(strict_mask, strength[..., :, None] * key_mix, 0.0)
    eye_small = jnp.eye(block_len, dtype=jnp.float32)
    right_side = jnp.concatenate([strength[..., None] * value_rows, strength[..., None] * key_up * first_doc], axis=-1)
    solved = jax.scipy.linalg.solve_triangular(eye_small + strict_part, right_side, lower=True, unit_diagonal=True)
    scores = jnp.where(incl_mask, jnp.einsum('...td,...sd->...ts', query_up, key_down, precision=highest), 0.0)
    combined = jnp.einsum('...ts,...se->...te', scores, solved, precision=highest)
    out_local = combined[..., :channels]
    lift = query_up * first_doc - combined[..., channels:]
    key_end = key_rows * jnp.exp(last_cum - cumulative) * last_doc
    summary = jnp.einsum('...sd,...se->...de', key_end, solved, precision=highest)
    state_feed = summary[..., :channels]
    eye_channels = jnp.eye(channels, dtype=jnp.float32)
    keep_diag = jnp.exp(last_cum[..., 0, :])[..., :, None] * eye_channels
    state_map = carry_flag[..., None, None] * keep_diag - summary[..., channels:]
    return (out_local, lift, state_map, state_feed)

def reference(hidden, qkv_weight, conv_weight, w_beta, gate_down, gate_up, a_log, dt_bias, norm_gain, prompt_lengths, send_slot, gather_src):
    highest = lax.Precision.HIGHEST
    owner_slots = send_slot.reshape(N_CTX, TOK_DEV)
    slot_table = jnp.zeros((N_CTX, 2 * TOK_DEV), jnp.int32).at[jnp.arange(N_CTX)[:, None], owner_slots].set(jnp.arange(TOK_DEV, dtype=jnp.int32)[None, :])
    positions = jnp.arange(TOKENS, dtype=jnp.int32)
    target = (positions // TOK_DEV).astype(jnp.int32)
    source = (gather_src // CAP).astype(jnp.int32)
    anchor = (source * TOK_DEV + slot_table[source, target * CAP + gather_src % CAP]).astype(jnp.int32)
    packed = hidden[anchor]
    projected = jnp.stack([jnp.dot(packed.astype(jnp.float32), qkv_weight[which].astype(jnp.float32), preferred_element_type=jnp.float32) for which in range(3)], axis=0).astype(jnp.bfloat16)
    prompt_id = doc_ids(prompt_lengths, positions)
    convolved = jnp.zeros(projected.shape, jnp.float32)
    for tap_index in range(CONV):
        offset = CONV - 1 - tap_index
        shifted = jnp.concatenate([jnp.zeros((3, offset, projected.shape[2]), jnp.float32), projected[:, :TOKENS - offset, :].astype(jnp.float32)], axis=1)
        earlier = doc_ids(prompt_lengths, positions - offset)
        valid = (earlier == prompt_id).astype(jnp.float32)
        convolved = convolved + conv_weight[tap_index][:, None, :] * shifted * valid[None, :, None]
    activated = jax.nn.silu(convolved).reshape(3, TOKENS, HEADS, HEAD_DIM)
    query = unit_norm(activated[0]) * HEAD_DIM ** (-0.5)
    key_rows = unit_norm(activated[1])
    value_rows = activated[2]
    low_rank = jnp.dot(packed.astype(jnp.float32), gate_down.astype(jnp.float32), preferred_element_type=jnp.float32).astype(jnp.bfloat16)
    drive = jnp.dot(low_rank.astype(jnp.float32), gate_up.astype(jnp.float32), preferred_element_type=jnp.float32) + dt_bias[None, :]
    decay_log = -jnp.exp(a_log)[None, :, None] * jax.nn.softplus(drive.reshape(TOKENS, HEADS, HEAD_DIM))
    strength = jax.nn.sigmoid(jnp.dot(packed.astype(jnp.float32), w_beta.astype(jnp.float32), preferred_element_type=jnp.float32))
    blocks = TOKENS // SPAN
    segments = prompt_id.reshape(blocks, SPAN)
    seg_before = doc_ids(prompt_lengths, positions[::SPAN] - 1)

    def per_head(head_items):
        query_h, key_h, value_h, decay_h, strength_h = head_items
        shape_blocks = (blocks, SPAN, HEAD_DIM)
        pieces = span_pieces(query_h.reshape(shape_blocks), key_h.reshape(shape_blocks), value_h.reshape(shape_blocks), decay_h.reshape(shape_blocks), strength_h.reshape(blocks, SPAN), segments, seg_before)

        def advance(carried, block_piece):
            out_part, lift_part, map_part, feed_part = block_piece
            emitted = out_part + jnp.dot(lift_part, carried, precision=highest)
            return (jnp.dot(map_part, carried, precision=highest) + feed_part, emitted)
        _, emitted_all = lax.scan(advance, jnp.zeros((HEAD_DIM, HEAD_DIM), jnp.float32), pieces)
        return emitted_all.reshape(TOKENS, HEAD_DIM)
    result = lax.map(per_head, (jnp.moveaxis(query, 1, 0), jnp.moveaxis(key_rows, 1, 0), jnp.moveaxis(value_rows, 1, 0), jnp.moveaxis(decay_log, 1, 0), strength.T))
    scaled = result * lax.rsqrt(lax.optimization_barrier(jnp.mean(result * result, axis=-1, keepdims=True)) + 1e-05) * norm_gain
    return jnp.moveaxis(scaled, 0, 1).reshape(TOKENS, HEADS * HEAD_DIM).astype(jnp.bfloat16)
```

```python
import functools

import jax
import jax.numpy as jnp
from jax import lax
from jax.experimental import pallas as pl
from jax.experimental.pallas import tpu as pltpu
from jax.sharding import PartitionSpec as P

CONV = 4
SPAN = 64
RIM = 16
X_SIZE = 4
CORES = 2
MESH = pl.DeviceIdType.MESH
F32 = jnp.float32
BF16 = jnp.bfloat16
VMEM = pl.BlockSpec(memory_space=pltpu.VMEM)
SMEM = pl.BlockSpec(memory_space=pltpu.SMEM)
ANY = pl.BlockSpec(memory_space=pl.ANY)

NN = (((1,), (0,)), ((), ()))
NT = (((1,), (1,)), ((), ()))
TN = (((0,), (0,)), ((), ()))


def mm(a, b, dims=NN):
    return lax.dot_general(a, b, dims, preferred_element_type=F32)


def split(v):
    high = v.astype(BF16)
    return high, (v - high.astype(F32)).astype(BF16)


def mm3(a, b, dims=NN):
    return mm(a[0], b[0], dims) + (mm(a[0], b[1], dims) + mm(a[1], b[0], dims))


def gather_kernel(
    slot_ref, src_ref, hidden_ref, wqkv_hbm, wdown_hbm, wbeta_hbm,
    ext_ref, low_ref, beta_ref,
    send_buf, landed, shards, w_qkv, w_down, w_beta, acc, acc_low, acc_beta, rim_buf,
    w_sem, s_sem, r_sem, hs_sem, hf_sem, hr_sem, rim_sem,
):
    n_ctx = lax.axis_size("ctx")
    n_head = lax.axis_size("head")
    n_y = n_head // CORES
    me = lax.axis_index("ctx")
    head = lax.axis_index("head")
    y = head // CORES
    core = head % CORES
    sibling = y * CORES + (1 - core)
    rows, width = hidden_ref.shape
    slots = send_buf.shape[0]
    cap = slots // n_ctx

    weights = [
        pltpu.make_async_copy(wqkv_hbm, w_qkv, w_sem.at[0]),
        pltpu.make_async_copy(wdown_hbm, w_down, w_sem.at[1]),
        pltpu.make_async_copy(wbeta_hbm, w_beta, w_sem.at[2]),
    ]
    for copy in weights:
        copy.start()

    barrier = pltpu.get_barrier_semaphore()

    def greet(k, carry):
        pl.semaphore_signal(
            barrier, inc=1, device_id={"ctx": lax.rem(me + k, n_ctx), "head": head}, device_id_type=MESH
        )
        return carry

    lax.fori_loop(1, n_ctx, greet, 0)
    for dy in range(1, n_y):
        other = lax.rem(y + dy, n_y) * CORES + core
        pl.semaphore_signal(barrier, inc=1, device_id={"ctx": me, "head": other}, device_id_type=MESH)
    pl.semaphore_signal(barrier, inc=1, device_id={"ctx": me, "head": sibling}, device_id_type=MESH)

    slot_ids = lax.broadcasted_iota(jnp.int32, (slots, rows), 0)
    place = (slot_ids == slot_ref[...]).astype(F32).astype(BF16)
    send_buf[...] = mm(place, hidden_ref[...]).astype(BF16)
    pick = (slot_ids == src_ref[...]).astype(F32).astype(BF16)

    pl.semaphore_wait(barrier, n_ctx - 1 + n_y)

    def piece(buf, index):
        return buf.at[pl.ds(pl.multiple_of(index * cap, cap), cap), :]

    def send(k, carry):
        to = lax.rem(me + k, n_ctx)
        pltpu.make_async_remote_copy(
            src_ref=piece(send_buf, to), dst_ref=piece(landed, me),
            send_sem=s_sem.at[to], recv_sem=r_sem.at[me],
            device_id={"ctx": to, "head": head}, device_id_type=MESH,
        ).start()
        return carry

    lax.fori_loop(1, n_ctx, send, 0)
    own = pl.ds(pl.multiple_of(me * cap, cap), cap)
    landed[own, :] = send_buf[own, :]

    def arrive(k, carry):
        frm = lax.rem(me + k, n_ctx)
        pltpu.make_async_remote_copy(
            src_ref=piece(send_buf, frm), dst_ref=piece(landed, frm),
            send_sem=s_sem.at[frm], recv_sem=r_sem.at[frm],
            device_id={"ctx": frm, "head": head}, device_id_type=MESH,
        ).wait_recv()
        return carry

    lax.fori_loop(1, n_ctx, arrive, 0)
    shards[head] = mm(pick, landed[...], TN).astype(BF16)

    def shard_copy(index, to, send_sem):
        return pltpu.make_async_remote_copy(
            src_ref=shards.at[index], dst_ref=shards.at[index],
            send_sem=send_sem, recv_sem=hr_sem.at[index],
            device_id={"ctx": me, "head": to}, device_id_type=MESH,
        )

    outgoing = [shard_copy(head, lax.rem(y + dy, n_y) * CORES + core, hs_sem.at[dy]) for dy in range(1, n_y)]
    outgoing.append(shard_copy(head, sibling, hs_sem.at[0]))
    for copy in outgoing:
        copy.start()
    for copy in weights:
        copy.wait()

    def multiply(index, first=False):
        part = shards[index]
        chunk = pl.ds(pl.multiple_of(index * width, 16), width)
        products = [(acc, j, mm(part, w_qkv[j, chunk, :])) for j in range(3)]
        for ref, j, value in products:
            ref[j] = value if first else ref[j] + value
        low = mm(part, w_down[chunk, :])
        beta = mm(part, w_beta[chunk, :])
        acc_low[...] = low if first else acc_low[...] + low
        acc_beta[...] = beta if first else acc_beta[...] + beta

    multiply(head, True)
    shard_copy(sibling, sibling, hs_sem.at[0]).wait_recv()
    multiply(sibling)
    order = [dy for dy in (1, n_y - 1) if 0 < dy < n_y]
    order = sorted(set(order)) + [dy for dy in range(1, n_y) if dy not in order]
    pending = []
    for dy in order:
        index = lax.rem(y + dy, n_y) * CORES + core
        shard_copy(index, sibling, hf_sem.at[dy]).wait_recv()
        forward = shard_copy(index, sibling, hf_sem.at[dy])
        forward.start()
        outgoing.append(forward)
        multiply(index)
        pending.append(lax.rem(y + dy, n_y) * CORES + (1 - core))
    for index in pending:
        shard_copy(index, sibling, hs_sem.at[0]).wait_recv()
        multiply(index)

    columns = acc.shape[2]
    for j in range(3):
        ext_ref[RIM:, j * columns : (j + 1) * columns] = acc[j].astype(BF16)
    rim = pltpu.make_async_remote_copy(
        src_ref=ext_ref.at[pl.ds(rows, RIM), :], dst_ref=rim_buf,
        send_sem=rim_sem.at[0], recv_sem=rim_sem.at[1],
        device_id={"ctx": lax.rem(me + 1, n_ctx), "head": head}, device_id_type=MESH,
    )
    rim.start()
    low_ref[...] = acc_low[...].astype(BF16)
    beta_ref[...] = acc_beta[...]
    for copy in outgoing:
        copy.wait_send()

    def sent(k, carry):
        to = lax.rem(me + k, n_ctx)
        pltpu.make_async_remote_copy(
            src_ref=piece(send_buf, to), dst_ref=piece(landed, me),
            send_sem=s_sem.at[to], recv_sem=r_sem.at[me],
            device_id={"ctx": to, "head": head}, device_id_type=MESH,
        ).wait_send()
        return carry

    lax.fori_loop(1, n_ctx, sent, 0)
    rim.wait()
    ext_ref[:RIM, :] = rim_buf[...]


def gather_and_project(hidden, qkv_weight, gate_down, w_beta, send_slot, gather_src):
    rows, width = hidden.shape
    _, features, columns = qkv_weight.shape
    n_ctx, n_head = lax.axis_size("ctx"), lax.axis_size("head")
    slots = 2 * rows
    rank, betas = gate_down.shape[1], w_beta.shape[1]
    return pl.pallas_call(
        gather_kernel,
        out_shape=(
            jax.ShapeDtypeStruct((RIM + rows, 3 * columns), BF16),
            jax.ShapeDtypeStruct((rows, rank), BF16),
            jax.ShapeDtypeStruct((rows, betas), F32),
        ),
        in_specs=[VMEM, VMEM, VMEM, ANY, ANY, ANY],
        out_specs=(VMEM, VMEM, VMEM),
        scratch_shapes=[
            pltpu.VMEM((slots, width), BF16),
            pltpu.VMEM((slots, width), BF16),
            pltpu.VMEM((n_head, rows, width), BF16),
            pltpu.VMEM((3, features, columns), BF16),
            pltpu.VMEM((features, rank), BF16),
            pltpu.VMEM((features, betas), BF16),
            pltpu.VMEM((3, rows, columns), F32),
            pltpu.VMEM((rows, rank), F32),
            pltpu.VMEM((rows, betas), F32),
            pltpu.VMEM((RIM, 3 * columns), BF16),
            pltpu.SemaphoreType.DMA((3,)),
            pltpu.SemaphoreType.DMA((n_ctx,)),
            pltpu.SemaphoreType.DMA((n_ctx,)),
            pltpu.SemaphoreType.DMA((n_head // CORES,)),
            pltpu.SemaphoreType.DMA((n_head // CORES,)),
            pltpu.SemaphoreType.DMA((n_head,)),
            pltpu.SemaphoreType.DMA((2,)),
        ],
        compiler_params=pltpu.CompilerParams(
            collective_id=0, has_side_effects=True, vmem_limit_bytes=48 * 1024 * 1024
        ),
        name="gather_project",
    )(send_slot.reshape(1, rows), gather_src.reshape(1, rows), hidden, qkv_weight, gate_down, w_beta)


def chunk_pieces(
    lengths_ref, rate_ref, ext_ref, low_ref, beta_ref, conv_ref, up_ref, bias_ref,
    ab_ref, local_ref, lift_ref, base,
):
    rows = low_ref.shape[0]
    channels = local_ref.shape[2]
    heads = local_ref.shape[0]
    columns = heads * channels
    blocks = rows // SPAN

    ends, total = [], 0
    for i in range(lengths_ref.shape[0]):
        total = total + lengths_ref[i]
        ends.append(total)

    def doc_of(positions):
        ended = sum((positions >= end).astype(jnp.int32) for end in ends)
        return jnp.where(positions < 0, -1, ended)

    pos = base + lax.broadcasted_iota(jnp.int32, (rows, channels), 0)
    doc = doc_of(pos)
    valid = [None] + [(doc_of(pos - shift) == doc).astype(F32) for shift in range(1, CONV)]
    before = doc_of(jnp.zeros((1, channels), jnp.int32) + (base - 1))
    final = doc_of(jnp.zeros((1, channels), jnp.int32) + (base + rows - 1))
    first_doc = (doc == before).astype(F32)
    last_doc = (doc == final).astype(F32)
    carry = (final == before).astype(F32)

    row = lax.broadcasted_iota(jnp.int32, (rows, rows), 0)
    col = lax.broadcasted_iota(jnp.int32, (rows, rows), 1)
    same = doc_of(base + row) == doc_of(base + col)
    strict = (row > col) & same
    inclusive = (row >= col) & same
    apart = row ^ col
    running = ((row >= col) & (apart < SPAN)).astype(F32).astype(BF16)
    eye = (row == col).astype(F32)
    eye_channels = (
        lax.broadcasted_iota(jnp.int32, (channels, channels), 0)
        == lax.broadcasted_iota(jnp.int32, (channels, channels), 1)
    ).astype(F32)

    low = low_ref[...]
    betas = 1.0 / (1.0 + jnp.exp(-beta_ref[...]))

    def activated(j, h):
        at = j * columns + h * channels
        values = ext_ref[:, at : at + channels].astype(F32)
        total = None
        for tap in range(CONV):
            shift = CONV - 1 - tap
            weight = conv_ref[tap, j : j + 1, h * channels : (h + 1) * channels]
            part = weight * values[RIM - shift : RIM - shift + rows]
            if shift:
                part = part * valid[shift]
            total = part if total is None else total + part
        return total / (1.0 + jnp.exp(-total))

    def unit(values):
        return values * lax.rsqrt(jnp.sum(values * values, axis=-1, keepdims=True) + 1e-06)

    for h in range(heads):
        lanes = slice(h * channels, (h + 1) * channels)
        query = unit(activated(0, h)) * channels ** (-0.5)
        key = unit(activated(1, h))
        value = activated(2, h)
        drive = mm(low, up_ref[:, lanes]) + bias_ref[:, lanes]
        soft = jnp.maximum(drive, 0.0) + jnp.log1p(jnp.exp(-jnp.abs(drive)))
        rate = jnp.exp(jnp.full((1, channels), rate_ref[h], F32))
        decay = -rate * soft
        d_high, d_rest = split(decay)
        d_mid = d_rest
        d_low = (decay - d_high.astype(F32) - d_mid.astype(F32)).astype(BF16)
        cum = mm(running, d_high) + (mm(running, d_mid) + mm(running, d_low))
        strength = jnp.broadcast_to(betas[:, h : h + 1], (rows, channels))

        grow = jnp.exp(cum)
        key_up = key * grow
        query_up = query * grow
        key_down = key * jnp.exp(-cum)
        lasts = [cum[(b + 1) * SPAN - 1 : (b + 1) * SPAN] for b in range(blocks)]
        part_of = lambda v, b: v[b * SPAN : (b + 1) * SPAN]
        key_tail = [part_of(key, b) * jnp.exp(lasts[b] - part_of(cum, b)) for b in range(blocks)]

        mixes, scores = [], []
        for i in range(blocks):
            cols = []
            for b in range(blocks):
                if b < i:
                    between = sum(lasts[b + 1 : i], jnp.zeros_like(lasts[0]))
                    cols.append(key_tail[b] * jnp.exp(between))
                elif b == i:
                    cols.append(part_of(key_down, b))
                else:
                    cols.append(jnp.zeros((SPAN, channels), F32))
            left = split(jnp.concatenate([part_of(key_up, i), part_of(query_up, i)], axis=0))
            product = mm3(left, split(jnp.concatenate(cols, axis=0)), NT)
            mixes.append(product[:SPAN])
            scores.append(product[SPAN:])
        strength_wide = jnp.broadcast_to(betas[:, h : h + 1], (rows, rows))
        lower = jnp.where(strict, strength_wide * jnp.concatenate(mixes, axis=0), 0.0)
        score = jnp.where(inclusive, jnp.concatenate(scores, axis=0), 0.0)

        small = jnp.where(apart < 8, lower, 0.0)
        power = split(small)
        square = mm3(power, power)
        power = split(square)
        inverse = eye - small
        inverse = inverse + mm3(split(inverse), power)
        fourth = mm3(power, power)
        inverse = inverse + mm3(split(inverse), split(fourth))
        size = 8
        while size < rows:
            off = jnp.where((apart >= size) & (apart < 2 * size), lower, 0.0)
            parts = split(inverse)
            inverse = inverse - mm3(parts, split(mm3(split(off), parts)))
            size *= 2

        prefix = jnp.zeros_like(lasts[0])
        ups, tails, q_ups = [], [], []
        for b in range(blocks):
            scale = jnp.exp(prefix)
            ups.append(part_of(key_up, b) * scale)
            q_ups.append(part_of(query_up, b) * scale)
            prefix = prefix + lasts[b]
            tails.append(key_tail[b] * jnp.exp(sum(lasts[b + 1 :], jnp.zeros_like(lasts[0]))))
        key_full = jnp.concatenate(ups, axis=0) * first_doc
        query_full = jnp.concatenate(q_ups, axis=0) * first_doc
        tail = jnp.concatenate(tails, axis=0) * last_doc
        right = jnp.concatenate([strength * key_full, strength * value], axis=1)
        solved = split(mm3(split(inverse), split(right)))
        summary = mm3(split(tail), solved, TN)
        keep = carry * jnp.exp(prefix)
        ab_ref[h, :, :channels] = keep * eye_channels - summary[:, :channels]
        ab_ref[h, :, channels:] = summary[:, channels:]
        combined = mm3(split(score), solved)
        lift_ref[h] = query_full - combined[:, :channels]
        local_ref[h] = combined[:, channels:]


def chunk_kernel(base_ref, *refs):
    chunk_pieces(*refs, base_ref[0])


def delta_chunk(ext, low, beta, conv_weight, gate_up, a_log, dt_bias, prompt_lengths, base, channels):
    rows = low.shape[0]
    heads = a_log.shape[0]
    return pl.pallas_call(
        chunk_kernel,
        out_shape=(
            jax.ShapeDtypeStruct((heads, channels, 2 * channels), F32),
            jax.ShapeDtypeStruct((heads, rows, channels), F32),
            jax.ShapeDtypeStruct((heads, rows, channels), F32),
        ),
        in_specs=[SMEM, SMEM, SMEM] + [VMEM] * 6,
        out_specs=(VMEM, VMEM, VMEM),
        compiler_params=pltpu.CompilerParams(vmem_limit_bytes=48 * 1024 * 1024),
        name="delta_chunk",
    )(base, prompt_lengths, a_log, ext, low, beta, conv_weight, gate_up, dt_bias.reshape(1, -1))


def relay_kernel(
    ab_ref, local_ref, lift_ref, gain_ref, out_ref,
    maps, passed, arrived, entry_out, entry,
    xs_sem, xr_sem, c_sem, bs_sem, br_sem,
):
    n_z = lax.axis_size("ctx") // X_SIZE
    me = lax.axis_index("ctx")
    head = lax.axis_index("head")
    z, x = me // X_SIZE, me % X_SIZE
    heads, rows, channels = local_ref.shape

    def at(ctx):
        return {"ctx": ctx, "head": head}

    barrier = pltpu.get_barrier_semaphore()
    for dx in range(1, X_SIZE):
        pl.semaphore_signal(
            barrier, inc=1, device_id=at(z * X_SIZE + lax.rem(x + dx, X_SIZE)), device_id_type=MESH
        )

    @pl.when(z > 0)
    def _():
        pl.semaphore_signal(barrier, inc=1, device_id=at(me - X_SIZE), device_id_type=MESH)

    @pl.when(z < n_z - 1)
    def _():
        pl.semaphore_signal(barrier, inc=1, device_id=at(me + X_SIZE), device_id_type=MESH)

    greeted = X_SIZE - 1 + (z > 0).astype(jnp.int32) + (z < n_z - 1).astype(jnp.int32)
    pl.semaphore_wait(barrier, greeted)

    def map_copy(dx):
        to = lax.rem(x + dx, X_SIZE)
        return pltpu.make_async_remote_copy(
            src_ref=ab_ref.at[to], dst_ref=maps.at[x],
            send_sem=xs_sem.at[dx], recv_sem=xr_sem.at[x],
            device_id=at(z * X_SIZE + to), device_id_type=MESH,
        )

    copies = [map_copy(dx) for dx in range(1, X_SIZE)]
    for copy in copies:
        copy.start()
    maps[x] = ab_ref[x]
    for dx in range(1, X_SIZE):
        frm = lax.rem(x + dx, X_SIZE)
        pltpu.make_async_remote_copy(
            src_ref=ab_ref.at[frm], dst_ref=maps.at[frm],
            send_sem=xs_sem.at[dx], recv_sem=xr_sem.at[frm],
            device_id=at(z * X_SIZE + frm), device_id_type=MESH,
        ).wait_recv()

    whole = maps[0]
    prefixes = [whole]
    for j in range(1, X_SIZE):
        step = maps[j]
        product = mm3(split(step[:, :channels]), split(whole))
        whole = jnp.concatenate([product[:, :channels], product[:, channels:] + step[:, channels:]], axis=1)
        prefixes.append(whole)
    group_map = split(whole[:, :channels])
    group_feed = whole[:, channels:]

    chain = pltpu.make_async_remote_copy(
        src_ref=passed, dst_ref=arrived, send_sem=c_sem.at[0], recv_sem=c_sem.at[1],
        device_id=at(lax.rem(me + X_SIZE, n_z * X_SIZE)), device_id_type=MESH,
    )

    @pl.when(z == 0)
    def _():
        arrived[...] = jnp.zeros_like(arrived)

    @pl.when(z > 0)
    def _():
        chain.wait_recv()

    state = arrived[...]
    state_parts = split(state)
    passed[...] = mm3(group_map, state_parts) + group_feed

    @pl.when(z < n_z - 1)
    def _():
        chain.start()

    entry_out[0] = state
    for j in range(1, X_SIZE):
        before = prefixes[j - 1]
        entry_out[j] = mm3(split(before[:, :channels]), state_parts) + before[:, channels:]

    def entry_copy(dx):
        to = lax.rem(x + dx, X_SIZE)
        return pltpu.make_async_remote_copy(
            src_ref=entry_out.at[to], dst_ref=entry.at[x],
            send_sem=bs_sem.at[dx], recv_sem=br_sem.at[x],
            device_id=at(z * X_SIZE + to), device_id_type=MESH,
        )

    returns = [entry_copy(dx) for dx in range(1, X_SIZE)]
    for copy in returns:
        copy.start()
    entry[x] = entry_out[x]
    for dx in range(1, X_SIZE):
        frm = lax.rem(x + dx, X_SIZE)
        pltpu.make_async_remote_copy(
            src_ref=entry_out.at[frm], dst_ref=entry.at[frm],
            send_sem=bs_sem.at[dx], recv_sem=br_sem.at[frm],
            device_id=at(z * X_SIZE + frm), device_id_type=MESH,
        ).wait_recv()

    for h in range(heads):
        result = local_ref[h] + mm3(split(lift_ref[h]), split(entry[h]))
        mean = jnp.mean(result * result, axis=-1, keepdims=True)
        scaled = result * lax.rsqrt(mean + 1e-05) * gain_ref[...]
        out_ref[:, h * channels : (h + 1) * channels] = scaled.astype(BF16)

    for copy in copies + returns:
        copy.wait_send()

    @pl.when(z < n_z - 1)
    def _():
        chain.wait_send()


def relay(ab, local, lift, norm_gain):
    heads, rows, channels = local.shape
    state = (channels, channels)
    return pl.pallas_call(
        relay_kernel,
        out_shape=jax.ShapeDtypeStruct((rows, heads * channels), BF16),
        in_specs=[VMEM] * 4,
        out_specs=VMEM,
        scratch_shapes=[
            pltpu.VMEM((X_SIZE, channels, 2 * channels), F32),
            pltpu.VMEM(state, F32),
            pltpu.VMEM(state, F32),
            pltpu.VMEM((X_SIZE,) + state, F32),
            pltpu.VMEM((X_SIZE,) + state, F32),
            pltpu.SemaphoreType.DMA((X_SIZE,)),
            pltpu.SemaphoreType.DMA((X_SIZE,)),
            pltpu.SemaphoreType.DMA((2,)),
            pltpu.SemaphoreType.DMA((X_SIZE,)),
            pltpu.SemaphoreType.DMA((X_SIZE,)),
        ],
        compiler_params=pltpu.CompilerParams(
            collective_id=1, has_side_effects=True, vmem_limit_bytes=32 * 1024 * 1024
        ),
        name="relay",
    )(ab, local, lift, norm_gain.reshape(1, channels))


def on_device(
    hidden, qkv_weight, conv_weight, w_beta, gate_down, gate_up,
    a_log, dt_bias, norm_gain, prompt_lengths, send_slot, gather_src,
):
    rows = send_slot.shape[0]
    channels = norm_gain.shape[0]
    ext, low, beta = gather_and_project(hidden, qkv_weight, gate_down, w_beta, send_slot, gather_src)
    base = (lax.axis_index("ctx") * rows).astype(jnp.int32).reshape(1)
    ab, local, lift = delta_chunk(
        ext, low, beta, conv_weight, gate_up, a_log, dt_bias, prompt_lengths, base, channels
    )
    return relay(ab, local, lift, norm_gain)


def solution(mesh):
    placed = (
        P("ctx", "head"),
        P(None, None, "head"),
        P(None, None, "head"),
        P(None, "head"),
        P(),
        P(None, "head"),
        P("head"),
        P("head"),
        P(),
        P(),
        P("ctx"),
        P("ctx"),
    )
    return jax.shard_map(
        on_device, mesh=mesh, in_specs=placed, out_specs=P("ctx", "head"), check_vma=False
    )
```

```python
import functools

import jax
import jax.numpy as jnp
from jax import lax
from jax.experimental import pallas as pl
from jax.experimental.pallas import tpu as pltpu
from jax.sharding import PartitionSpec as P

CONV = 4
SPAN = 64
RIM = 8
X_SIZE = 4
CORES = 2
GROUP = 8
MESH = pl.DeviceIdType.MESH
F32 = jnp.float32
BF16 = jnp.bfloat16
VMEM = pl.BlockSpec(memory_space=pltpu.VMEM)
SMEM = pl.BlockSpec(memory_space=pltpu.SMEM)
HBM = pl.BlockSpec(memory_space=pltpu.HBM)

NN = (((1,), (0,)), ((), ()))
NT = (((1,), (1,)), ((), ()))
TN = (((0,), (0,)), ((), ()))


def mm(a, b, dims=NN):
    return lax.dot_general(a, b, dims, preferred_element_type=F32)


def split(v):
    high = v.astype(BF16)
    return high, (v - high.astype(F32)).astype(BF16)


def mm3(a, b, dims=NN):
    return mm(a[0], b[0], dims) + (mm(a[0], b[1], dims) + mm(a[1], b[0], dims))


def mm3_narrow(a, b, dims=NN):
    axis = dims[0][1][0]
    wide = mm(jnp.concatenate(a, axis=1), jnp.concatenate([b[0], b[0]], axis=axis), dims)
    return wide + mm(a[0], b[1], dims)


def gather_kernel(
    slot_hbm, src_hbm, hidden_hbm, wqkv_hbm, wdown_hbm, wbeta_hbm,
    ext_ref, low_ref, beta_ref,
    slot_buf, src_buf, hidden_buf, wbeta_buf,
    send_buf, landed, shards, w_qkv, w_down, w_beta, acc, acc_low, acc_beta, rim_buf,
    w_sem, s_sem, r_sem, hs_sem, hf_sem, hr_sem, rim_sem,
):
    n_ctx = lax.axis_size("ctx")
    n_head = lax.axis_size("head")
    n_y = n_head // CORES
    me = lax.axis_index("ctx")
    head = lax.axis_index("head")
    y = head // CORES
    core = head % CORES
    sibling = y * CORES + (1 - core)
    width, rows = hidden_buf.shape
    slots = send_buf.shape[0]
    cap = slots // n_ctx

    early = [
        pltpu.make_async_copy(slot_hbm, slot_buf, w_sem.at[3]),
        pltpu.make_async_copy(hidden_hbm, hidden_buf, w_sem.at[4]),
        pltpu.make_async_copy(src_hbm, src_buf, w_sem.at[5]),
        pltpu.make_async_copy(wbeta_hbm, wbeta_buf, w_sem.at[2]),
    ]
    weights = [
        pltpu.make_async_copy(wqkv_hbm, w_qkv, w_sem.at[0]),
        pltpu.make_async_copy(wdown_hbm, w_down, w_sem.at[1]),
    ]
    for copy in early + weights:
        copy.start()

    barrier = pltpu.get_barrier_semaphore()

    def greet(k, carry):
        pl.semaphore_signal(
            barrier, inc=1, device_id={"ctx": lax.rem(me + k, n_ctx), "head": head}, device_id_type=MESH
        )
        return carry

    lax.fori_loop(1, n_ctx, greet, 0)
    for dy in range(1, n_y):
        other = lax.rem(y + dy, n_y) * CORES + core
        pl.semaphore_signal(barrier, inc=1, device_id={"ctx": me, "head": other}, device_id_type=MESH)
    pl.semaphore_signal(barrier, inc=1, device_id={"ctx": me, "head": sibling}, device_id_type=MESH)

    for copy in early:
        copy.wait()
    slot_ids = lax.broadcasted_iota(jnp.int32, (slots, rows), 0)
    place = (slot_ids == slot_buf[...]).astype(F32).astype(BF16)
    send_buf[...] = mm(place, hidden_buf[...], NT).astype(BF16)
    pick = (slot_ids == src_buf[...]).astype(F32).astype(BF16)

    for index in range(n_head):
        w_beta[index] = wbeta_buf[:, index * width : (index + 1) * width]

    pl.semaphore_wait(barrier, n_ctx - 1 + n_y)

    def piece(buf, index):
        return buf.at[pl.ds(pl.multiple_of(index * cap, cap), cap), :]

    def send(k, carry):
        to = lax.rem(me + k, n_ctx)
        pltpu.make_async_remote_copy(
            src_ref=piece(send_buf, to), dst_ref=piece(landed, me),
            send_sem=s_sem.at[to], recv_sem=r_sem.at[me],
            device_id={"ctx": to, "head": head}, device_id_type=MESH,
        ).start()
        return carry

    lax.fori_loop(1, n_ctx, send, 0)
    own = pl.ds(pl.multiple_of(me * cap, cap), cap)
    landed[own, :] = send_buf[own, :]

    def arrive(k, carry):
        frm = lax.rem(me + k, n_ctx)
        pltpu.make_async_remote_copy(
            src_ref=piece(send_buf, frm), dst_ref=piece(landed, frm),
            send_sem=s_sem.at[frm], recv_sem=r_sem.at[frm],
            device_id={"ctx": frm, "head": head}, device_id_type=MESH,
        ).wait_recv()
        return carry

    lax.fori_loop(1, n_ctx, arrive, 0)
    shards[head] = mm(pick, landed[...], TN).astype(BF16)

    def shard_copy(index, to, send_sem):
        return pltpu.make_async_remote_copy(
            src_ref=shards.at[index], dst_ref=shards.at[index],
            send_sem=send_sem, recv_sem=hr_sem.at[index],
            device_id={"ctx": me, "head": to}, device_id_type=MESH,
        )

    outgoing = [shard_copy(head, lax.rem(y + dy, n_y) * CORES + core, hs_sem.at[dy]) for dy in range(1, n_y)]
    outgoing.append(shard_copy(head, sibling, hs_sem.at[0]))
    for copy in outgoing:
        copy.start()
    for copy in weights:
        copy.wait()

    def multiply(index, first=False):
        part = shards[index]
        chunk = pl.ds(pl.multiple_of(index * width, 16), width)
        products = [(acc, j, mm(part, w_qkv[j, chunk, :])) for j in range(3)]
        for ref, j, value in products:
            ref[j] = value if first else ref[j] + value
        low = mm(part, w_down[chunk, :])
        beta = mm(part, w_beta[index], NT)
        acc_low[...] = low if first else acc_low[...] + low
        acc_beta[...] = beta if first else acc_beta[...] + beta

    multiply(head, True)
    shard_copy(sibling, sibling, hs_sem.at[0]).wait_recv()
    multiply(sibling)
    order = [dy for dy in (1, n_y - 1) if 0 < dy < n_y]
    order = sorted(set(order)) + [dy for dy in range(1, n_y) if dy not in order]
    pending = []
    for dy in order:
        index = lax.rem(y + dy, n_y) * CORES + core
        shard_copy(index, sibling, hf_sem.at[dy]).wait_recv()
        forward = shard_copy(index, sibling, hf_sem.at[dy])
        forward.start()
        outgoing.append(forward)
        multiply(index)
        pending.append(lax.rem(y + dy, n_y) * CORES + (1 - core))
    for index in pending:
        shard_copy(index, sibling, hs_sem.at[0]).wait_recv()
        multiply(index)

    columns = acc.shape[2]
    for j in range(3):
        ext_ref[RIM:, j * columns : (j + 1) * columns] = acc[j].astype(BF16).astype(F32)
    rim = pltpu.make_async_remote_copy(
        src_ref=ext_ref.at[pl.ds(rows, RIM), :], dst_ref=rim_buf,
        send_sem=rim_sem.at[0], recv_sem=rim_sem.at[1],
        device_id={"ctx": lax.rem(me + 1, n_ctx), "head": head}, device_id_type=MESH,
    )
    rim.start()
    low_ref[...] = acc_low[...].astype(BF16)
    beta_ref[...] = acc_beta[...]
    for copy in outgoing:
        copy.wait_send()

    def sent(k, carry):
        to = lax.rem(me + k, n_ctx)
        pltpu.make_async_remote_copy(
            src_ref=piece(send_buf, to), dst_ref=piece(landed, me),
            send_sem=s_sem.at[to], recv_sem=r_sem.at[me],
            device_id={"ctx": to, "head": head}, device_id_type=MESH,
        ).wait_send()
        return carry

    lax.fori_loop(1, n_ctx, sent, 0)
    rim.wait()
    ext_ref[:RIM, :] = rim_buf[...]


def gather_and_project(hidden, qkv_weight, gate_down, w_beta, send_slot, gather_src):
    width, rows = hidden.shape
    _, features, columns = qkv_weight.shape
    n_ctx, n_head = lax.axis_size("ctx"), lax.axis_size("head")
    slots = 2 * rows
    rank, betas = gate_down.shape[1], w_beta.shape[0]
    return pl.pallas_call(
        gather_kernel,
        out_shape=(
            jax.ShapeDtypeStruct((RIM + rows, 3 * columns), F32),
            jax.ShapeDtypeStruct((rows, rank), BF16),
            jax.ShapeDtypeStruct((rows, betas), F32),
        ),
        in_specs=[HBM] * 6,
        out_specs=(VMEM, VMEM, VMEM),
        scratch_shapes=[
            pltpu.VMEM((1, rows), jnp.int32),
            pltpu.VMEM((1, rows), jnp.int32),
            pltpu.VMEM((width, rows), BF16),
            pltpu.VMEM((betas, features), BF16),
            pltpu.VMEM((slots, width), BF16),
            pltpu.VMEM((slots, width), BF16),
            pltpu.VMEM((n_head, rows, width), BF16),
            pltpu.VMEM((3, features, columns), BF16),
            pltpu.VMEM((features, rank), BF16),
            pltpu.VMEM((n_head, betas, width), BF16),
            pltpu.VMEM((3, rows, columns), F32),
            pltpu.VMEM((rows, rank), F32),
            pltpu.VMEM((rows, betas), F32),
            pltpu.VMEM((RIM, 3 * columns), F32),
            pltpu.SemaphoreType.DMA((6,)),
            pltpu.SemaphoreType.DMA((n_ctx,)),
            pltpu.SemaphoreType.DMA((n_ctx,)),
            pltpu.SemaphoreType.DMA((n_head // CORES,)),
            pltpu.SemaphoreType.DMA((n_head // CORES,)),
            pltpu.SemaphoreType.DMA((n_head,)),
            pltpu.SemaphoreType.DMA((2,)),
        ],
        compiler_params=pltpu.CompilerParams(
            collective_id=0, has_side_effects=True, vmem_limit_bytes=48 * 1024 * 1024
        ),
        name="gather_project",
    )(send_slot.reshape(1, rows), gather_src.reshape(1, rows), hidden, qkv_weight, gate_down, w_beta)


def delta_kernel(
    lengths_ref, rate_ref, ext_ref, low_ref, beta_ref, conv_ref, up_ref, bias_ref, gain_ref,
    out_ref,
    stack, local, lift, maps, total, others, state, entry_out, entry,
    xs_sem, xr_sem, zs_sem, zr_sem, bs_sem, br_sem,
):
    n_ctx = lax.axis_size("ctx")
    n_groups = n_ctx // GROUP
    me = lax.axis_index("ctx")
    head = lax.axis_index("head")
    member = lax.rem(me, GROUP)
    group = me // GROUP
    x, side = lax.rem(member, X_SIZE), member // X_SIZE
    heads, rows, channels = local.shape
    columns = heads * channels
    half = channels // 2
    blocks = rows // SPAN
    base = me * rows

    def at(ctx):
        return {"ctx": ctx, "head": head}

    def mate(index):
        return at(group * GROUP + index)

    barrier = pltpu.get_barrier_semaphore()
    for k in range(1, GROUP):
        pl.semaphore_signal(
            barrier, inc=1, device_id=mate(lax.rem(member + k, GROUP)), device_id_type=MESH
        )
    for k in range(1, n_groups):
        pl.semaphore_signal(
            barrier, inc=1, device_id=at(lax.rem(me + k * GROUP, n_ctx)), device_id_type=MESH
        )

    ends, total_len = [], 0
    for i in range(lengths_ref.shape[0]):
        total_len = total_len + lengths_ref[i]
        ends.append(total_len)

    def doc_of(positions):
        ended = sum((positions >= end).astype(jnp.int32) for end in ends)
        return jnp.where(positions < 0, -1, ended)

    pos = base + lax.broadcasted_iota(jnp.int32, (rows, channels), 0)
    doc = doc_of(pos)
    valid = [None] + [(doc_of(pos - shift) == doc).astype(F32) for shift in range(1, CONV)]
    before = doc_of(jnp.zeros((1, channels), jnp.int32) + (base - 1))
    final = doc_of(jnp.zeros((1, channels), jnp.int32) + (base + rows - 1))
    first_doc = (doc == before).astype(F32)
    last_doc = (doc == final).astype(F32)
    carry = (final == before).astype(F32)
    row = lax.broadcasted_iota(jnp.int32, (rows, rows), 0)
    col = lax.broadcasted_iota(jnp.int32, (rows, rows), 1)
    col_doc = doc_of(base + lax.broadcasted_iota(jnp.int32, (1, rows), 1))
    same = jnp.concatenate([doc, doc], axis=1) == col_doc
    strict = (row > col) & same
    inclusive = (row >= col) & same
    apart = row ^ col
    running = ((row >= col) & (apart < SPAN)).astype(F32).astype(BF16)
    small_row = lax.broadcasted_iota(jnp.int32, (SPAN, rows), 0)
    small_col = lax.broadcasted_iota(jnp.int32, (SPAN, rows), 1)
    small_apart = small_row ^ (small_col & (SPAN - 1))
    small_block = small_col // SPAN
    small_eye = (small_apart == 0).astype(F32)

    def activated(j):
        lanes = slice(j * columns, (j + 1) * columns)
        out = None
        for tap in range(CONV):
            shift = CONV - 1 - tap
            part = conv_ref[j, tap : tap + 1, :] * ext_ref[pl.ds(RIM - shift, rows), lanes]
            if shift:
                part = part * jnp.concatenate([valid[shift]] * heads, axis=1)
            out = part if out is None else out + part
        return out / (1.0 + jnp.exp(-out))

    def of_head(v, h):
        return v[:, h * channels : (h + 1) * channels]

    def unit(v):
        return v * lax.rsqrt(jnp.sum(v * v, axis=-1, keepdims=True) + 1e-06)

    def block(v, b):
        return v[b * SPAN : (b + 1) * SPAN]

    drive = mm(low_ref[...], up_ref[...]) + bias_ref[...]
    soft = jnp.maximum(drive, 0.0) + jnp.log1p(jnp.exp(-jnp.abs(drive)))
    rates = jnp.concatenate(
        [jnp.exp(jnp.full((1, channels), rate_ref[h], F32)) for h in range(heads)], axis=1
    )
    decay = -rates * soft
    d_high, d_mid = split(decay)
    d_low = (decay - d_high.astype(F32) - d_mid.astype(F32)).astype(BF16)
    cum_all = mm(running, d_high) + (mm(running, d_mid) + mm(running, d_low))
    betas = 1.0 / (1.0 + jnp.exp(-beta_ref[...]))
    acts = [activated(j) for j in range(3)]

    every = range(heads)
    cums = [of_head(cum_all, h) for h in every]
    strengths = [jnp.broadcast_to(betas[:, h : h + 1], (rows, channels)) for h in every]
    queries = [unit(of_head(acts[0], h)) * channels ** (-0.5) for h in every]
    keys = [unit(of_head(acts[1], h)) for h in every]
    values = [strengths[h] * of_head(acts[2], h) for h in every]
    lasts = [[cums[h][(b + 1) * SPAN - 1 : (b + 1) * SPAN] for b in range(blocks)] for h in every]
    nothing = jnp.zeros((1, channels), F32)

    lower, score, solved = [], [], []
    bk_ups, q_ups, tails = [], [], []
    for h in every:
        grow = jnp.exp(cums[h])
        bk_ups.append(strengths[h] * keys[h] * grow)
        q_ups.append(queries[h] * grow)
        key_down = keys[h] * jnp.exp(-cums[h])
        tails.append([block(keys[h], b) * jnp.exp(lasts[h][b] - block(cums[h], b)) for b in range(blocks)])
        mixes, reads = [], []
        for i in range(blocks):
            cols = []
            for b in range(blocks):
                if b < i - 1:
                    cols.append(tails[h][b] * jnp.exp(sum(lasts[h][b + 1 : i], nothing)))
                elif b == i - 1:
                    cols.append(tails[h][b])
                elif b == i:
                    cols.append(block(key_down, b))
                else:
                    cols.append(jnp.zeros((SPAN, channels), F32))
            left = split(jnp.concatenate([block(bk_ups[h], i), block(q_ups[h], i)], axis=0))
            product = mm3_narrow(left, split(jnp.concatenate(cols, axis=0)), NT)
            mixes.append(jnp.where(block(strict, i), product[:SPAN], 0.0))
            reads.append(jnp.where(block(inclusive, i), product[SPAN:], 0.0))
        lower.append(mixes)
        score.append(reads)

    def spread(v):
        return jnp.concatenate(
            [jnp.where(small_block == b, v, 0.0) for b in range(blocks)], axis=0
        )

    def times(lefts, rights):
        return [mm3(split(a), split(spread(b))) for a, b in zip(lefts, rights)]

    diagonal = []
    for h in every:
        picked = jnp.zeros((SPAN, rows), F32)
        for b in range(blocks):
            picked = jnp.where(small_block == b, lower[h][b], picked)
        diagonal.append(picked)
    power = [jnp.where(small_apart < 8, d, 0.0) for d in diagonal]
    inverse = [small_eye - p for p in power]
    power = times(power, power)
    inverse = [i + t for i, t in zip(inverse, times(inverse, power))]
    power = times(power, power)
    inverse = [i + t for i, t in zip(inverse, times(inverse, power))]
    size = 8
    while size < SPAN:
        off = [jnp.where((small_apart >= size) & (small_apart < 2 * size), d, 0.0) for d in diagonal]
        inverse = [i - t for i, t in zip(inverse, times(inverse, times(off, inverse)))]
        size *= 2

    full_keys, full_queries, ends_k, keeps = [], [], [], []
    for h in every:
        prefix = nothing
        k_rows, q_rows, t_rows = [], [], []
        for b in range(blocks):
            scale = jnp.exp(prefix)
            k_rows.append(block(bk_ups[h], b) * scale)
            q_rows.append(block(q_ups[h], b) * scale)
            prefix = prefix + lasts[h][b]
            t_rows.append(tails[h][b] * jnp.exp(sum(lasts[h][b + 1 :], nothing)))
        full_keys.append(jnp.concatenate(k_rows, axis=0) * first_doc)
        full_queries.append(jnp.concatenate(q_rows, axis=0) * first_doc)
        ends_k.append(split(jnp.concatenate(t_rows, axis=0) * last_doc))
        keeps.append(carry * jnp.exp(prefix))
    rights = [jnp.concatenate([full_keys[h], values[h]], axis=1) for h in every]
    done = [[] for _ in every]
    for i in range(blocks):
        rest = []
        for h in every:
            part = block(rights[h], i)
            if i:
                seen = tuple(jnp.concatenate([d[k] for d in done[h]], axis=0) for k in range(2))
                part = part - mm3(split(lower[h][i][:, : i * SPAN]), seen)
            rest.append(split(part))
        for h in every:
            own = split(inverse[h][:, i * SPAN : (i + 1) * SPAN])
            done[h].append(split(mm3(own, rest[h])))
    solved = [tuple(jnp.concatenate([d[k] for d in done[h]], axis=0) for k in range(2)) for h in every]

    eye_channels = (
        lax.broadcasted_iota(jnp.int32, (channels, channels), 0)
        == lax.broadcasted_iota(jnp.int32, (channels, channels), 1)
    ).astype(F32)
    for h in every:
        summary = mm3(solved[h], ends_k[h], TN)
        stack[h, :half] = summary[channels : channels + half]
        stack[h, half : half + channels] = keeps[h] * eye_channels - summary[:channels]
        stack[h, half + channels :] = summary[channels + half :]

    pl.semaphore_wait(barrier, GROUP + n_groups - 2)

    def map_copy(k):
        to = lax.rem(member + k, GROUP)
        start = pl.multiple_of((to // X_SIZE) * half, half)
        return pltpu.make_async_remote_copy(
            src_ref=stack.at[lax.rem(to, X_SIZE), pl.ds(start, channels + half), :],
            dst_ref=maps.at[member],
            send_sem=xs_sem.at[k], recv_sem=xr_sem.at[member],
            device_id=mate(to), device_id_type=MESH,
        )

    sends = [map_copy(k) for k in range(1, GROUP)]
    for copy in sends:
        copy.start()
    maps[member] = stack[x, pl.ds(pl.multiple_of(side * half, half), channels + half), :]

    for h in every:
        combined = mm3(split(jnp.concatenate(score[h], axis=0)), solved[h])
        lift[h] = full_queries[h] - combined[:, :channels]
        local[h] = combined[:, channels:]

    for k in range(1, GROUP):
        frm = lax.rem(member + k, GROUP)
        pltpu.make_async_remote_copy(
            src_ref=maps.at[frm], dst_ref=maps.at[frm],
            send_sem=xs_sem.at[k], recv_sem=xr_sem.at[frm],
            device_id=mate(frm), device_id_type=MESH,
        ).wait_recv()

    map_at = pl.ds(pl.multiple_of((1 - side) * half, half), channels)
    feed_at = pl.ds(pl.multiple_of(side * channels, channels), half)

    def follow(whole, step):
        moved = mm3_narrow(split(whole), split(step[:channels]))
        return jnp.concatenate([moved[:channels], moved[channels:] + step[channels:]], axis=0)

    steps = [jnp.concatenate([maps[j, map_at, :], maps[j, feed_at, :]], axis=0) for j in range(GROUP)]
    prefixes = [steps[0]]
    late = [steps[X_SIZE]]
    for j in range(1, X_SIZE):
        prefixes.append(follow(prefixes[-1], steps[j]))
        late.append(follow(late[-1], steps[X_SIZE + j]))
    total[...] = follow(prefixes[-1], late[-1])

    def total_copy(k, only_feed):
        span = pl.ds(channels, half) if only_feed else pl.ds(0, channels + half)
        return pltpu.make_async_remote_copy(
            src_ref=total.at[span, :], dst_ref=others.at[group, span, :],
            send_sem=zs_sem.at[k], recv_sem=zr_sem.at[group],
            device_id=at(lax.rem(me + k * GROUP, n_ctx)), device_id_type=MESH,
        )

    def for_later_groups(act):
        for k in range(1, n_groups):
            @pl.when((group > 0) & (group + k < n_groups))
            def _():
                act(total_copy(k, False))

        @pl.when(group == 0)
        def _():
            for k in range(1, n_groups):
                act(total_copy(k, True))

    for_later_groups(lambda copy: copy.start())
    for j in range(X_SIZE - 1):
        prefixes.append(follow(prefixes[X_SIZE - 1], late[j]))
    into = split(jnp.concatenate([p[:channels] for p in prefixes], axis=1))

    state[...] = jnp.zeros_like(state)
    for frm in range(n_groups - 1):
        @pl.when(group > frm)
        def _():
            span = pl.ds(channels, half) if frm == 0 else pl.ds(0, channels + half)
            pltpu.make_async_remote_copy(
                src_ref=total.at[span, :], dst_ref=others.at[frm, span, :],
                send_sem=zs_sem.at[0], recv_sem=zr_sem.at[frm],
                device_id=at(lax.rem(me + GROUP, n_ctx)), device_id_type=MESH,
            ).wait_recv()
            feed = others[frm, pl.ds(channels, half), :]
            if frm:
                feed = feed + mm3_narrow(split(state[...]), split(others[frm, pl.ds(0, channels), :]))
            state[...] = feed

    start_state = state[...]
    moved = mm3_narrow(split(start_state), into)
    entry_out[0] = start_state
    for j in range(1, GROUP):
        entry_out[j] = moved[:, (j - 1) * channels : j * channels] + prefixes[j - 1][channels:]

    def entry_copy(k):
        to = lax.rem(member + k, GROUP)
        return pltpu.make_async_remote_copy(
            src_ref=entry_out.at[to], dst_ref=entry.at[member],
            send_sem=bs_sem.at[k], recv_sem=br_sem.at[member],
            device_id=mate(to), device_id_type=MESH,
        )

    returns = [entry_copy(k) for k in range(1, GROUP)]
    for copy in returns:
        copy.start()
    entry[member] = entry_out[member]
    for k in range(1, GROUP):
        frm = lax.rem(member + k, GROUP)
        pltpu.make_async_remote_copy(
            src_ref=entry_out.at[frm], dst_ref=entry.at[frm],
            send_sem=bs_sem.at[k], recv_sem=br_sem.at[frm],
            device_id=mate(frm), device_id_type=MESH,
        ).wait_recv()

    for h in every:
        incoming = jnp.concatenate([entry[h], entry[X_SIZE + h]], axis=0)
        result = local[h] + mm3_narrow(split(lift[h]), split(incoming), NT)
        mean = jnp.mean(result * result, axis=-1, keepdims=True)
        scaled = result * lax.rsqrt(mean + 1e-05) * gain_ref[...]
        out_ref[:, h * channels : (h + 1) * channels] = scaled.astype(BF16)

    for copy in sends + returns:
        copy.wait_send()
    for_later_groups(lambda copy: copy.wait_send())


def delta(ext, low, beta, conv_weight, gate_up, a_log, dt_bias, norm_gain, prompt_lengths):
    rows = low.shape[0]
    heads = a_log.shape[0]
    channels = norm_gain.shape[0]
    n_groups = lax.axis_size("ctx") // GROUP
    half = channels // 2
    return pl.pallas_call(
        delta_kernel,
        out_shape=jax.ShapeDtypeStruct((rows, heads * channels), BF16),
        in_specs=[SMEM, SMEM] + [VMEM] * 7,
        out_specs=VMEM,
        scratch_shapes=[
            pltpu.VMEM((heads, 2 * channels, channels), F32),
            pltpu.VMEM((heads, rows, channels), F32),
            pltpu.VMEM((heads, rows, channels), F32),
            pltpu.VMEM((GROUP, channels + half, channels), F32),
            pltpu.VMEM((channels + half, channels), F32),
            pltpu.VMEM((n_groups, channels + half, channels), F32),
            pltpu.VMEM((half, channels), F32),
            pltpu.VMEM((GROUP, half, channels), F32),
            pltpu.VMEM((GROUP, half, channels), F32),
            pltpu.SemaphoreType.DMA((GROUP,)),
            pltpu.SemaphoreType.DMA((GROUP,)),
            pltpu.SemaphoreType.DMA((n_groups,)),
            pltpu.SemaphoreType.DMA((n_groups,)),
            pltpu.SemaphoreType.DMA((GROUP,)),
            pltpu.SemaphoreType.DMA((GROUP,)),
        ],
        compiler_params=pltpu.CompilerParams(
            collective_id=1, has_side_effects=True, vmem_limit_bytes=48 * 1024 * 1024
        ),
        name="delta",
    )(
        prompt_lengths, a_log, ext, low, beta, conv_weight, gate_up,
        dt_bias.reshape(1, -1), norm_gain.reshape(1, -1),
    )


def on_device(
    hidden, qkv_weight, conv_weight, w_beta, gate_down, gate_up,
    a_log, dt_bias, norm_gain, prompt_lengths, send_slot, gather_src,
):
    ext, low, beta = gather_and_project(hidden.T, qkv_weight, gate_down, w_beta.T, send_slot, gather_src)
    return delta(
        ext, low, beta, conv_weight.transpose(1, 0, 2), gate_up, a_log, dt_bias, norm_gain, prompt_lengths
    )


def solution(mesh):
    placed = (
        P("ctx", "head"),
        P(None, None, "head"),
        P(None, None, "head"),
        P(None, "head"),
        P(),
        P(None, "head"),
        P("head"),
        P("head"),
        P(),
        P(),
        P("ctx"),
        P("ctx"),
    )
    return jax.shard_map(
        on_device, mesh=mesh, in_specs=placed, out_specs=P("ctx", "head"), check_vma=False
    )
```

```python
import functools

import jax
import jax.numpy as jnp
from jax import lax
from jax.experimental import pallas as pl
from jax.experimental.pallas import tpu as pltpu
from jax.sharding import PartitionSpec as P

CONV = 4
SPAN = 64
RIM = 8
X_SIZE = 4
CORES = 2
GROUP = 8
MESH = pl.DeviceIdType.MESH
F32 = jnp.float32
BF16 = jnp.bfloat16
SMEM = pl.BlockSpec(memory_space=pltpu.SMEM)
HBM = pl.BlockSpec(memory_space=pltpu.HBM)

NN = (((1,), (0,)), ((), ()))
NT = (((1,), (1,)), ((), ()))
TN = (((0,), (0,)), ((), ()))


def mm(a, b, dims=NN):
    return lax.dot_general(a, b, dims, preferred_element_type=F32)


def split(v):
    high = v.astype(BF16)
    return high, (v - high.astype(F32)).astype(BF16)


def mm3(a, b, dims=NN):
    return mm(a[0], b[0], dims) + (mm(a[0], b[1], dims) + mm(a[1], b[0], dims))


def mm3_narrow(a, b, dims=NN):
    axis = dims[0][1][0]
    wide = mm(jnp.concatenate(a, axis=1), jnp.concatenate([b[0], b[0]], axis=axis), dims)
    return wide + mm(a[0], b[1], dims)


def fused_kernel(
    lengths_ref, rate_ref, slot_hbm, src_hbm, hidden_hbm, wqkv_hbm, wdown_hbm, wbeta_hbm,
    conv_hbm, up_hbm, bias_hbm, gain_hbm,
    out_hbm,
    slot_buf, src_buf, hidden_buf, w_qkv, w_down, wbeta_buf, conv_ref, up_ref, bias_ref, gain_ref,
    send_buf, landed, shards, w_beta, acc, acc_low, acc_beta, ext_ref,
    stack, local, lift, maps, total, others, state, entry_out, entry, out_buf,
    in_sem, s_sem, r_sem, hs_sem, hr_sem, rim_sem,
    xs_sem, xr_sem, zs_sem, zr_sem, bs_sem, br_sem, out_sem,
):
    n_ctx = lax.axis_size("ctx")
    n_z = n_ctx // X_SIZE
    n_head = lax.axis_size("head")
    n_y = n_head // CORES
    n_groups = n_ctx // GROUP
    me = lax.axis_index("ctx")
    head = lax.axis_index("head")
    z, own_x = me // X_SIZE, lax.rem(me, X_SIZE)
    y, core = head // CORES, lax.rem(head, CORES)
    sibling = y * CORES + (1 - core)
    member = lax.rem(me, GROUP)
    group = me // GROUP
    x, side = lax.rem(member, X_SIZE), member // X_SIZE
    width, rows = hidden_buf.shape
    slots = send_buf.shape[0]
    cap = slots // n_ctx
    heads, _, channels = local.shape
    columns = heads * channels
    half = channels // 2
    blocks = rows // SPAN
    base = me * rows

    def at(ctx):
        return {"ctx": ctx, "head": head}

    def mate(index):
        return at(group * GROUP + index)

    operands = [
        (slot_hbm, slot_buf), (hidden_hbm, hidden_buf), (src_hbm, src_buf), (wbeta_hbm, wbeta_buf),
        (wqkv_hbm, w_qkv), (wdown_hbm, w_down),
        (up_hbm, up_ref), (bias_hbm, bias_ref), (conv_hbm, conv_ref), (gain_hbm, gain_ref),
    ]
    loads = [pltpu.make_async_copy(a, b, in_sem.at[i]) for i, (a, b) in enumerate(operands)]
    for copy in loads:
        copy.start()

    far = sorted(
        ((dz, dx) for dz in range(n_z) for dx in range(X_SIZE) if dz or dx),
        key=lambda d: -(min(d[0], n_z - d[0]) * 2 + min(d[1], X_SIZE - d[1])),
    )
    peers = [lax.rem(z + dz, n_z) * X_SIZE + lax.rem(own_x + dx, X_SIZE) for dz, dx in far]
    ring = {dy: lax.rem(y + dy, n_y) for dy in range(n_y)}

    barrier = pltpu.get_barrier_semaphore()
    for to in peers:
        pl.semaphore_signal(barrier, inc=1, device_id=at(to), device_id_type=MESH)
    for to in (ring[1] * CORES + core, ring[n_y - 1] * CORES + core, sibling):
        pl.semaphore_signal(barrier, inc=1, device_id={"ctx": me, "head": to}, device_id_type=MESH)

    for copy in loads[:4]:
        copy.wait()
    slot_ids = lax.broadcasted_iota(jnp.int32, (slots, rows), 0)
    place = (slot_ids == slot_buf[...]).astype(F32).astype(BF16)
    send_buf[...] = mm(place, hidden_buf[...], NT).astype(BF16)
    pick = (slot_ids == src_buf[...]).astype(F32).astype(BF16)
    pair = CORES * width
    w_beta[...] = jnp.zeros_like(w_beta)
    for i in range(n_y):
        w_beta[i, : wbeta_buf.shape[0], :] = wbeta_buf[:, i * pair : (i + 1) * pair]

    pl.semaphore_wait(barrier, n_ctx - 1 + 3)

    def slots_of(index):
        return pl.ds(pl.multiple_of(index * cap, cap), cap)

    def slot_copy(to, frm):
        return pltpu.make_async_remote_copy(
            src_ref=send_buf.at[slots_of(to), :], dst_ref=landed.at[slots_of(frm), :],
            send_sem=s_sem.at[to], recv_sem=r_sem.at[frm],
            device_id=at(to), device_id_type=MESH,
        )

    for to in peers:
        slot_copy(to, me).start()
    landed[slots_of(me), :] = send_buf[slots_of(me), :]
    for frm in reversed(peers):
        slot_copy(frm, frm).wait_recv()

    def features(index, start=0, size=None):
        return pl.ds(pl.multiple_of(index * width + start, 16), width if size is None else size)

    shards[features(head), :] = mm(landed[...], pick, TN).astype(BF16)
    middle = width // 2

    def shard_copy(index, to, send, recv, start=0, size=None):
        return pltpu.make_async_remote_copy(
            src_ref=shards.at[features(index, start, size), :],
            dst_ref=shards.at[features(index, start, size), :],
            send_sem=hs_sem.at[send], recv_sem=hr_sem.at[recv],
            device_id={"ctx": me, "head": to}, device_id_type=MESH,
        )

    here = [ring[dy] * CORES + core for dy in range(n_y)]
    there = [ring[dy] * CORES + (1 - core) for dy in range(n_y)]
    up_y, down_y = here[1], here[n_y - 1]
    passed = [
        shard_copy(head, up_y, 0, n_y - 1),
        shard_copy(head, down_y, 1, 1),
        shard_copy(head, sibling, 2, n_y + 1),
    ]
    for copy in passed:
        copy.start()
    for copy in loads[4:6]:
        copy.wait()

    def multiply(dy, first=False):
        part = shards[pl.ds(pl.multiple_of(ring[dy] * pair, 16), pair), :].T
        chunk = pl.ds(pl.multiple_of(ring[dy] * pair, 16), pair)
        products = [mm(part, w_qkv[j, chunk, :]) for j in range(3)]
        low = mm(part, w_down[chunk, :])
        beta = mm(part, w_beta[ring[dy]], NT)
        for j in range(3):
            acc[j] = products[j] if first else acc[j] + products[j]
        acc_low[...] = low if first else acc_low[...] + low
        acc_beta[...] = beta if first else acc_beta[...] + beta

    def pass_on(copy):
        copy.start()
        passed.append(copy)

    shard_copy(there[0], sibling, 2, n_y + 1).wait_recv()
    multiply(0, True)
    shard_copy(here[3], sibling, 3, 3).wait_recv()
    pass_on(shard_copy(here[3], up_y, 3, 2, 0, middle))
    pass_on(shard_copy(here[3], sibling, 4, n_y + 1 + 3))
    shard_copy(here[1], sibling, 5, 1).wait_recv()
    pass_on(shard_copy(here[1], down_y, 5, n_y, middle, width - middle))
    pass_on(shard_copy(here[1], sibling, 6, n_y + 1 + 1))
    shard_copy(there[3], sibling, 4, n_y + 1 + 3).wait_recv()
    multiply(3)
    shard_copy(here[2], sibling, 7, 2, 0, middle).wait_recv()
    shard_copy(here[2], sibling, 7, n_y, middle, width - middle).wait_recv()
    pass_on(shard_copy(here[2], sibling, 7, n_y + 1 + 2))
    shard_copy(there[1], sibling, 6, n_y + 1 + 1).wait_recv()
    multiply(1)
    shard_copy(there[2], sibling, 7, n_y + 1 + 2).wait_recv()
    multiply(2)

    for j in range(3):
        ext_ref[RIM:, j * columns : (j + 1) * columns] = acc[j].astype(BF16).astype(F32)
    rim = pltpu.make_async_remote_copy(
        src_ref=ext_ref.at[pl.ds(rows, RIM), :], dst_ref=ext_ref.at[pl.ds(0, RIM), :],
        send_sem=rim_sem.at[0], recv_sem=rim_sem.at[1],
        device_id=at(lax.rem(me + 1, n_ctx)), device_id_type=MESH,
    )
    rim.start()
    for copy in loads[6:]:
        copy.wait()

    ends, total_len = [], 0
    for i in range(lengths_ref.shape[0]):
        total_len = total_len + lengths_ref[i]
        ends.append(total_len)

    def doc_of(positions):
        ended = sum((positions >= end).astype(jnp.int32) for end in ends)
        return jnp.where(positions < 0, -1, ended)

    pos = base + lax.broadcasted_iota(jnp.int32, (rows, channels), 0)
    doc = doc_of(pos)
    valid = [None] + [(doc_of(pos - shift) == doc).astype(F32) for shift in range(1, CONV)]
    before = doc_of(jnp.zeros((1, channels), jnp.int32) + (base - 1))
    final = doc_of(jnp.zeros((1, channels), jnp.int32) + (base + rows - 1))
    first_doc = (doc == before).astype(F32)
    last_doc = (doc == final).astype(F32)
    carry = (final == before).astype(F32)
    row = lax.broadcasted_iota(jnp.int32, (rows, rows), 0)
    col = lax.broadcasted_iota(jnp.int32, (rows, rows), 1)
    col_doc = doc_of(base + lax.broadcasted_iota(jnp.int32, (1, rows), 1))
    same = jnp.concatenate([doc, doc], axis=1) == col_doc
    strict = (row > col) & same
    inclusive = (row >= col) & same
    apart = row ^ col
    running = ((row >= col) & (apart < SPAN)).astype(F32).astype(BF16)
    small_row = lax.broadcasted_iota(jnp.int32, (SPAN, rows), 0)
    small_col = lax.broadcasted_iota(jnp.int32, (SPAN, rows), 1)
    small_apart = small_row ^ (small_col & (SPAN - 1))
    small_block = small_col // SPAN
    small_eye = (small_apart == 0).astype(F32)

    def activated(j):
        lanes = slice(j * columns, (j + 1) * columns)
        out = None
        for tap in range(CONV):
            shift = CONV - 1 - tap
            part = conv_ref[j, tap : tap + 1, :] * ext_ref[pl.ds(RIM - shift, rows), lanes]
            if shift:
                part = part * jnp.concatenate([valid[shift]] * heads, axis=1)
            out = part if out is None else out + part
        return out / (1.0 + jnp.exp(-out))

    def of_head(v, h):
        return v[:, h * channels : (h + 1) * channels]

    def unit(v):
        return v * lax.rsqrt(jnp.sum(v * v, axis=-1, keepdims=True) + 1e-06)

    def block(v, b):
        return v[b * SPAN : (b + 1) * SPAN]

    drive = mm(acc_low[...].astype(BF16), up_ref[...]) + bias_ref[...]
    soft = jnp.maximum(drive, 0.0) + jnp.log1p(jnp.exp(-jnp.abs(drive)))
    rates = jnp.concatenate(
        [jnp.exp(jnp.full((1, channels), rate_ref[h], F32)) for h in range(heads)], axis=1
    )
    decay = -rates * soft
    d_high, d_mid = split(decay)
    d_low = (decay - d_high.astype(F32) - d_mid.astype(F32)).astype(BF16)
    cum_all = mm(running, d_high) + (mm(running, d_mid) + mm(running, d_low))
    betas = 1.0 / (1.0 + jnp.exp(-acc_beta[...]))
    rim.wait_recv()
    acts = [activated(j) for j in range(3)]

    every = range(heads)
    cums = [of_head(cum_all, h) for h in every]
    strengths = [jnp.broadcast_to(betas[:, h : h + 1], (rows, channels)) for h in every]
    queries = [unit(of_head(acts[0], h)) * channels ** (-0.5) for h in every]
    keys = [unit(of_head(acts[1], h)) for h in every]
    values = [strengths[h] * of_head(acts[2], h) for h in every]
    lasts = [[cums[h][(b + 1) * SPAN - 1 : (b + 1) * SPAN] for b in range(blocks)] for h in every]
    nothing = jnp.zeros((1, channels), F32)

    lower, score, solved = [], [], []
    bk_ups, q_ups, tails = [], [], []
    for h in every:
        grow = jnp.exp(cums[h])
        bk_ups.append(strengths[h] * keys[h] * grow)
        q_ups.append(queries[h] * grow)
        key_down = keys[h] * jnp.exp(-cums[h])
        tails.append([block(keys[h], b) * jnp.exp(lasts[h][b] - block(cums[h], b)) for b in range(blocks)])
        mixes, reads = [], []
        for i in range(blocks):
            cols = []
            for b in range(blocks):
                if b < i - 1:
                    cols.append(tails[h][b] * jnp.exp(sum(lasts[h][b + 1 : i], nothing)))
                elif b == i - 1:
                    cols.append(tails[h][b])
                elif b == i:
                    cols.append(block(key_down, b))
                else:
                    cols.append(jnp.zeros((SPAN, channels), F32))
            left = split(jnp.concatenate([block(bk_ups[h], i), block(q_ups[h], i)], axis=0))
            product = mm3_narrow(left, split(jnp.concatenate(cols, axis=0)), NT)
            mixes.append(jnp.where(block(strict, i), product[:SPAN], 0.0))
            reads.append(jnp.where(block(inclusive, i), product[SPAN:], 0.0))
        lower.append(mixes)
        score.append(reads)

    def spread(v):
        return jnp.concatenate(
            [jnp.where(small_block == b, v, 0.0) for b in range(blocks)], axis=0
        )

    def times(lefts, rights):
        return [mm3(split(a), split(spread(b))) for a, b in zip(lefts, rights)]

    diagonal = []
    for h in every:
        picked = jnp.zeros((SPAN, rows), F32)
        for b in range(blocks):
            picked = jnp.where(small_block == b, lower[h][b], picked)
        diagonal.append(picked)
    power = [jnp.where(small_apart < 8, d, 0.0) for d in diagonal]
    inverse = [small_eye - p for p in power]
    power = times(power, power)
    inverse = [i + t for i, t in zip(inverse, times(inverse, power))]
    power = times(power, power)
    inverse = [i + t for i, t in zip(inverse, times(inverse, power))]
    size = 8
    while size < SPAN:
        off = [jnp.where((small_apart >= size) & (small_apart < 2 * size), d, 0.0) for d in diagonal]
        inverse = [i - t for i, t in zip(inverse, times(inverse, times(off, inverse)))]
        size *= 2

    full_keys, full_queries, ends_k, keeps = [], [], [], []
    for h in every:
        prefix = nothing
        k_rows, q_rows, t_rows = [], [], []
        for b in range(blocks):
            scale = jnp.exp(prefix)
            k_rows.append(block(bk_ups[h], b) * scale)
            q_rows.append(block(q_ups[h], b) * scale)
            prefix = prefix + lasts[h][b]
            t_rows.append(tails[h][b] * jnp.exp(sum(lasts[h][b + 1 :], nothing)))
        full_keys.append(jnp.concatenate(k_rows, axis=0) * first_doc)
        full_queries.append(jnp.concatenate(q_rows, axis=0) * first_doc)
        ends_k.append(split(jnp.concatenate(t_rows, axis=0) * last_doc))
        keeps.append(carry * jnp.exp(prefix))
    rights = [jnp.concatenate([full_keys[h], values[h]], axis=1) for h in every]
    done = [[] for _ in every]
    for i in range(blocks):
        rest = []
        for h in every:
            part = block(rights[h], i)
            if i:
                seen = tuple(jnp.concatenate([d[k] for d in done[h]], axis=0) for k in range(2))
                part = part - mm3(split(lower[h][i][:, : i * SPAN]), seen)
            rest.append(split(part))
        for h in every:
            own = split(inverse[h][:, i * SPAN : (i + 1) * SPAN])
            done[h].append(split(mm3(own, rest[h])))
    solved = [tuple(jnp.concatenate([d[k] for d in done[h]], axis=0) for k in range(2)) for h in every]

    eye_channels = (
        lax.broadcasted_iota(jnp.int32, (channels, channels), 0)
        == lax.broadcasted_iota(jnp.int32, (channels, channels), 1)
    ).astype(F32)
    for h in every:
        summary = mm3(solved[h], ends_k[h], TN)
        stack[h, :half] = summary[channels : channels + half]
        stack[h, half : half + channels] = keeps[h] * eye_channels - summary[:channels]
        stack[h, half + channels :] = summary[channels + half :]

    def map_copy(k):
        to = lax.rem(member + k, GROUP)
        start = pl.multiple_of((to // X_SIZE) * half, half)
        return pltpu.make_async_remote_copy(
            src_ref=stack.at[lax.rem(to, X_SIZE), pl.ds(start, channels + half), :],
            dst_ref=maps.at[member],
            send_sem=xs_sem.at[k], recv_sem=xr_sem.at[member],
            device_id=mate(to), device_id_type=MESH,
        )

    sends = [map_copy(k) for k in range(1, GROUP)]
    for copy in sends:
        copy.start()
    maps[member] = stack[x, pl.ds(pl.multiple_of(side * half, half), channels + half), :]

    for h in every:
        combined = mm3(split(jnp.concatenate(score[h], axis=0)), solved[h])
        lift[h] = full_queries[h] - combined[:, :channels]
        local[h] = combined[:, channels:]

    for k in range(1, GROUP):
        frm = lax.rem(member + k, GROUP)
        pltpu.make_async_remote_copy(
            src_ref=maps.at[frm], dst_ref=maps.at[frm],
            send_sem=xs_sem.at[k], recv_sem=xr_sem.at[frm],
            device_id=mate(frm), device_id_type=MESH,
        ).wait_recv()

    map_at = pl.ds(pl.multiple_of((1 - side) * half, half), channels)
    feed_at = pl.ds(pl.multiple_of(side * channels, channels), half)

    def follow(whole, step):
        moved = mm3_narrow(split(whole), split(step[:channels]))
        return jnp.concatenate([moved[:channels], moved[channels:] + step[channels:]], axis=0)

    steps = [jnp.concatenate([maps[j, map_at, :], maps[j, feed_at, :]], axis=0) for j in range(GROUP)]
    prefixes = [steps[0]]
    late = [steps[X_SIZE]]
    for j in range(1, X_SIZE):
        prefixes.append(follow(prefixes[-1], steps[j]))
        late.append(follow(late[-1], steps[X_SIZE + j]))
    total[...] = follow(prefixes[-1], late[-1])

    def total_copy(k, only_feed):
        span = pl.ds(channels, half) if only_feed else pl.ds(0, channels + half)
        return pltpu.make_async_remote_copy(
            src_ref=total.at[span, :], dst_ref=others.at[group, span, :],
            send_sem=zs_sem.at[k], recv_sem=zr_sem.at[group],
            device_id=at(lax.rem(me + k * GROUP, n_ctx)), device_id_type=MESH,
        )

    def for_later_groups(act):
        for k in range(1, n_groups):
            @pl.when((group > 0) & (group + k < n_groups))
            def _():
                act(total_copy(k, False))

        @pl.when(group == 0)
        def _():
            for k in range(1, n_groups):
                act(total_copy(k, True))

    for_later_groups(lambda copy: copy.start())
    for j in range(X_SIZE - 1):
        prefixes.append(follow(prefixes[X_SIZE - 1], late[j]))
    into = split(jnp.concatenate([p[:channels] for p in prefixes], axis=1))

    state[...] = jnp.zeros_like(state)
    for frm in range(n_groups - 1):
        @pl.when(group > frm)
        def _():
            span = pl.ds(channels, half) if frm == 0 else pl.ds(0, channels + half)
            pltpu.make_async_remote_copy(
                src_ref=total.at[span, :], dst_ref=others.at[frm, span, :],
                send_sem=zs_sem.at[0], recv_sem=zr_sem.at[frm],
                device_id=at(lax.rem(me + GROUP, n_ctx)), device_id_type=MESH,
            ).wait_recv()
            feed = others[frm, pl.ds(channels, half), :]
            if frm:
                feed = feed + mm3_narrow(split(state[...]), split(others[frm, pl.ds(0, channels), :]))
            state[...] = feed

    start_state = state[...]
    moved = mm3_narrow(split(start_state), into)
    entry_out[0] = start_state
    for j in range(1, GROUP):
        entry_out[j] = moved[:, (j - 1) * channels : j * channels] + prefixes[j - 1][channels:]

    def entry_copy(k):
        to = lax.rem(member + k, GROUP)
        return pltpu.make_async_remote_copy(
            src_ref=entry_out.at[to], dst_ref=entry.at[member],
            send_sem=bs_sem.at[k], recv_sem=br_sem.at[member],
            device_id=mate(to), device_id_type=MESH,
        )

    returns = [entry_copy(k) for k in range(1, GROUP)]
    for copy in returns:
        copy.start()
    entry[member] = entry_out[member]
    for k in range(1, GROUP):
        frm = lax.rem(member + k, GROUP)
        pltpu.make_async_remote_copy(
            src_ref=entry_out.at[frm], dst_ref=entry.at[frm],
            send_sem=bs_sem.at[k], recv_sem=br_sem.at[frm],
            device_id=mate(frm), device_id_type=MESH,
        ).wait_recv()

    for h in every:
        incoming = jnp.concatenate([entry[h], entry[X_SIZE + h]], axis=0)
        result = local[h] + mm3_narrow(split(lift[h]), split(incoming), NT)
        mean = jnp.mean(result * result, axis=-1, keepdims=True)
        scaled = result * lax.rsqrt(mean + 1e-05) * gain_ref[...]
        lanes = pl.ds(h * channels, channels)
        out_buf[:, lanes] = scaled.astype(BF16)
        pltpu.make_async_copy(out_buf.at[:, lanes], out_hbm.at[:, lanes], out_sem.at[h]).start()

    for to in peers:
        slot_copy(to, me).wait_send()
    for copy in passed + sends + returns:
        copy.wait_send()
    rim.wait_send()
    for_later_groups(lambda copy: copy.wait_send())
    for h in every:
        lanes = pl.ds(h * channels, channels)
        pltpu.make_async_copy(out_buf.at[:, lanes], out_hbm.at[:, lanes], out_sem.at[h]).wait()


def on_device(
    hidden, qkv_weight, conv_weight, w_beta, gate_down, gate_up,
    a_log, dt_bias, norm_gain, prompt_lengths, send_slot, gather_src,
):
    rows, width = hidden.shape
    _, features, columns = qkv_weight.shape
    n_ctx, n_head = lax.axis_size("ctx"), lax.axis_size("head")
    n_y, n_groups = n_head // CORES, n_ctx // GROUP
    heads, channels = a_log.shape[0], norm_gain.shape[0]
    rank = gate_down.shape[1]
    half = channels // 2
    slots = 2 * rows
    dma = pltpu.SemaphoreType.DMA
    return pl.pallas_call(
        fused_kernel,
        out_shape=jax.ShapeDtypeStruct((rows, columns), BF16),
        in_specs=[SMEM, SMEM] + [HBM] * 10,
        out_specs=HBM,
        scratch_shapes=[
            pltpu.VMEM((1, rows), jnp.int32),
            pltpu.VMEM((1, rows), jnp.int32),
            pltpu.VMEM((width, rows), BF16),
            pltpu.VMEM((3, features, columns), BF16),
            pltpu.VMEM((features, rank), BF16),
            pltpu.VMEM((heads, features), BF16),
            pltpu.VMEM((3, CONV, columns), F32),
            pltpu.VMEM((rank, columns), BF16),
            pltpu.VMEM((1, columns), F32),
            pltpu.VMEM((1, channels), F32),
            pltpu.VMEM((slots, width), BF16),
            pltpu.VMEM((slots, width), BF16),
            pltpu.VMEM((features, rows), BF16),
            pltpu.VMEM((n_y, 16, CORES * width), BF16),
            pltpu.VMEM((3, rows, columns), F32),
            pltpu.VMEM((rows, rank), F32),
            pltpu.VMEM((rows, 16), F32),
            pltpu.VMEM((RIM + rows, 3 * columns), F32),
            pltpu.VMEM((heads, 2 * channels, channels), F32),
            pltpu.VMEM((heads, rows, channels), F32),
            pltpu.VMEM((heads, rows, channels), F32),
            pltpu.VMEM((GROUP, channels + half, channels), F32),
            pltpu.VMEM((channels + half, channels), F32),
            pltpu.VMEM((n_groups, channels + half, channels), F32),
            pltpu.VMEM((half, channels), F32),
            pltpu.VMEM((GROUP, half, channels), F32),
            pltpu.VMEM((GROUP, half, channels), F32),
            pltpu.VMEM((rows, columns), BF16),
            dma((10,)), dma((n_ctx,)), dma((n_ctx,)), dma((2 * n_y,)), dma((2 * n_y + 1,)), dma((2,)),
            dma((GROUP,)), dma((GROUP,)), dma((n_groups,)), dma((n_groups,)), dma((GROUP,)), dma((GROUP,)),
            dma((heads,)),
        ],
        compiler_params=pltpu.CompilerParams(
            collective_id=0, has_side_effects=True, vmem_limit_bytes=60 * 1024 * 1024
        ),
        name="delta_prefill",
    )(
        prompt_lengths, a_log, send_slot.reshape(1, rows), gather_src.reshape(1, rows), hidden.T,
        qkv_weight, gate_down, w_beta.T, conv_weight.transpose(1, 0, 2), gate_up,
        dt_bias.reshape(1, columns), norm_gain.reshape(1, channels),
    )


def solution(mesh):
    placed = (
        P("ctx", "head"),
        P(None, None, "head"),
        P(None, None, "head"),
        P(None, "head"),
        P(),
        P(None, "head"),
        P("head"),
        P("head"),
        P(),
        P(),
        P("ctx"),
        P("ctx"),
    )
    return jax.shard_map(
        on_device, mesh=mesh, in_specs=placed, out_specs=P("ctx", "head"), check_vma=False
    )
```

```python
import functools

import jax
import jax.numpy as jnp
from jax import lax
from jax.experimental import pallas as pl
from jax.experimental.pallas import tpu as pltpu
from jax.sharding import PartitionSpec as P

CONV = 4
SPAN = 64
RIM = 8
X_SIZE = 4
CORES = 2
GROUP = 8
KEEP = 16
MESH = pl.DeviceIdType.MESH
F32 = jnp.float32
BF16 = jnp.bfloat16
SMEM = pl.BlockSpec(memory_space=pltpu.SMEM)
HBM = pl.BlockSpec(memory_space=pltpu.HBM)

NN = (((1,), (0,)), ((), ()))
NT = (((1,), (1,)), ((), ()))
TN = (((0,), (0,)), ((), ()))


def mm(a, b, dims=NN):
    return lax.dot_general(a, b, dims, preferred_element_type=F32)


def split(v):
    high = v.astype(BF16)
    return high, (v - high.astype(F32)).astype(BF16)


def mm3(a, b, dims=NN):
    return mm(a[0], b[0], dims) + (mm(a[0], b[1], dims) + mm(a[1], b[0], dims))


def mm3_narrow(a, b, dims=NN):
    axis = dims[0][1][0]
    wide = mm(jnp.concatenate(a, axis=1), jnp.concatenate([b[0], b[0]], axis=axis), dims)
    return wide + mm(a[0], b[1], dims)


def fused_kernel(
    lengths_ref, rate_ref, slot_hbm, src_hbm, hidden_hbm, wqkv_hbm, wdown_hbm, wbeta_hbm,
    conv_hbm, up_hbm, bias_hbm, gain_hbm,
    out_hbm,
    slot_buf, src_buf, hidden_buf, w_qkv, w_down, wbeta_buf, conv_ref, up_ref, bias_ref, gain_ref,
    send_buf, landed, shards, w_beta, acc, acc_low, acc_beta, ext_ref,
    stack, local, lift, maps, total, others, state, entry_out, entry, out_buf,
    in_sem, s_sem, r_sem, hs_sem, hr_sem, rim_sem,
    xs_sem, xr_sem, zs_sem, zr_sem, bs_sem, br_sem, out_sem,
):
    n_ctx = lax.axis_size("ctx")
    n_z = n_ctx // X_SIZE
    n_head = lax.axis_size("head")
    n_y = n_head // CORES
    n_groups = n_ctx // GROUP
    me = lax.axis_index("ctx")
    head = lax.axis_index("head")
    z, own_x = me // X_SIZE, lax.rem(me, X_SIZE)
    y, core = head // CORES, lax.rem(head, CORES)
    sibling = y * CORES + (1 - core)
    member = lax.rem(me, GROUP)
    group = me // GROUP
    x, side = lax.rem(member, X_SIZE), member // X_SIZE
    width, rows = hidden_buf.shape
    slots = send_buf.shape[0]
    cap = slots // n_ctx
    heads, _, channels = local.shape
    columns = heads * channels
    half = channels // 2
    blocks = rows // SPAN
    base = me * rows

    def at(ctx):
        return {"ctx": ctx, "head": head}

    def mate(index):
        return at(group * GROUP + index)

    operands = [
        (slot_hbm, slot_buf), (hidden_hbm, hidden_buf), (src_hbm, src_buf), (wbeta_hbm, wbeta_buf),
        (wqkv_hbm, w_qkv), (wdown_hbm, w_down),
        (up_hbm, up_ref), (bias_hbm, bias_ref), (conv_hbm, conv_ref), (gain_hbm, gain_ref),
    ]
    loads = [pltpu.make_async_copy(a, b, in_sem.at[i]) for i, (a, b) in enumerate(operands)]
    for copy in loads:
        copy.start()

    far = sorted(
        ((dz, dx) for dz in range(n_z) for dx in range(X_SIZE) if dz or dx),
        key=lambda d: -(min(d[0], n_z - d[0]) * 2 + min(d[1], X_SIZE - d[1])),
    )
    peers = [lax.rem(z + dz, n_z) * X_SIZE + lax.rem(own_x + dx, X_SIZE) for dz, dx in far]
    ring = {dy: lax.rem(y + dy, n_y) for dy in range(n_y)}

    barrier = pltpu.get_barrier_semaphore()
    for to in peers:
        pl.semaphore_signal(barrier, inc=1, device_id=at(to), device_id_type=MESH)
    for to in (ring[1] * CORES + core, ring[n_y - 1] * CORES + core, sibling):
        pl.semaphore_signal(barrier, inc=1, device_id={"ctx": me, "head": to}, device_id_type=MESH)

    for copy in loads[:4]:
        copy.wait()
    slot_ids = lax.broadcasted_iota(jnp.int32, (slots, rows), 0)
    place = (slot_ids == slot_buf[...]).astype(F32).astype(BF16)
    send_buf[...] = mm(place, hidden_buf[...], NT).astype(BF16)
    pick = (slot_ids == src_buf[...]).astype(F32).astype(BF16)
    pair = CORES * width
    w_beta[...] = jnp.zeros_like(w_beta)
    for i in range(n_y):
        w_beta[i, : wbeta_buf.shape[0], :] = wbeta_buf[:, i * pair : (i + 1) * pair]

    pl.semaphore_wait(barrier, n_ctx - 1 + 3)

    def slots_of(index):
        return pl.ds(pl.multiple_of(index * cap, cap), cap)

    def slot_copy(to, frm):
        return pltpu.make_async_remote_copy(
            src_ref=send_buf.at[slots_of(to), :], dst_ref=landed.at[slots_of(frm), :],
            send_sem=s_sem.at[to], recv_sem=r_sem.at[frm],
            device_id=at(to), device_id_type=MESH,
        )

    for to in peers:
        slot_copy(to, me).start()
    landed[slots_of(me), :] = send_buf[slots_of(me), :]
    for frm in reversed(peers):
        slot_copy(frm, frm).wait_recv()

    def features(index, start=0, size=None):
        return pl.ds(pl.multiple_of(index * width + start, 16), width if size is None else size)

    shards[features(head), :] = mm(landed[...], pick, TN).astype(BF16)
    middle = width // 2

    def shard_copy(index, to, send, recv, start=0, size=None):
        return pltpu.make_async_remote_copy(
            src_ref=shards.at[features(index, start, size), :],
            dst_ref=shards.at[features(index, start, size), :],
            send_sem=hs_sem.at[send], recv_sem=hr_sem.at[recv],
            device_id={"ctx": me, "head": to}, device_id_type=MESH,
        )

    here = [ring[dy] * CORES + core for dy in range(n_y)]
    there = [ring[dy] * CORES + (1 - core) for dy in range(n_y)]
    up_y, down_y = here[1], here[n_y - 1]
    passed = [
        shard_copy(head, up_y, 0, n_y - 1),
        shard_copy(head, down_y, 1, 1),
        shard_copy(head, sibling, 2, n_y + 1),
    ]
    for copy in passed:
        copy.start()
    for copy in loads[4:6]:
        copy.wait()

    def multiply(dy, first=False):
        part = shards[pl.ds(pl.multiple_of(ring[dy] * pair, 16), pair), :].T
        chunk = pl.ds(pl.multiple_of(ring[dy] * pair, 16), pair)
        products = [mm(part, w_qkv[j, chunk, :]) for j in range(3)]
        low = mm(part, w_down[chunk, :])
        beta = mm(part, w_beta[ring[dy]], NT)
        for j in range(3):
            acc[j] = products[j] if first else acc[j] + products[j]
        acc_low[...] = low if first else acc_low[...] + low
        acc_beta[...] = beta if first else acc_beta[...] + beta

    def pass_on(copy):
        copy.start()
        passed.append(copy)

    shard_copy(there[0], sibling, 2, n_y + 1).wait_recv()
    multiply(0, True)
    shard_copy(here[3], sibling, 3, 3).wait_recv()
    pass_on(shard_copy(here[3], up_y, 3, 2, 0, middle))
    pass_on(shard_copy(here[3], sibling, 4, n_y + 1 + 3))
    shard_copy(here[1], sibling, 5, 1).wait_recv()
    pass_on(shard_copy(here[1], down_y, 5, n_y, middle, width - middle))
    pass_on(shard_copy(here[1], sibling, 6, n_y + 1 + 1))
    shard_copy(there[3], sibling, 4, n_y + 1 + 3).wait_recv()
    multiply(3)
    shard_copy(here[2], sibling, 7, 2, 0, middle).wait_recv()
    shard_copy(here[2], sibling, 7, n_y, middle, width - middle).wait_recv()
    pass_on(shard_copy(here[2], sibling, 7, n_y + 1 + 2))
    shard_copy(there[1], sibling, 6, n_y + 1 + 1).wait_recv()
    multiply(1)
    shard_copy(there[2], sibling, 7, n_y + 1 + 2).wait_recv()
    multiply(2)

    for j in range(3):
        ext_ref[RIM:, j * columns : (j + 1) * columns] = acc[j].astype(BF16).astype(F32)
    rim = pltpu.make_async_remote_copy(
        src_ref=ext_ref.at[pl.ds(rows, RIM), :], dst_ref=ext_ref.at[pl.ds(0, RIM), :],
        send_sem=rim_sem.at[0], recv_sem=rim_sem.at[1],
        device_id=at(lax.rem(me + 1, n_ctx)), device_id_type=MESH,
    )
    rim.start()
    for copy in loads[6:]:
        copy.wait()

    ends, total_len = [], 0
    for i in range(lengths_ref.shape[0]):
        total_len = total_len + lengths_ref[i]
        ends.append(total_len)

    def doc_of(positions):
        ended = sum((positions >= end).astype(jnp.int32) for end in ends)
        return jnp.where(positions < 0, -1, ended)

    pos = base + lax.broadcasted_iota(jnp.int32, (rows, channels), 0)
    doc = doc_of(pos)
    valid = [None] + [(doc_of(pos - shift) == doc).astype(F32) for shift in range(1, CONV)]
    before = doc_of(jnp.zeros((1, channels), jnp.int32) + (base - 1))
    final = doc_of(jnp.zeros((1, channels), jnp.int32) + (base + rows - 1))
    first_doc = (doc == before).astype(F32)
    last_doc = (doc == final).astype(F32)
    carry = (final == before).astype(F32)
    row = lax.broadcasted_iota(jnp.int32, (rows, rows), 0)
    col = lax.broadcasted_iota(jnp.int32, (rows, rows), 1)
    col_doc = doc_of(base + lax.broadcasted_iota(jnp.int32, (1, rows), 1))
    same = jnp.concatenate([doc, doc], axis=1) == col_doc
    strict = (row > col) & same
    inclusive = (row >= col) & same
    apart = row ^ col
    running = ((row >= col) & (apart < SPAN)).astype(F32).astype(BF16)
    small_row = lax.broadcasted_iota(jnp.int32, (SPAN, rows), 0)
    small_col = lax.broadcasted_iota(jnp.int32, (SPAN, rows), 1)
    small_apart = small_row ^ (small_col & (SPAN - 1))
    small_block = small_col // SPAN
    small_eye = (small_apart == 0).astype(F32)

    every = range(heads)
    nothing = jnp.zeros((1, channels), F32)

    def of_head(v, h):
        return v[:, h * channels : (h + 1) * channels]

    def block(v, b):
        return v[b * SPAN : (b + 1) * SPAN]

    def activated(j, first, size):
        lanes = slice(j * columns, (j + 1) * columns)
        out = None
        for tap in range(CONV):
            shift = CONV - 1 - tap
            part = conv_ref[j, tap : tap + 1, :] * ext_ref[pl.ds(RIM - shift + first, size), lanes]
            if shift:
                part = part * jnp.concatenate([valid[shift][first : first + size]] * heads, axis=1)
            out = part if out is None else out + part
        return out / (1.0 + jnp.exp(-out))

    def unit(v):
        return v * lax.rsqrt(jnp.sum(v * v, axis=-1, keepdims=True) + 1e-06)

    def activations(first, size):
        query, key, value = [activated(j, first, size) for j in range(3)]
        return (
            [unit(of_head(query, h)) * channels ** (-0.5) for h in every],
            [unit(of_head(key, h)) for h in every],
            [of_head(value, h) for h in every],
        )

    drive = mm(acc_low[...].astype(BF16), up_ref[...]) + bias_ref[...]
    soft = jnp.maximum(drive, 0.0) + jnp.log1p(jnp.exp(-jnp.abs(drive)))
    rates = jnp.concatenate([jnp.exp(jnp.full((1, channels), rate_ref[h], F32)) for h in every], axis=1)
    decay = -rates * soft
    d_high, d_mid = split(decay)
    d_low = (decay - d_high.astype(F32) - d_mid.astype(F32)).astype(BF16)
    cum_all = mm(running, d_high) + (mm(running, d_mid) + mm(running, d_low))
    betas = 1.0 / (1.0 + jnp.exp(-acc_beta[...]))
    cums = [of_head(cum_all, h) for h in every]
    strengths = [jnp.broadcast_to(betas[:, h : h + 1], (rows, channels)) for h in every]
    lasts = [[cums[h][(b + 1) * SPAN - 1 : (b + 1) * SPAN] for b in range(blocks)] for h in every]
    grows = [jnp.exp(c) for c in cums]
    shrinks = [jnp.exp(-c) for c in cums]
    fades = [
        jnp.concatenate([jnp.exp(lasts[h][b] - block(cums[h], b)) for b in range(blocks)], axis=0)
        for h in every
    ]
    later_rows = activations(SPAN, rows - SPAN)
    rim.wait_recv()
    first_rows = activations(0, SPAN)
    queries, keys, values = [
        [jnp.concatenate([a, b], axis=0) for a, b in zip(f, l)] for f, l in zip(first_rows, later_rows)
    ]
    values = [strengths[h] * values[h] for h in every]

    lower, score, solved = [], [], []
    bk_ups, q_ups, tails = [], [], []
    for h in every:
        bk_ups.append(strengths[h] * keys[h] * grows[h])
        q_ups.append(queries[h] * grows[h])
        key_down = keys[h] * shrinks[h]
        tail = keys[h] * fades[h]
        tails.append([block(tail, b) for b in range(blocks)])
        mixes, reads = [], []
        for i in range(blocks):
            cols = []
            for b in range(blocks):
                if b < i - 1:
                    cols.append(tails[h][b] * jnp.exp(sum(lasts[h][b + 1 : i], nothing)))
                elif b == i - 1:
                    cols.append(tails[h][b])
                elif b == i:
                    cols.append(block(key_down, b))
                else:
                    cols.append(jnp.zeros((SPAN, channels), F32))
            left = split(jnp.concatenate([block(bk_ups[h], i), block(q_ups[h], i)], axis=0))
            product = mm3_narrow(left, split(jnp.concatenate(cols, axis=0)), NT)
            mixes.append(jnp.where(block(strict, i), product[:SPAN], 0.0))
            reads.append(jnp.where(block(inclusive, i), product[SPAN:], 0.0))
        lower.append(mixes)
        score.append(reads)

    def spread(v):
        return jnp.concatenate(
            [jnp.where(small_block == b, v, 0.0) for b in range(blocks)], axis=0
        )

    def times(lefts, rights):
        return [mm3(split(a), split(spread(b))) for a, b in zip(lefts, rights)]

    diagonal = []
    for h in every:
        picked = jnp.zeros((SPAN, rows), F32)
        for b in range(blocks):
            picked = jnp.where(small_block == b, lower[h][b], picked)
        diagonal.append(picked)
    power = [jnp.where(small_apart < 8, d, 0.0) for d in diagonal]
    inverse = [small_eye - p for p in power]
    power = times(power, power)
    inverse = [i + t for i, t in zip(inverse, times(inverse, power))]
    power = times(power, power)
    inverse = [i + t for i, t in zip(inverse, times(inverse, power))]
    size = 8
    while size < SPAN:
        off = [jnp.where((small_apart >= size) & (small_apart < 2 * size), d, 0.0) for d in diagonal]
        inverse = [i - t for i, t in zip(inverse, times(inverse, times(off, inverse)))]
        size *= 2

    full_keys, full_queries, ends_k, keeps = [], [], [], []
    for h in every:
        prefix = nothing
        k_rows, q_rows, t_rows = [], [], []
        for b in range(blocks):
            scale = jnp.exp(prefix)
            k_rows.append(block(bk_ups[h], b) * scale)
            q_rows.append(block(q_ups[h], b) * scale)
            prefix = prefix + lasts[h][b]
            t_rows.append(tails[h][b] * jnp.exp(sum(lasts[h][b + 1 :], nothing)))
        full_keys.append(jnp.concatenate(k_rows, axis=0) * first_doc)
        full_queries.append(jnp.concatenate(q_rows, axis=0) * first_doc)
        ends_k.append(split(jnp.concatenate(t_rows, axis=0) * last_doc))
        keeps.append(carry * jnp.exp(prefix))
    rights = [jnp.concatenate([full_keys[h], values[h]], axis=1) for h in every]
    done = [[] for _ in every]
    for i in range(blocks):
        rest = []
        for h in every:
            part = block(rights[h], i)
            if i:
                seen = tuple(jnp.concatenate([d[k] for d in done[h]], axis=0) for k in range(2))
                part = part - mm3(split(lower[h][i][:, : i * SPAN]), seen)
            rest.append(split(part))
        for h in every:
            own = split(inverse[h][:, i * SPAN : (i + 1) * SPAN])
            done[h].append(split(mm3(own, rest[h])))
    solved = [tuple(jnp.concatenate([d[k] for d in done[h]], axis=0) for k in range(2)) for h in every]

    eye_channels = (
        lax.broadcasted_iota(jnp.int32, (channels, channels), 0)
        == lax.broadcasted_iota(jnp.int32, (channels, channels), 1)
    ).astype(F32)
    keep_at, late_at = half + channels, half + channels + KEEP
    message = late_at

    def keep_rows(keep):
        high, middle = split(keep)
        low = (keep - high.astype(F32) - middle.astype(F32)).astype(BF16)
        return jnp.concatenate([high, middle, low, jnp.zeros((KEEP - 3, channels), BF16)], axis=0)

    def keep_of(rows3):
        wide = rows3.astype(F32)
        return wide[0:1] + (wide[1:2] + wide[2:3])

    for h in every:
        summary = mm3(solved[h], ends_k[h], TN).astype(BF16)
        stack[h, :half, :] = summary[channels : channels + half]
        stack[h, half:keep_at, :] = -summary[:channels]
        stack[h, keep_at:late_at, :] = keep_rows(keeps[h])
        stack[h, late_at:, :] = summary[channels + half :]

    mates = [(1, 2), (1, 1), (1, 3), (0, 2), (1, 0), (0, 1), (0, 3)]
    mates = [lax.rem(side + ds, 2) * X_SIZE + lax.rem(x + dx, X_SIZE) for ds, dx in mates]

    def map_copy(k, to):
        start = pl.multiple_of((to // X_SIZE) * half, half)
        return pltpu.make_async_remote_copy(
            src_ref=stack.at[lax.rem(to, X_SIZE), pl.ds(start, message), :],
            dst_ref=maps.at[member],
            send_sem=xs_sem.at[k], recv_sem=xr_sem.at[member],
            device_id=mate(to), device_id_type=MESH,
        )

    sends = [map_copy(k, to) for k, to in enumerate(mates)]
    for copy in sends:
        copy.start()
    maps[member] = stack[x, pl.ds(pl.multiple_of(side * half, half), message), :]

    for h in every:
        combined = mm3(split(jnp.concatenate(score[h], axis=0)), solved[h])
        lift[h] = full_queries[h] - combined[:, :channels]
        local[h] = combined[:, channels:]

    for frm in mates:
        pltpu.make_async_remote_copy(
            src_ref=maps.at[frm], dst_ref=maps.at[frm],
            send_sem=xs_sem.at[0], recv_sem=xr_sem.at[frm],
            device_id=mate(frm), device_id_type=MESH,
        ).wait_recv()

    map_at = pl.ds(pl.multiple_of((1 - side) * half, half), channels)
    keeps_at = pl.ds(pl.multiple_of(channels + (1 - side) * half, 16), KEEP)
    feed_at = pl.ds(pl.multiple_of(side * (channels + KEEP), 16), half)

    def apply(v, keep, exact_map):
        parts = jnp.concatenate(split(v), axis=1)
        return v * keep + mm(parts, jnp.concatenate([exact_map, exact_map], axis=0))

    def follow(whole, j):
        moved = apply(whole, step_keeps[j], maps[j, map_at, :])
        return jnp.concatenate([moved[:channels], moved[channels:] + maps[j, feed_at, :].astype(F32)], axis=0)

    def single(j):
        return jnp.concatenate(
            [step_keeps[j] * eye_channels + maps[j, map_at, :].astype(F32), maps[j, feed_at, :].astype(F32)], axis=0
        )

    def join(first, second):
        moved = mm3_narrow(split(first), split(second[:channels]))
        return jnp.concatenate([moved[:channels], moved[channels:] + second[channels:]], axis=0)

    step_keeps = [keep_of(maps[j, keeps_at, :]) for j in range(GROUP)]
    prefixes = [single(0)]
    late = [single(X_SIZE)]
    for j in range(1, X_SIZE):
        prefixes.append(follow(prefixes[-1], j))
        late.append(follow(late[-1], X_SIZE + j))
    group_total = join(prefixes[-1], late[-1])
    group_keep = functools.reduce(lambda a, b: a * b, step_keeps)
    total[:channels, :] = (group_total[:channels] - group_keep * eye_channels).astype(BF16)
    total[channels : channels + KEEP, :] = keep_rows(group_keep)
    total[channels + KEEP :, :] = group_total[channels:].astype(BF16)
    whole_span, feed_span = pl.ds(0, message), pl.ds(channels + KEEP, half)

    def total_copy(k, only_feed):
        span = feed_span if only_feed else whole_span
        return pltpu.make_async_remote_copy(
            src_ref=total.at[span, :], dst_ref=others.at[group, span, :],
            send_sem=zs_sem.at[k], recv_sem=zr_sem.at[group],
            device_id=at(lax.rem(me + k * GROUP, n_ctx)), device_id_type=MESH,
        )

    def for_later_groups(act):
        for k in range(1, n_groups):
            @pl.when((group > 0) & (group + k < n_groups))
            def _():
                act(total_copy(k, False))

        @pl.when(group == 0)
        def _():
            for k in range(1, n_groups):
                act(total_copy(k, True))

    for_later_groups(lambda copy: copy.start())
    for j in range(X_SIZE - 1):
        prefixes.append(join(prefixes[X_SIZE - 1], late[j]))
    into = split(jnp.concatenate([p[:channels] for p in prefixes], axis=1))

    state[...] = jnp.zeros_like(state)
    for frm in range(n_groups - 1):
        @pl.when(group > frm)
        def _():
            span = whole_span if frm else feed_span
            pltpu.make_async_remote_copy(
                src_ref=total.at[span, :], dst_ref=others.at[frm, span, :],
                send_sem=zs_sem.at[0], recv_sem=zr_sem.at[frm],
                device_id=at(lax.rem(me + GROUP, n_ctx)), device_id_type=MESH,
            ).wait_recv()
            feed = others[frm, feed_span, :].astype(F32)
            if frm:
                keep = keep_of(others[frm, pl.ds(channels, KEEP), :])
                feed = feed + apply(state[...], keep, others[frm, pl.ds(0, channels), :])
            state[...] = feed

    start_state = state[...]
    moved = mm3_narrow(split(start_state), into)
    entry_out[0] = start_state.astype(BF16)
    for j in range(1, GROUP):
        there_state = moved[:, (j - 1) * channels : j * channels] + prefixes[j - 1][channels:]
        entry_out[j] = there_state.astype(BF16)

    def entry_copy(k, to):
        return pltpu.make_async_remote_copy(
            src_ref=entry_out.at[to], dst_ref=entry.at[member],
            send_sem=bs_sem.at[k], recv_sem=br_sem.at[member],
            device_id=mate(to), device_id_type=MESH,
        )

    returns = [entry_copy(k, to) for k, to in enumerate(mates)]
    for copy in returns:
        copy.start()
    entry[member] = entry_out[member]
    for frm in mates:
        pltpu.make_async_remote_copy(
            src_ref=entry_out.at[frm], dst_ref=entry.at[frm],
            send_sem=bs_sem.at[0], recv_sem=br_sem.at[frm],
            device_id=mate(frm), device_id_type=MESH,
        ).wait_recv()

    for h in every:
        incoming = jnp.concatenate([entry[h], entry[X_SIZE + h]], axis=0)
        parts = jnp.concatenate(split(lift[h]), axis=1)
        result = local[h] + mm(parts, jnp.concatenate([incoming, incoming], axis=1), NT)
        mean = jnp.mean(result * result, axis=-1, keepdims=True)
        scaled = result * lax.rsqrt(mean + 1e-05) * gain_ref[...]
        lanes = pl.ds(h * channels, channels)
        out_buf[:, lanes] = scaled.astype(BF16)
        pltpu.make_async_copy(out_buf.at[:, lanes], out_hbm.at[:, lanes], out_sem.at[h]).start()

    for to in peers:
        slot_copy(to, me).wait_send()
    for copy in passed + sends + returns:
        copy.wait_send()
    rim.wait_send()
    for_later_groups(lambda copy: copy.wait_send())
    for h in every:
        lanes = pl.ds(h * channels, channels)
        pltpu.make_async_copy(out_buf.at[:, lanes], out_hbm.at[:, lanes], out_sem.at[h]).wait()


def on_device(
    hidden, qkv_weight, conv_weight, w_beta, gate_down, gate_up,
    a_log, dt_bias, norm_gain, prompt_lengths, send_slot, gather_src,
):
    rows, width = hidden.shape
    _, features, columns = qkv_weight.shape
    n_ctx, n_head = lax.axis_size("ctx"), lax.axis_size("head")
    n_y, n_groups = n_head // CORES, n_ctx // GROUP
    heads, channels = a_log.shape[0], norm_gain.shape[0]
    rank = gate_down.shape[1]
    half = channels // 2
    message = channels + KEEP + half
    slots = 2 * rows
    dma = pltpu.SemaphoreType.DMA
    return pl.pallas_call(
        fused_kernel,
        out_shape=jax.ShapeDtypeStruct((rows, columns), BF16),
        in_specs=[SMEM, SMEM] + [HBM] * 10,
        out_specs=HBM,
        scratch_shapes=[
            pltpu.VMEM((1, rows), jnp.int32),
            pltpu.VMEM((1, rows), jnp.int32),
            pltpu.VMEM((width, rows), BF16),
            pltpu.VMEM((3, features, columns), BF16),
            pltpu.VMEM((features, rank), BF16),
            pltpu.VMEM((heads, features), BF16),
            pltpu.VMEM((3, CONV, columns), F32),
            pltpu.VMEM((rank, columns), BF16),
            pltpu.VMEM((1, columns), F32),
            pltpu.VMEM((1, channels), F32),
            pltpu.VMEM((slots, width), BF16),
            pltpu.VMEM((slots, width), BF16),
            pltpu.VMEM((features, rows), BF16),
            pltpu.VMEM((n_y, 16, CORES * width), BF16),
            pltpu.VMEM((3, rows, columns), F32),
            pltpu.VMEM((rows, rank), F32),
            pltpu.VMEM((rows, 16), F32),
            pltpu.VMEM((RIM + rows, 3 * columns), F32),
            pltpu.VMEM((heads, 2 * channels + KEEP, channels), BF16),
            pltpu.VMEM((heads, rows, channels), F32),
            pltpu.VMEM((heads, rows, channels), F32),
            pltpu.VMEM((GROUP, message, channels), BF16),
            pltpu.VMEM((message, channels), BF16),
            pltpu.VMEM((n_groups, message, channels), BF16),
            pltpu.VMEM((half, channels), F32),
            pltpu.VMEM((GROUP, half, channels), BF16),
            pltpu.VMEM((GROUP, half, channels), BF16),
            pltpu.VMEM((rows, columns), BF16),
            dma((10,)), dma((n_ctx,)), dma((n_ctx,)), dma((2 * n_y,)), dma((2 * n_y + 1,)), dma((2,)),
            dma((GROUP,)), dma((GROUP,)), dma((n_groups,)), dma((n_groups,)), dma((GROUP,)), dma((GROUP,)),
            dma((heads,)),
        ],
        compiler_params=pltpu.CompilerParams(
            collective_id=0, has_side_effects=True, vmem_limit_bytes=60 * 1024 * 1024
        ),
        name="delta_prefill",
    )(
        prompt_lengths, a_log, send_slot.reshape(1, rows), gather_src.reshape(1, rows), hidden.T,
        qkv_weight, gate_down, w_beta.T, conv_weight.transpose(1, 0, 2), gate_up,
        dt_bias.reshape(1, columns), norm_gain.reshape(1, channels),
    )


def solution(mesh):
    placed = (
        P("ctx", "head"),
        P(None, None, "head"),
        P(None, None, "head"),
        P(None, "head"),
        P(),
        P(None, "head"),
        P("head"),
        P("head"),
        P(),
        P(),
        P("ctx"),
        P("ctx"),
    )
    return jax.shard_map(
        on_device, mesh=mesh, in_specs=placed, out_specs=P("ctx", "head"), check_vma=False
    )
```

```python
import functools

import jax
import jax.numpy as jnp
from jax import lax
from jax.experimental import pallas as pl
from jax.experimental.pallas import tpu as pltpu
from jax.sharding import PartitionSpec as P

CONV = 4
SPAN = 64
RIM = 8
X_SIZE = 4
CORES = 2
GROUP = 8
KEEP = 16
MESH = pl.DeviceIdType.MESH
F32 = jnp.float32
BF16 = jnp.bfloat16
VMEM = pl.BlockSpec(memory_space=pltpu.VMEM)
SMEM = pl.BlockSpec(memory_space=pltpu.SMEM)
HBM = pl.BlockSpec(memory_space=pltpu.HBM)

NN = (((1,), (0,)), ((), ()))
NT = (((1,), (1,)), ((), ()))
TN = (((0,), (0,)), ((), ()))


def mm(a, b, dims=NN):
    return lax.dot_general(a, b, dims, preferred_element_type=F32)


def split(v):
    high = v.astype(BF16)
    return high, (v - high.astype(F32)).astype(BF16)


def mm3(a, b, dims=NN):
    return mm(a[0], b[0], dims) + (mm(a[0], b[1], dims) + mm(a[1], b[0], dims))


def mm3_narrow(a, b, dims=NN):
    axis = dims[0][1][0]
    wide = mm(jnp.concatenate(a, axis=1), jnp.concatenate([b[0], b[0]], axis=axis), dims)
    return wide + mm(a[0], b[1], dims)


def fused_kernel(
    lengths_ref, rate_ref, slot_hbm, src_hbm, hidden_hbm, wqkv_hbm, wdown_hbm, wbeta_hbm,
    conv_hbm, up_hbm, bias_hbm, gain_hbm,
    out_ref,
    slot_buf, src_buf, hidden_buf, w_qkv, w_down, wbeta_buf, conv_ref, up_ref, bias_ref, gain_ref,
    send_buf, landed, shards, w_beta, acc, acc_low, acc_beta, ext_ref,
    stack, local, lift, maps, total, others, state, entry_out, entry,
    in_sem, s_sem, r_sem, hs_sem, hr_sem, rim_sem,
    xs_sem, xr_sem, zs_sem, zr_sem, bs_sem, br_sem,
):
    n_ctx = lax.axis_size("ctx")
    n_z = n_ctx // X_SIZE
    n_head = lax.axis_size("head")
    n_y = n_head // CORES
    n_groups = n_ctx // GROUP
    me = lax.axis_index("ctx")
    head = lax.axis_index("head")
    z, own_x = me // X_SIZE, lax.rem(me, X_SIZE)
    y, core = head // CORES, lax.rem(head, CORES)
    sibling = y * CORES + (1 - core)
    member = lax.rem(me, GROUP)
    group = me // GROUP
    x, side = lax.rem(member, X_SIZE), member // X_SIZE
    width, rows = hidden_buf.shape
    slots = send_buf.shape[0]
    cap = slots // n_ctx
    heads, _, channels = local.shape
    columns = heads * channels
    half = channels // 2
    blocks = rows // SPAN
    base = me * rows

    def at(ctx):
        return {"ctx": ctx, "head": head}

    def mate(index):
        return at(group * GROUP + index)

    operands = [
        (slot_hbm, slot_buf), (hidden_hbm, hidden_buf), (src_hbm, src_buf), (wbeta_hbm, wbeta_buf),
        (wqkv_hbm, w_qkv), (wdown_hbm, w_down),
        (up_hbm, up_ref), (bias_hbm, bias_ref), (conv_hbm, conv_ref), (gain_hbm, gain_ref),
    ]
    loads = [pltpu.make_async_copy(a, b, in_sem.at[i]) for i, (a, b) in enumerate(operands)]
    for copy in loads:
        copy.start()

    far = sorted(
        ((dz, dx) for dz in range(n_z) for dx in range(X_SIZE) if dz or dx),
        key=lambda d: -(min(d[0], n_z - d[0]) * 2 + min(d[1], X_SIZE - d[1])),
    )
    peers = [lax.rem(z + dz, n_z) * X_SIZE + lax.rem(own_x + dx, X_SIZE) for dz, dx in far]
    ring = {dy: lax.rem(y + dy, n_y) for dy in range(n_y)}

    barrier = pltpu.get_barrier_semaphore()
    for to in peers:
        pl.semaphore_signal(barrier, inc=1, device_id=at(to), device_id_type=MESH)
    for to in (ring[1] * CORES + core, ring[n_y - 1] * CORES + core, sibling):
        pl.semaphore_signal(barrier, inc=1, device_id={"ctx": me, "head": to}, device_id_type=MESH)

    for copy in loads[:4]:
        copy.wait()
    slot_ids = lax.broadcasted_iota(jnp.int32, (slots, rows), 0)
    place = (slot_ids == slot_buf[...]).astype(F32).astype(BF16)
    send_buf[...] = mm(place, hidden_buf[...], NT).astype(BF16)
    pick = (slot_ids == src_buf[...]).astype(F32).astype(BF16)
    pair = CORES * width
    w_beta[...] = jnp.zeros_like(w_beta)
    for i in range(n_y):
        w_beta[i, : wbeta_buf.shape[0], :] = wbeta_buf[:, i * pair : (i + 1) * pair]

    pl.semaphore_wait(barrier, n_ctx - 1 + 3)

    def slots_of(index):
        return pl.ds(pl.multiple_of(index * cap, cap), cap)

    def slot_copy(to, frm):
        return pltpu.make_async_remote_copy(
            src_ref=send_buf.at[slots_of(to), :], dst_ref=landed.at[slots_of(frm), :],
            send_sem=s_sem.at[to], recv_sem=r_sem.at[frm],
            device_id=at(to), device_id_type=MESH,
        )

    for to in peers:
        slot_copy(to, me).start()
    landed[slots_of(me), :] = send_buf[slots_of(me), :]
    for frm in reversed(peers):
        slot_copy(frm, frm).wait_recv()

    def features(index, start=0, size=None):
        return pl.ds(pl.multiple_of(index * width + start, 16), width if size is None else size)

    shards[features(head), :] = mm(landed[...], pick, TN).astype(BF16)
    middle = width // 2
    parts_of = ((0, middle), (middle, width - middle))
    passed = []

    def shard_copy(index, to, send, recv, part=None):
        start, size = (0, width) if part is None else parts_of[part]
        return pltpu.make_async_remote_copy(
            src_ref=shards.at[features(index, start, size), :],
            dst_ref=shards.at[features(index, start, size), :],
            send_sem=hs_sem.at[send], recv_sem=hr_sem.at[recv],
            device_id={"ctx": me, "head": to}, device_id_type=MESH,
        )

    def push(index, to, recv, part=None):
        copy = shard_copy(index, to, len(passed), recv, part)
        copy.start()
        passed.append(copy)

    here = [ring[dy] * CORES + core for dy in range(n_y)]
    there = [ring[dy] * CORES + (1 - core) for dy in range(n_y)]
    up_y, down_y, across = here[1], here[n_y - 1], 2 * n_y
    push(head, up_y, 2 * 3, 0)
    push(head, down_y, 2 * 1 + 1, 1)
    push(head, sibling, across)
    push(head, up_y, 2 * 3 + 1, 1)
    push(head, down_y, 2 * 1, 0)
    for copy in loads[4:6]:
        copy.wait()

    def landed_half(dy, part, other=False):
        index, offset = (there[dy], across) if other else (here[dy], 0)
        shard_copy(index, sibling, 0, offset + 2 * dy + part, part).wait_recv()

    def products(dy):
        part = shards[pl.ds(pl.multiple_of(ring[dy] * pair, 16), pair), :].T
        chunk = pl.ds(pl.multiple_of(ring[dy] * pair, 16), pair)
        return [mm(part, w_qkv[j, chunk, :]) for j in range(3)] + [
            mm(part, w_down[chunk, :]), mm(part, w_beta[ring[dy]], NT)
        ]

    def multiply(dy, first=False):
        for ref, value in zip(sums, products(dy)):
            ref[...] = value if first else ref[...] + value

    sums = [acc.at[0], acc.at[1], acc.at[2], acc_low, acc_beta]
    shard_copy(there[0], sibling, 0, across).wait_recv()
    multiply(0, True)
    landed_half(3, 0)
    push(here[3], up_y, 2 * 2, 0)
    landed_half(1, 1)
    push(here[1], down_y, 2 * 2 + 1, 1)
    push(here[3], sibling, across + 2 * 3, 0)
    push(here[1], sibling, across + 2 * 1 + 1, 1)
    landed_half(3, 1)
    push(here[3], sibling, across + 2 * 3 + 1, 1)
    landed_half(1, 0)
    push(here[1], sibling, across + 2 * 1, 0)
    landed_half(3, 0, True)
    landed_half(3, 1, True)
    multiply(3)
    landed_half(2, 0)
    push(here[2], sibling, across + 2 * 2, 0)
    landed_half(2, 1)
    push(here[2], sibling, across + 2 * 2 + 1, 1)
    landed_half(1, 0, True)
    landed_half(1, 1, True)
    multiply(1)
    landed_half(2, 0, True)
    landed_half(2, 1, True)
    last = [ref[...] + value for ref, value in zip(sums, products(2))]
    for j in range(3):
        ext_ref[RIM:, j * columns : (j + 1) * columns] = last[j].astype(BF16).astype(F32)
    low_rank, beta_logit = last[3].astype(BF16), last[4]
    rim = pltpu.make_async_remote_copy(
        src_ref=ext_ref.at[pl.ds(rows, RIM), :], dst_ref=ext_ref.at[pl.ds(0, RIM), :],
        send_sem=rim_sem.at[0], recv_sem=rim_sem.at[1],
        device_id=at(lax.rem(me + 1, n_ctx)), device_id_type=MESH,
    )
    rim.start()
    for copy in loads[6:]:
        copy.wait()

    ends, total_len = [], 0
    for i in range(lengths_ref.shape[0]):
        total_len = total_len + lengths_ref[i]
        ends.append(total_len)

    def doc_of(positions):
        ended = sum((positions >= end).astype(jnp.int32) for end in ends)
        return jnp.where(positions < 0, -1, ended)

    pos = base + lax.broadcasted_iota(jnp.int32, (rows, channels), 0)
    doc = doc_of(pos)
    valid = [None] + [(doc_of(pos - shift) == doc).astype(F32) for shift in range(1, CONV)]
    before = doc_of(jnp.zeros((1, channels), jnp.int32) + (base - 1))
    final = doc_of(jnp.zeros((1, channels), jnp.int32) + (base + rows - 1))
    first_doc = (doc == before).astype(F32)
    last_doc = (doc == final).astype(F32)
    carry = (final == before).astype(F32)
    row = lax.broadcasted_iota(jnp.int32, (rows, rows), 0)
    col = lax.broadcasted_iota(jnp.int32, (rows, rows), 1)
    col_doc = doc_of(base + lax.broadcasted_iota(jnp.int32, (1, rows), 1))
    same = jnp.concatenate([doc, doc], axis=1) == col_doc
    strict = (row > col) & same
    inclusive = (row >= col) & same
    apart = row ^ col
    running = ((row >= col) & (apart < SPAN)).astype(F32).astype(BF16)
    small_row = lax.broadcasted_iota(jnp.int32, (SPAN, rows), 0)
    small_col = lax.broadcasted_iota(jnp.int32, (SPAN, rows), 1)
    small_apart = small_row ^ (small_col & (SPAN - 1))
    small_block = small_col // SPAN
    small_eye = (small_apart == 0).astype(F32)

    every = range(heads)
    nothing = jnp.zeros((1, channels), F32)

    def of_head(v, h):
        return v[:, h * channels : (h + 1) * channels]

    def block(v, b):
        return v[b * SPAN : (b + 1) * SPAN]

    def activated(j, first, size):
        lanes = slice(j * columns, (j + 1) * columns)
        out = None
        for tap in range(CONV):
            shift = CONV - 1 - tap
            part = conv_ref[j, tap : tap + 1, :] * ext_ref[pl.ds(RIM - shift + first, size), lanes]
            if shift:
                part = part * jnp.concatenate([valid[shift][first : first + size]] * heads, axis=1)
            out = part if out is None else out + part
        return out / (1.0 + jnp.exp(-out))

    def unit(v):
        return v * lax.rsqrt(jnp.sum(v * v, axis=-1, keepdims=True) + 1e-06)

    def activations(first, size):
        query, key, value = [activated(j, first, size) for j in range(3)]
        return (
            [unit(of_head(query, h)) * channels ** (-0.5) for h in every],
            [unit(of_head(key, h)) for h in every],
            [of_head(value, h) for h in every],
        )

    drive = mm(low_rank, up_ref[...]) + bias_ref[...]
    soft = jnp.maximum(drive, 0.0) + jnp.log1p(jnp.exp(-jnp.abs(drive)))
    rates = jnp.concatenate([jnp.exp(jnp.full((1, channels), rate_ref[h], F32)) for h in every], axis=1)
    decay = -rates * soft
    d_high, d_mid = split(decay)
    d_low = (decay - d_high.astype(F32) - d_mid.astype(F32)).astype(BF16)
    cum_all = mm(running, d_high) + (mm(running, d_mid) + mm(running, d_low))
    betas = 1.0 / (1.0 + jnp.exp(-beta_logit))
    cums = [of_head(cum_all, h) for h in every]
    strengths = [jnp.broadcast_to(betas[:, h : h + 1], (rows, channels)) for h in every]
    lasts = [[cums[h][(b + 1) * SPAN - 1 : (b + 1) * SPAN] for b in range(blocks)] for h in every]
    grows = [jnp.exp(c) for c in cums]
    shrinks = [jnp.exp(-c) for c in cums]
    fades = [
        jnp.concatenate([jnp.exp(lasts[h][b] - block(cums[h], b)) for b in range(blocks)], axis=0)
        for h in every
    ]
    later_rows = activations(SPAN, rows - SPAN)
    rim.wait_recv()
    first_rows = activations(0, SPAN)
    queries, keys, values = [
        [jnp.concatenate([a, b], axis=0) for a, b in zip(f, l)] for f, l in zip(first_rows, later_rows)
    ]
    values = [strengths[h] * values[h] for h in every]

    lower, score, solved = [], [], []
    bk_ups, q_ups, tails = [], [], []
    for h in every:
        bk_ups.append(strengths[h] * keys[h] * grows[h])
        q_ups.append(queries[h] * grows[h])
        key_down = keys[h] * shrinks[h]
        tail = keys[h] * fades[h]
        tails.append([block(tail, b) for b in range(blocks)])
        mixes, reads = [], []
        for i in range(blocks):
            cols = []
            for b in range(blocks):
                if b < i - 1:
                    cols.append(tails[h][b] * jnp.exp(sum(lasts[h][b + 1 : i], nothing)))
                elif b == i - 1:
                    cols.append(tails[h][b])
                elif b == i:
                    cols.append(block(key_down, b))
                else:
                    cols.append(jnp.zeros((SPAN, channels), F32))
            left = split(jnp.concatenate([block(bk_ups[h], i), block(q_ups[h], i)], axis=0))
            product = mm3_narrow(left, split(jnp.concatenate(cols, axis=0)), NT)
            mixes.append(jnp.where(block(strict, i), product[:SPAN], 0.0))
            reads.append(jnp.where(block(inclusive, i), product[SPAN:], 0.0))
        lower.append(mixes)
        score.append(reads)

    def spread(v):
        return jnp.concatenate(
            [jnp.where(small_block == b, v, 0.0) for b in range(blocks)], axis=0
        )

    def times(lefts, rights):
        return [mm3(split(a), split(spread(b))) for a, b in zip(lefts, rights)]

    diagonal = []
    for h in every:
        picked = jnp.zeros((SPAN, rows), F32)
        for b in range(blocks):
            picked = jnp.where(small_block == b, lower[h][b], picked)
        diagonal.append(picked)
    power = [jnp.where(small_apart < 8, d, 0.0) for d in diagonal]
    inverse = [small_eye - p for p in power]
    power = times(power, power)
    inverse = [i + t for i, t in zip(inverse, times(inverse, power))]
    power = times(power, power)
    inverse = [i + t for i, t in zip(inverse, times(inverse, power))]
    size = 8
    while size < SPAN:
        off = [jnp.where((small_apart >= size) & (small_apart < 2 * size), d, 0.0) for d in diagonal]
        inverse = [i - t for i, t in zip(inverse, times(inverse, times(off, inverse)))]
        size *= 2

    full_keys, full_queries, ends_k, keeps = [], [], [], []
    for h in every:
        prefix = nothing
        k_rows, q_rows, t_rows = [], [], []
        for b in range(blocks):
            scale = jnp.exp(prefix)
            k_rows.append(block(bk_ups[h], b) * scale)
            q_rows.append(block(q_ups[h], b) * scale)
            prefix = prefix + lasts[h][b]
            t_rows.append(tails[h][b] * jnp.exp(sum(lasts[h][b + 1 :], nothing)))
        full_keys.append(jnp.concatenate(k_rows, axis=0) * first_doc)
        full_queries.append(jnp.concatenate(q_rows, axis=0) * first_doc)
        ends_k.append(split(jnp.concatenate(t_rows, axis=0) * last_doc))
        keeps.append(carry * jnp.exp(prefix))
    rights = [jnp.concatenate([full_keys[h], values[h]], axis=1) for h in every]
    done = [[] for _ in every]
    for i in range(blocks):
        rest = []
        for h in every:
            part = block(rights[h], i)
            if i:
                seen = tuple(jnp.concatenate([d[k] for d in done[h]], axis=0) for k in range(2))
                part = part - mm3(split(lower[h][i][:, : i * SPAN]), seen)
            rest.append(split(part))
        for h in every:
            own = split(inverse[h][:, i * SPAN : (i + 1) * SPAN])
            done[h].append(split(mm3(own, rest[h])))
    solved = [tuple(jnp.concatenate([d[k] for d in done[h]], axis=0) for k in range(2)) for h in every]

    eye_channels = (
        lax.broadcasted_iota(jnp.int32, (channels, channels), 0)
        == lax.broadcasted_iota(jnp.int32, (channels, channels), 1)
    ).astype(F32)
    keep_at, late_at = half + channels, half + channels + KEEP
    message = late_at

    def keep_rows(keep):
        high, middle = split(keep)
        low = (keep - high.astype(F32) - middle.astype(F32)).astype(BF16)
        return jnp.concatenate([high, middle, low, jnp.zeros((KEEP - 3, channels), BF16)], axis=0)

    def keep_of(rows3):
        wide = rows3.astype(F32)
        return wide[0:1] + (wide[1:2] + wide[2:3])

    for h in every:
        summary = mm3(solved[h], ends_k[h], TN).astype(BF16)
        stack[h, :half, :] = summary[channels : channels + half]
        stack[h, half:keep_at, :] = -summary[:channels]
        stack[h, keep_at:late_at, :] = keep_rows(keeps[h])
        stack[h, late_at:, :] = summary[channels + half :]

    mates = [(1, 2), (1, 1), (1, 3), (0, 2), (1, 0), (0, 1), (0, 3)]
    mates = [lax.rem(side + ds, 2) * X_SIZE + lax.rem(x + dx, X_SIZE) for ds, dx in mates]

    def map_copy(k, to):
        start = pl.multiple_of((to // X_SIZE) * half, half)
        return pltpu.make_async_remote_copy(
            src_ref=stack.at[lax.rem(to, X_SIZE), pl.ds(start, message), :],
            dst_ref=maps.at[member],
            send_sem=xs_sem.at[k], recv_sem=xr_sem.at[member],
            device_id=mate(to), device_id_type=MESH,
        )

    sends = [map_copy(k, to) for k, to in enumerate(mates)]
    for copy in sends:
        copy.start()
    maps[member] = stack[x, pl.ds(pl.multiple_of(side * half, half), message), :]

    for h in every:
        combined = mm3(split(jnp.concatenate(score[h], axis=0)), solved[h])
        lift[h] = full_queries[h] - combined[:, :channels]
        local[h] = combined[:, channels:]

    for frm in mates:
        pltpu.make_async_remote_copy(
            src_ref=maps.at[frm], dst_ref=maps.at[frm],
            send_sem=xs_sem.at[0], recv_sem=xr_sem.at[frm],
            device_id=mate(frm), device_id_type=MESH,
        ).wait_recv()

    map_at = pl.ds(pl.multiple_of((1 - side) * half, half), channels)
    keeps_at = pl.ds(pl.multiple_of(channels + (1 - side) * half, 16), KEEP)
    feed_at = pl.ds(pl.multiple_of(side * (channels + KEEP), 16), half)

    def apply(v, keep, exact_map):
        parts = jnp.concatenate(split(v), axis=1)
        return v * keep + mm(parts, jnp.concatenate([exact_map, exact_map], axis=0))

    def follow(whole, j):
        moved = apply(whole, step_keeps[j], maps[j, map_at, :])
        return jnp.concatenate([moved[:channels], moved[channels:] + maps[j, feed_at, :].astype(F32)], axis=0)

    def single(j):
        return jnp.concatenate(
            [step_keeps[j] * eye_channels + maps[j, map_at, :].astype(F32), maps[j, feed_at, :].astype(F32)], axis=0
        )

    def join(first, second):
        moved = mm3_narrow(split(first), split(second[:channels]))
        return jnp.concatenate([moved[:channels], moved[channels:] + second[channels:]], axis=0)

    step_keeps = [keep_of(maps[j, keeps_at, :]) for j in range(GROUP)]
    prefixes = [single(0)]
    late = [single(X_SIZE)]
    for j in range(1, X_SIZE):
        prefixes.append(follow(prefixes[-1], j))
        late.append(follow(late[-1], X_SIZE + j))
    group_total = join(prefixes[-1], late[-1])
    group_keep = functools.reduce(lambda a, b: a * b, step_keeps)
    total[:channels, :] = (group_total[:channels] - group_keep * eye_channels).astype(BF16)
    total[channels : channels + KEEP, :] = keep_rows(group_keep)
    total[channels + KEEP :, :] = group_total[channels:].astype(BF16)
    whole_span, feed_span = pl.ds(0, message), pl.ds(channels + KEEP, half)

    def total_copy(k, only_feed):
        span = feed_span if only_feed else whole_span
        return pltpu.make_async_remote_copy(
            src_ref=total.at[span, :], dst_ref=others.at[group, span, :],
            send_sem=zs_sem.at[k], recv_sem=zr_sem.at[group],
            device_id=at(lax.rem(me + k * GROUP, n_ctx)), device_id_type=MESH,
        )

    def for_later_groups(act):
        for k in sorted(range(1, n_groups), key=lambda k: -min(k, n_groups - k)):
            @pl.when((group > 0) & (group + k < n_groups))
            def _():
                act(total_copy(k, False))

        @pl.when(group == 0)
        def _():
            for k in range(1, n_groups):
                act(total_copy(k, True))

    for_later_groups(lambda copy: copy.start())
    for j in range(X_SIZE - 1):
        prefixes.append(join(prefixes[X_SIZE - 1], late[j]))
    into = split(jnp.concatenate([p[:channels] for p in prefixes], axis=1))

    state[...] = jnp.zeros_like(state)
    for frm in range(n_groups - 1):
        @pl.when(group > frm)
        def _():
            span = whole_span if frm else feed_span
            pltpu.make_async_remote_copy(
                src_ref=total.at[span, :], dst_ref=others.at[frm, span, :],
                send_sem=zs_sem.at[0], recv_sem=zr_sem.at[frm],
                device_id=at(lax.rem(me + GROUP, n_ctx)), device_id_type=MESH,
            ).wait_recv()
            feed = others[frm, feed_span, :].astype(F32)
            if frm:
                keep = keep_of(others[frm, pl.ds(channels, KEEP), :])
                feed = feed + apply(state[...], keep, others[frm, pl.ds(0, channels), :])
            state[...] = feed

    start_state = state[...]
    moved = mm3_narrow(split(start_state), into)
    entry_out[0] = start_state.astype(BF16)
    for j in range(1, GROUP):
        there_state = moved[:, (j - 1) * channels : j * channels] + prefixes[j - 1][channels:]
        entry_out[j] = there_state.astype(BF16)

    def entry_copy(k, to):
        return pltpu.make_async_remote_copy(
            src_ref=entry_out.at[to], dst_ref=entry.at[member],
            send_sem=bs_sem.at[k], recv_sem=br_sem.at[member],
            device_id=mate(to), device_id_type=MESH,
        )

    returns = [entry_copy(k, to) for k, to in enumerate(mates)]
    for copy in returns:
        copy.start()
    entry[member] = entry_out[member]
    for frm in mates:
        pltpu.make_async_remote_copy(
            src_ref=entry_out.at[frm], dst_ref=entry.at[frm],
            send_sem=bs_sem.at[0], recv_sem=br_sem.at[frm],
            device_id=mate(frm), device_id_type=MESH,
        ).wait_recv()

    for h in every:
        incoming = jnp.concatenate([entry[h], entry[X_SIZE + h]], axis=0)
        parts = jnp.concatenate(split(lift[h]), axis=1)
        result = local[h] + mm(parts, jnp.concatenate([incoming, incoming], axis=1), NT)
        mean = jnp.mean(result * result, axis=-1, keepdims=True)
        scaled = result * lax.rsqrt(mean + 1e-05) * gain_ref[...]
        out_ref[:, h * channels : (h + 1) * channels] = scaled.astype(BF16)

    for to in peers:
        slot_copy(to, me).wait_send()
    for copy in passed + sends + returns:
        copy.wait_send()
    rim.wait_send()
    for_later_groups(lambda copy: copy.wait_send())


def on_device(
    hidden, qkv_weight, conv_weight, w_beta, gate_down, gate_up,
    a_log, dt_bias, norm_gain, prompt_lengths, send_slot, gather_src,
):
    rows, width = hidden.shape
    _, features, columns = qkv_weight.shape
    n_ctx, n_head = lax.axis_size("ctx"), lax.axis_size("head")
    n_y, n_groups = n_head // CORES, n_ctx // GROUP
    heads, channels = a_log.shape[0], norm_gain.shape[0]
    rank = gate_down.shape[1]
    half = channels // 2
    message = channels + KEEP + half
    slots = 2 * rows
    dma = pltpu.SemaphoreType.DMA
    call = pl.pallas_call(
        fused_kernel,
        out_shape=jax.ShapeDtypeStruct((rows, columns), BF16),
        in_specs=[SMEM, SMEM] + [HBM] * 10,
        out_specs=VMEM,
        scratch_shapes=[
            pltpu.VMEM((1, rows), jnp.int32),
            pltpu.VMEM((1, rows), jnp.int32),
            pltpu.VMEM((width, rows), BF16),
            pltpu.VMEM((3, features, columns), BF16),
            pltpu.VMEM((features, rank), BF16),
            pltpu.VMEM((heads, features), BF16),
            pltpu.VMEM((3, CONV, columns), F32),
            pltpu.VMEM((rank, columns), BF16),
            pltpu.VMEM((1, columns), F32),
            pltpu.VMEM((1, channels), F32),
            pltpu.VMEM((slots, width), BF16),
            pltpu.VMEM((slots, width), BF16),
            pltpu.VMEM((features, rows), BF16),
            pltpu.VMEM((n_y, 16, CORES * width), BF16),
            pltpu.VMEM((3, rows, columns), F32),
            pltpu.VMEM((rows, rank), F32),
            pltpu.VMEM((rows, 16), F32),
            pltpu.VMEM((RIM + rows, 3 * columns), F32),
            pltpu.VMEM((heads, 2 * channels + KEEP, channels), BF16),
            pltpu.VMEM((heads, rows, channels), F32),
            pltpu.VMEM((heads, rows, channels), F32),
            pltpu.VMEM((GROUP, message, channels), BF16),
            pltpu.VMEM((message, channels), BF16),
            pltpu.VMEM((n_groups, message, channels), BF16),
            pltpu.VMEM((half, channels), F32),
            pltpu.VMEM((GROUP, half, channels), BF16),
            pltpu.VMEM((GROUP, half, channels), BF16),
            dma((10,)), dma((n_ctx,)), dma((n_ctx,)), dma((13,)), dma((4 * n_y,)), dma((2,)),
            dma((GROUP,)), dma((GROUP,)), dma((n_groups,)), dma((n_groups,)), dma((GROUP,)), dma((GROUP,)),
        ],
        compiler_params=pltpu.CompilerParams(
            collective_id=0, has_side_effects=True, vmem_limit_bytes=48 * 1024 * 1024
        ),
        name="delta_prefill",
    )
    operands = (
        prompt_lengths, a_log, send_slot.reshape(1, rows), gather_src.reshape(1, rows), hidden.T,
        qkv_weight, gate_down, w_beta.T, conv_weight.transpose(1, 0, 2), gate_up,
        dt_bias.reshape(1, columns), norm_gain.reshape(1, channels),
    )
    return call(*[pltpu.with_memory_space_constraint(v, pltpu.HBM) for v in operands])


def solution(mesh):
    placed = (
        P("ctx", "head"),
        P(None, None, "head"),
        P(None, None, "head"),
        P(None, "head"),
        P(),
        P(None, "head"),
        P("head"),
        P("head"),
        P(),
        P(),
        P("ctx"),
        P("ctx"),
    )
    return jax.shard_map(
        on_device, mesh=mesh, in_specs=placed, out_specs=P("ctx", "head"), check_vma=False
    )
```

```python
import functools

import jax
import jax.numpy as jnp
from jax import lax
from jax.experimental import pallas as pl
from jax.experimental.pallas import tpu as pltpu
from jax.sharding import PartitionSpec as P

CONV = 4
SPAN = 64
RIM = 8
X_SIZE = 4
CORES = 2
GROUP = 8
KEEP = 16
LANES = 128
MESH = pl.DeviceIdType.MESH
F32 = jnp.float32
BF16 = jnp.bfloat16
VMEM = pl.BlockSpec(memory_space=pltpu.VMEM)
SMEM = pl.BlockSpec(memory_space=pltpu.SMEM)
HBM = pl.BlockSpec(memory_space=pltpu.HBM)

NN = (((1,), (0,)), ((), ()))
NT = (((1,), (1,)), ((), ()))
TN = (((0,), (0,)), ((), ()))


def mm(a, b, dims=NN):
    return lax.dot_general(a, b, dims, preferred_element_type=F32)


def split(v):
    high = v.astype(BF16)
    return high, (v - high.astype(F32)).astype(BF16)


def mm3(a, b, dims=NN):
    return mm(a[0], b[0], dims) + (mm(a[0], b[1], dims) + mm(a[1], b[0], dims))


def mm3_narrow(a, b, dims=NN):
    axis = dims[0][1][0]
    wide = mm(jnp.concatenate(a, axis=1), jnp.concatenate([b[0], b[0]], axis=axis), dims)
    return wide + mm(a[0], b[1], dims)


def fused_kernel(
    lengths_ref, rate_ref, slot_hbm, src_hbm, hidden_hbm, wqkv_hbm, wdown_hbm, wbeta_hbm,
    conv_hbm, up_hbm, bias_hbm, gain_hbm,
    out_ref,
    slot_buf, src_buf, hidden_buf, w_qkv, w_down, wbeta_buf, conv_ref, up_ref, bias_ref, gain_ref,
    send_a, send_b, send_c, landed_a, landed_b, landed_c, shards, w_beta, acc, acc_low, acc_beta, ext_ref,
    stack, local, lift, maps, total, others, state, entry_out, entry,
    in_sem, s_sem, r_sem, hs_sem, hr_sem, rim_sem,
    xs_sem, xr_sem, zs_sem, zr_sem, bs_sem, br_sem,
):
    n_ctx = lax.axis_size("ctx")
    n_z = n_ctx // X_SIZE
    n_head = lax.axis_size("head")
    n_y = n_head // CORES
    n_groups = n_ctx // GROUP
    me = lax.axis_index("ctx")
    head = lax.axis_index("head")
    z, own_x = me // X_SIZE, lax.rem(me, X_SIZE)
    y, core = head // CORES, lax.rem(head, CORES)
    sibling = y * CORES + (1 - core)
    member = lax.rem(me, GROUP)
    group = me // GROUP
    x, side = lax.rem(member, X_SIZE), member // X_SIZE
    width, rows = hidden_buf.shape
    slots = send_a.shape[0]
    cap = slots // n_ctx
    heads, _, channels = local.shape
    columns = heads * channels
    half = channels // 2
    blocks = rows // SPAN
    base = me * rows

    def at(ctx):
        return {"ctx": ctx, "head": head}

    def mate(index):
        return at(group * GROUP + index)

    operands = [
        (slot_hbm, slot_buf), (hidden_hbm, hidden_buf), (src_hbm, src_buf), (wbeta_hbm, wbeta_buf),
        (wqkv_hbm, w_qkv), (wdown_hbm, w_down),
        (up_hbm, up_ref), (bias_hbm, bias_ref), (conv_hbm, conv_ref), (gain_hbm, gain_ref),
    ]
    loads = [pltpu.make_async_copy(a, b, in_sem.at[i]) for i, (a, b) in enumerate(operands)]
    for copy in loads:
        copy.start()

    far = sorted(
        ((dz, dx) for dz in range(n_z) for dx in range(X_SIZE) if dz or dx),
        key=lambda d: -(min(d[0], n_z - d[0]) * 2 + min(d[1], X_SIZE - d[1])),
    )
    peers = [lax.rem(z + dz, n_z) * X_SIZE + lax.rem(own_x + dx, X_SIZE) for dz, dx in far]
    ring = {dy: lax.rem(y + dy, n_y) for dy in range(n_y)}

    barrier = pltpu.get_barrier_semaphore()
    for to in peers:
        pl.semaphore_signal(barrier, inc=1, device_id=at(to), device_id_type=MESH)
    here = [ring[dy] * CORES + core for dy in range(n_y)]
    there = [ring[dy] * CORES + (1 - core) for dy in range(n_y)]
    for to in here[1:] + [sibling]:
        pl.semaphore_signal(barrier, inc=1, device_id={"ctx": me, "head": to}, device_id_type=MESH)

    for copy in loads[:4]:
        copy.wait()
    slot_ids = lax.broadcasted_iota(jnp.int32, (slots, rows), 0)
    place = (slot_ids == slot_buf[...]).astype(F32).astype(BF16)
    spans, start = [], 0
    while start < width:
        spans.append((start, min(LANES, width - start)))
        start += LANES
    sent, landed = (send_a, send_b, send_c), (landed_a, landed_b, landed_c)
    for c, (start, size) in enumerate(spans):
        sent[c][...] = mm(place, hidden_buf[start : start + size, :], NT).astype(BF16)
    pick = (slot_ids == src_buf[...]).astype(F32).astype(BF16)
    w_beta[...] = jnp.zeros_like(w_beta)
    for c, (start, size) in enumerate(spans):
        for i in range(n_head):
            at_lane = i * width + start
            w_beta[c, : wbeta_buf.shape[0], i * size : (i + 1) * size] = wbeta_buf[:, at_lane : at_lane + size]

    pl.semaphore_wait(barrier, n_ctx - 1 + n_y)

    def slots_of(index):
        return pl.ds(pl.multiple_of(index * cap, cap), cap)

    def slot_copy(c, to, frm):
        return pltpu.make_async_remote_copy(
            src_ref=sent[c].at[slots_of(to), :], dst_ref=landed[c].at[slots_of(frm), :],
            send_sem=s_sem.at[c * n_ctx + to], recv_sem=r_sem.at[c * n_ctx + frm],
            device_id=at(to), device_id_type=MESH,
        )

    for c in range(len(spans)):
        for to in peers:
            slot_copy(c, to, me).start()
    for c in range(len(spans)):
        landed[c][slots_of(me), :] = sent[c][slots_of(me), :]

    passed = []

    def shard_copy(c, index, to, send, recv):
        start, size = spans[c]
        rows_at = pl.ds(pl.multiple_of(index * width + start, 16), size)
        return pltpu.make_async_remote_copy(
            src_ref=shards.at[rows_at, :], dst_ref=shards.at[rows_at, :],
            send_sem=hs_sem.at[send], recv_sem=hr_sem.at[recv],
            device_id={"ctx": me, "head": to}, device_id_type=MESH,
        )

    def push(c, index, to, recv):
        copy = shard_copy(c, index, to, len(passed), recv)
        copy.start()
        passed.append(copy)

    def mine(c, dy):
        return c * 2 * n_y + dy

    def other(c, dy):
        return c * 2 * n_y + n_y + dy

    def collect(c):
        start, size = spans[c]
        for frm in reversed(peers):
            slot_copy(c, frm, frm).wait_recv()
        own_at = pl.ds(pl.multiple_of(head * width + start, 16), size)
        shards[own_at, :] = mm(landed[c][...], pick, TN).astype(BF16)
        for dy in (2, 1, 3):
            push(c, head, here[dy], mine(c, n_y - dy))
        push(c, head, sibling, other(c, 0))

    def hand_over(c, dy):
        shard_copy(c, here[dy], sibling, 0, mine(c, dy)).wait_recv()
        push(c, here[dy], sibling, other(c, dy))

    def products(c):
        start, size = spans[c]
        for dy in range(n_y):
            shard_copy(c, there[dy], sibling, 0, other(c, dy)).wait_recv()
        at_rows = [slice(i * width + start, i * width + start + size) for i in range(n_head)]
        part = jnp.concatenate([shards[r, :] for r in at_rows], axis=0).T

        def chunk(ref):
            return jnp.concatenate([ref[r, :] for r in at_rows], axis=0)

        return [mm(part, chunk(w_qkv.at[j])) for j in range(3)] + [
            mm(part, chunk(w_down)), mm(part, w_beta[c, :, : n_head * size], NT)
        ]

    collect(0)
    collect(1)
    hand_over(0, 1)
    hand_over(0, 3)
    collect(2)
    hand_over(0, 2)
    for c in (1, 2):
        hand_over(c, 1)
        hand_over(c, 3)
    for copy in loads[4:6]:
        copy.wait()
    sums = [acc.at[0], acc.at[1], acc.at[2], acc_low, acc_beta]
    for ref, value in zip(sums, products(0)):
        ref[...] = value
    hand_over(1, 2)
    hand_over(2, 2)
    for ref, value in zip(sums, products(1)):
        ref[...] = ref[...] + value
    last = [ref[...] + value for ref, value in zip(sums, products(2))]
    for j in range(3):
        ext_ref[RIM:, j * columns : (j + 1) * columns] = last[j].astype(BF16).astype(F32)
    low_rank, beta_logit = last[3].astype(BF16), last[4]
    rim = pltpu.make_async_remote_copy(
        src_ref=ext_ref.at[pl.ds(rows, RIM), :], dst_ref=ext_ref.at[pl.ds(0, RIM), :],
        send_sem=rim_sem.at[0], recv_sem=rim_sem.at[1],
        device_id=at(lax.rem(me + 1, n_ctx)), device_id_type=MESH,
    )
    rim.start()
    for copy in loads[6:]:
        copy.wait()

    ends, total_len = [], 0
    for i in range(lengths_ref.shape[0]):
        total_len = total_len + lengths_ref[i]
        ends.append(total_len)

    def doc_of(positions):
        ended = sum((positions >= end).astype(jnp.int32) for end in ends)
        return jnp.where(positions < 0, -1, ended)

    pos = base + lax.broadcasted_iota(jnp.int32, (rows, channels), 0)
    doc = doc_of(pos)
    valid = [None] + [(doc_of(pos - shift) == doc).astype(F32) for shift in range(1, CONV)]
    before = doc_of(jnp.zeros((1, channels), jnp.int32) + (base - 1))
    final = doc_of(jnp.zeros((1, channels), jnp.int32) + (base + rows - 1))
    first_doc = (doc == before).astype(F32)
    last_doc = (doc == final).astype(F32)
    carry = (final == before).astype(F32)
    row = lax.broadcasted_iota(jnp.int32, (rows, rows), 0)
    col = lax.broadcasted_iota(jnp.int32, (rows, rows), 1)
    col_doc = doc_of(base + lax.broadcasted_iota(jnp.int32, (1, rows), 1))
    same = jnp.concatenate([doc, doc], axis=1) == col_doc
    strict = (row > col) & same
    inclusive = (row >= col) & same
    apart = row ^ col
    running = ((row >= col) & (apart < SPAN)).astype(F32).astype(BF16)
    small_row = lax.broadcasted_iota(jnp.int32, (SPAN, rows), 0)
    small_col = lax.broadcasted_iota(jnp.int32, (SPAN, rows), 1)
    small_apart = small_row ^ (small_col & (SPAN - 1))
    small_block = small_col // SPAN
    small_eye = (small_apart == 0).astype(F32)

    every = range(heads)
    nothing = jnp.zeros((1, channels), F32)

    def of_head(v, h):
        return v[:, h * channels : (h + 1) * channels]

    def block(v, b):
        return v[b * SPAN : (b + 1) * SPAN]

    def activated(j, first, size):
        lanes = slice(j * columns, (j + 1) * columns)
        out = None
        for tap in range(CONV):
            shift = CONV - 1 - tap
            part = conv_ref[j, tap : tap + 1, :] * ext_ref[pl.ds(RIM - shift + first, size), lanes]
            if shift:
                part = part * jnp.concatenate([valid[shift][first : first + size]] * heads, axis=1)
            out = part if out is None else out + part
        grown = 1.0 + jnp.exp(jnp.minimum(-out, 80.0))
        inverted = pl.reciprocal(grown, approx=True)
        return out * (inverted * (2.0 - grown * inverted))

    def unit(v):
        return v * lax.rsqrt(jnp.sum(v * v, axis=-1, keepdims=True) + 1e-06)

    def activations(first, size):
        query, key, value = [activated(j, first, size) for j in range(3)]
        return (
            [unit(of_head(query, h)) * channels ** (-0.5) for h in every],
            [unit(of_head(key, h)) for h in every],
            [of_head(value, h) for h in every],
        )

    drive = mm(low_rank, up_ref[...]) + bias_ref[...]
    soft = jnp.maximum(drive, 0.0) + jnp.log(1.0 + jnp.exp(-jnp.abs(drive)))
    rates = jnp.concatenate([jnp.exp(jnp.full((1, channels), rate_ref[h], F32)) for h in every], axis=1)
    decay = -rates * soft
    d_high, d_mid = split(decay)
    d_low = (decay - d_high.astype(F32) - d_mid.astype(F32)).astype(BF16)
    cum_all = mm(running, d_high) + (mm(running, d_mid) + mm(running, d_low))
    betas = 1.0 / (1.0 + jnp.exp(-beta_logit))
    cums = [of_head(cum_all, h) for h in every]
    strengths = [jnp.broadcast_to(betas[:, h : h + 1], (rows, channels)) for h in every]
    lasts = [[cums[h][(b + 1) * SPAN - 1 : (b + 1) * SPAN] for b in range(blocks)] for h in every]
    grows = [jnp.exp(c) for c in cums]
    shrinks = [jnp.exp(-c) for c in cums]
    fades = [
        jnp.concatenate([jnp.exp(lasts[h][b] - block(cums[h], b)) for b in range(blocks)], axis=0)
        for h in every
    ]
    later_rows = activations(SPAN, rows - SPAN)
    rim.wait_recv()
    first_rows = activations(0, SPAN)
    queries, keys, values = [
        [jnp.concatenate([a, b], axis=0) for a, b in zip(f, l)] for f, l in zip(first_rows, later_rows)
    ]
    values = [strengths[h] * values[h] for h in every]

    lower, score, solved = [], [], []
    bk_ups, q_ups, tails = [], [], []
    for h in every:
        bk_ups.append(strengths[h] * keys[h] * grows[h])
        q_ups.append(queries[h] * grows[h])
        key_down = keys[h] * shrinks[h]
        tail = keys[h] * fades[h]
        tails.append([block(tail, b) for b in range(blocks)])
        mixes, reads = [], []
        for i in range(blocks):
            cols = []
            for b in range(blocks):
                if b < i - 1:
                    cols.append(tails[h][b] * jnp.exp(sum(lasts[h][b + 1 : i], nothing)))
                elif b == i - 1:
                    cols.append(tails[h][b])
                elif b == i:
                    cols.append(block(key_down, b))
                else:
                    cols.append(jnp.zeros((SPAN, channels), F32))
            left = split(jnp.concatenate([block(bk_ups[h], i), block(q_ups[h], i)], axis=0))
            product = mm3_narrow(left, split(jnp.concatenate(cols, axis=0)), NT)
            mixes.append(jnp.where(block(strict, i), product[:SPAN], 0.0))
            reads.append(jnp.where(block(inclusive, i), product[SPAN:], 0.0))
        lower.append(mixes)
        score.append(reads)

    def spread(v):
        return jnp.concatenate(
            [jnp.where(small_block == b, v, 0.0) for b in range(blocks)], axis=0
        )

    def times(lefts, rights):
        return [mm3(split(a), split(spread(b))) for a, b in zip(lefts, rights)]

    diagonal = []
    for h in every:
        picked = jnp.zeros((SPAN, rows), F32)
        for b in range(blocks):
            picked = jnp.where(small_block == b, lower[h][b], picked)
        diagonal.append(picked)
    power = [jnp.where(small_apart < 8, d, 0.0) for d in diagonal]
    inverse = [small_eye - p for p in power]
    power = times(power, power)
    inverse = [i + t for i, t in zip(inverse, times(inverse, power))]
    power = times(power, power)
    inverse = [i + t for i, t in zip(inverse, times(inverse, power))]
    size = 8
    while size < SPAN:
        off = [jnp.where((small_apart >= size) & (small_apart < 2 * size), d, 0.0) for d in diagonal]
        inverse = [i - t for i, t in zip(inverse, times(inverse, times(off, inverse)))]
        size *= 2

    full_keys, full_queries, ends_k, keeps = [], [], [], []
    for h in every:
        prefix = nothing
        k_rows, q_rows, t_rows = [], [], []
        for b in range(blocks):
            scale = jnp.exp(prefix)
            k_rows.append(block(bk_ups[h], b) * scale)
            q_rows.append(block(q_ups[h], b) * scale)
            prefix = prefix + lasts[h][b]
            t_rows.append(tails[h][b] * jnp.exp(sum(lasts[h][b + 1 :], nothing)))
        full_keys.append(jnp.concatenate(k_rows, axis=0) * first_doc)
        full_queries.append(jnp.concatenate(q_rows, axis=0) * first_doc)
        ends_k.append(split(jnp.concatenate(t_rows, axis=0) * last_doc))
        keeps.append(carry * jnp.exp(prefix))
    rights = [jnp.concatenate([full_keys[h], values[h]], axis=1) for h in every]
    done = [[] for _ in every]
    for i in range(blocks):
        rest = []
        for h in every:
            part = block(rights[h], i)
            if i:
                seen = tuple(jnp.concatenate([d[k] for d in done[h]], axis=0) for k in range(2))
                part = part - mm3(split(lower[h][i][:, : i * SPAN]), seen)
            rest.append(split(part))
        for h in every:
            own = split(inverse[h][:, i * SPAN : (i + 1) * SPAN])
            done[h].append(split(mm3(own, rest[h])))
    solved = [tuple(jnp.concatenate([d[k] for d in done[h]], axis=0) for k in range(2)) for h in every]

    eye_channels = (
        lax.broadcasted_iota(jnp.int32, (channels, channels), 0)
        == lax.broadcasted_iota(jnp.int32, (channels, channels), 1)
    ).astype(F32)
    keep_at, late_at = half + channels, half + channels + KEEP
    message = late_at

    def keep_rows(keep):
        high, middle = split(keep)
        low = (keep - high.astype(F32) - middle.astype(F32)).astype(BF16)
        return jnp.concatenate([high, middle, low, jnp.zeros((KEEP - 3, channels), BF16)], axis=0)

    def keep_of(rows3):
        wide = rows3.astype(F32)
        return wide[0:1] + (wide[1:2] + wide[2:3])

    for h in every:
        summary = mm3(solved[h], ends_k[h], TN).astype(BF16)
        stack[h, :half, :] = summary[channels : channels + half]
        stack[h, half:keep_at, :] = -summary[:channels]
        stack[h, keep_at:late_at, :] = keep_rows(keeps[h])
        stack[h, late_at:, :] = summary[channels + half :]

    mates = [(1, 2), (1, 1), (1, 3), (0, 2), (1, 0), (0, 1), (0, 3)]
    mates = [lax.rem(side + ds, 2) * X_SIZE + lax.rem(x + dx, X_SIZE) for ds, dx in mates]

    def map_copy(k, to):
        start = pl.multiple_of((to // X_SIZE) * half, half)
        return pltpu.make_async_remote_copy(
            src_ref=stack.at[lax.rem(to, X_SIZE), pl.ds(start, message), :],
            dst_ref=maps.at[member],
            send_sem=xs_sem.at[k], recv_sem=xr_sem.at[member],
            device_id=mate(to), device_id_type=MESH,
        )

    sends = [map_copy(k, to) for k, to in enumerate(mates)]
    for copy in sends:
        copy.start()
    maps[member] = stack[x, pl.ds(pl.multiple_of(side * half, half), message), :]

    for h in every:
        combined = mm3(split(jnp.concatenate(score[h], axis=0)), solved[h])
        lift[h] = full_queries[h] - combined[:, :channels]
        local[h] = combined[:, channels:]

    for frm in mates:
        pltpu.make_async_remote_copy(
            src_ref=maps.at[frm], dst_ref=maps.at[frm],
            send_sem=xs_sem.at[0], recv_sem=xr_sem.at[frm],
            device_id=mate(frm), device_id_type=MESH,
        ).wait_recv()

    map_at = pl.ds(pl.multiple_of((1 - side) * half, half), channels)
    keeps_at = pl.ds(pl.multiple_of(channels + (1 - side) * half, 16), KEEP)
    feed_at = pl.ds(pl.multiple_of(side * (channels + KEEP), 16), half)

    def apply(v, keep, exact_map):
        parts = jnp.concatenate(split(v), axis=1)
        return v * keep + mm(parts, jnp.concatenate([exact_map, exact_map], axis=0))

    def follow(whole, j):
        moved = apply(whole, step_keeps[j], maps[j, map_at, :])
        return jnp.concatenate([moved[:channels], moved[channels:] + maps[j, feed_at, :].astype(F32)], axis=0)

    def single(j):
        return jnp.concatenate(
            [step_keeps[j] * eye_channels + maps[j, map_at, :].astype(F32), maps[j, feed_at, :].astype(F32)], axis=0
        )

    def join(first, second):
        moved = mm3_narrow(split(first), split(second[:channels]))
        return jnp.concatenate([moved[:channels], moved[channels:] + second[channels:]], axis=0)

    step_keeps = [keep_of(maps[j, keeps_at, :]) for j in range(GROUP)]
    prefixes = [single(0)]
    late = [single(X_SIZE)]
    for j in range(1, X_SIZE):
        prefixes.append(follow(prefixes[-1], j))
        late.append(follow(late[-1], X_SIZE + j))
    group_total = join(prefixes[-1], late[-1])
    group_keep = functools.reduce(lambda a, b: a * b, step_keeps)
    total[:channels, :] = (group_total[:channels] - group_keep * eye_channels).astype(BF16)
    total[channels : channels + KEEP, :] = keep_rows(group_keep)
    total[channels + KEEP :, :] = group_total[channels:].astype(BF16)
    whole_span, feed_span = pl.ds(0, message), pl.ds(channels + KEEP, half)

    def total_copy(k, only_feed):
        span = feed_span if only_feed else whole_span
        return pltpu.make_async_remote_copy(
            src_ref=total.at[span, :], dst_ref=others.at[group, span, :],
            send_sem=zs_sem.at[k], recv_sem=zr_sem.at[group],
            device_id=at(lax.rem(me + k * GROUP, n_ctx)), device_id_type=MESH,
        )

    def for_later_groups(act):
        for k in sorted(range(1, n_groups), key=lambda k: -min(k, n_groups - k)):
            @pl.when((group > 0) & (group + k < n_groups))
            def _():
                act(total_copy(k, False))

        @pl.when(group == 0)
        def _():
            for k in range(1, n_groups):
                act(total_copy(k, True))

    for_later_groups(lambda copy: copy.start())
    for j in range(X_SIZE - 1):
        prefixes.append(join(prefixes[X_SIZE - 1], late[j]))
    into = split(jnp.concatenate([p[:channels] for p in prefixes], axis=1))

    state[...] = jnp.zeros_like(state)
    for frm in range(n_groups - 1):
        @pl.when(group > frm)
        def _():
            span = whole_span if frm else feed_span
            pltpu.make_async_remote_copy(
                src_ref=total.at[span, :], dst_ref=others.at[frm, span, :],
                send_sem=zs_sem.at[0], recv_sem=zr_sem.at[frm],
                device_id=at(lax.rem(me + GROUP, n_ctx)), device_id_type=MESH,
            ).wait_recv()
            feed = others[frm, feed_span, :].astype(F32)
            if frm:
                keep = keep_of(others[frm, pl.ds(channels, KEEP), :])
                feed = feed + apply(state[...], keep, others[frm, pl.ds(0, channels), :])
            state[...] = feed

    start_state = state[...]
    moved = mm3_narrow(split(start_state), into)
    entry_out[0] = start_state.astype(BF16)
    for j in range(1, GROUP):
        there_state = moved[:, (j - 1) * channels : j * channels] + prefixes[j - 1][channels:]
        entry_out[j] = there_state.astype(BF16)

    def entry_copy(k, to):
        return pltpu.make_async_remote_copy(
            src_ref=entry_out.at[to], dst_ref=entry.at[member],
            send_sem=bs_sem.at[k], recv_sem=br_sem.at[member],
            device_id=mate(to), device_id_type=MESH,
        )

    returns = [entry_copy(k, to) for k, to in enumerate(mates)]
    for copy in returns:
        copy.start()
    entry[member] = entry_out[member]
    for frm in mates:
        pltpu.make_async_remote_copy(
            src_ref=entry_out.at[frm], dst_ref=entry.at[frm],
            send_sem=bs_sem.at[0], recv_sem=br_sem.at[frm],
            device_id=mate(frm), device_id_type=MESH,
        ).wait_recv()

    for h in every:
        incoming = jnp.concatenate([entry[h], entry[X_SIZE + h]], axis=0)
        parts = jnp.concatenate(split(lift[h]), axis=1)
        result = local[h] + mm(parts, jnp.concatenate([incoming, incoming], axis=1), NT)
        mean = jnp.mean(result * result, axis=-1, keepdims=True)
        scaled = result * lax.rsqrt(mean + 1e-05) * gain_ref[...]
        out_ref[:, h * channels : (h + 1) * channels] = scaled.astype(BF16)

    for c in range(len(spans)):
        for to in peers:
            slot_copy(c, to, me).wait_send()
    for copy in passed + sends + returns:
        copy.wait_send()
    rim.wait_send()
    for_later_groups(lambda copy: copy.wait_send())


def on_device(
    hidden, qkv_weight, conv_weight, w_beta, gate_down, gate_up,
    a_log, dt_bias, norm_gain, prompt_lengths, send_slot, gather_src,
):
    rows, width = hidden.shape
    _, features, columns = qkv_weight.shape
    n_ctx, n_head = lax.axis_size("ctx"), lax.axis_size("head")
    n_y, n_groups = n_head // CORES, n_ctx // GROUP
    heads, channels = a_log.shape[0], norm_gain.shape[0]
    rank = gate_down.shape[1]
    half = channels // 2
    message = channels + KEEP + half
    slots = 2 * rows
    pieces = [pltpu.VMEM((slots, min(LANES, width - start)), BF16) for start in range(0, width, LANES)]
    dma = pltpu.SemaphoreType.DMA
    call = pl.pallas_call(
        fused_kernel,
        out_shape=jax.ShapeDtypeStruct((rows, columns), BF16),
        in_specs=[SMEM, SMEM] + [HBM] * 10,
        out_specs=VMEM,
        scratch_shapes=[
            pltpu.VMEM((1, rows), jnp.int32),
            pltpu.VMEM((1, rows), jnp.int32),
            pltpu.VMEM((width, rows), BF16),
            pltpu.VMEM((3, features, columns), BF16),
            pltpu.VMEM((features, rank), BF16),
            pltpu.VMEM((heads, features), BF16),
            pltpu.VMEM((3, CONV, columns), F32),
            pltpu.VMEM((rank, columns), BF16),
            pltpu.VMEM((1, columns), F32),
            pltpu.VMEM((1, channels), F32),
            *pieces,
            *pieces,
            pltpu.VMEM((features, rows), BF16),
            pltpu.VMEM((len(pieces), 16, n_head * LANES), BF16),
            pltpu.VMEM((3, rows, columns), F32),
            pltpu.VMEM((rows, rank), F32),
            pltpu.VMEM((rows, 16), F32),
            pltpu.VMEM((RIM + rows, 3 * columns), F32),
            pltpu.VMEM((heads, 2 * channels + KEEP, channels), BF16),
            pltpu.VMEM((heads, rows, channels), F32),
            pltpu.VMEM((heads, rows, channels), F32),
            pltpu.VMEM((GROUP, message, channels), BF16),
            pltpu.VMEM((message, channels), BF16),
            pltpu.VMEM((n_groups, message, channels), BF16),
            pltpu.VMEM((half, channels), F32),
            pltpu.VMEM((GROUP, half, channels), BF16),
            pltpu.VMEM((GROUP, half, channels), BF16),
            dma((10,)), dma((3 * n_ctx,)), dma((3 * n_ctx,)), dma((21,)), dma((6 * n_y,)), dma((2,)),
            dma((GROUP,)), dma((GROUP,)), dma((n_groups,)), dma((n_groups,)), dma((GROUP,)), dma((GROUP,)),
        ],
        compiler_params=pltpu.CompilerParams(
            collective_id=0, has_side_effects=True, vmem_limit_bytes=48 * 1024 * 1024
        ),
        name="delta_prefill",
    )
    operands = (
        prompt_lengths, a_log, send_slot.reshape(1, rows), gather_src.reshape(1, rows), hidden.T,
        qkv_weight, gate_down, w_beta.T, conv_weight.transpose(1, 0, 2), gate_up,
        dt_bias.reshape(1, columns), norm_gain.reshape(1, channels),
    )
    return call(*[pltpu.with_memory_space_constraint(v, pltpu.HBM) for v in operands])


def solution(mesh):
    placed = (
        P("ctx", "head"),
        P(None, None, "head"),
        P(None, None, "head"),
        P(None, "head"),
        P(),
        P(None, "head"),
        P("head"),
        P("head"),
        P(),
        P(),
        P("ctx"),
        P("ctx"),
    )
    return jax.shard_map(
        on_device, mesh=mesh, in_specs=placed, out_specs=P("ctx", "head"), check_vma=False
    )
```

```python
import functools

import jax
import jax.numpy as jnp
from jax import lax
from jax.experimental import pallas as pl
from jax.experimental.pallas import tpu as pltpu
from jax.sharding import PartitionSpec as P

CONV = 4
SPAN = 64
RIM = 8
X_SIZE = 4
CORES = 2
GROUP = 8
KEEP = 16
LANES = 128
MESH = pl.DeviceIdType.MESH
F32 = jnp.float32
BF16 = jnp.bfloat16
VMEM = pl.BlockSpec(memory_space=pltpu.VMEM)
SMEM = pl.BlockSpec(memory_space=pltpu.SMEM)
HBM = pl.BlockSpec(memory_space=pltpu.HBM)

NN = (((1,), (0,)), ((), ()))
NT = (((1,), (1,)), ((), ()))
TN = (((0,), (0,)), ((), ()))


def mm(a, b, dims=NN):
    return lax.dot_general(a, b, dims, preferred_element_type=F32)


def split(v):
    high = v.astype(BF16)
    return high, (v - high.astype(F32)).astype(BF16)


def mm3(a, b, dims=NN):
    axis = 1 - dims[0][0][0]
    count = a[0].shape[axis]
    both = mm(jnp.concatenate(a, axis=axis), b[0], dims)
    return both[:count] + (both[count:] + mm(a[0], b[1], dims))


def mm3_narrow(a, b, dims=NN):
    axis = dims[0][1][0]
    wide = mm(jnp.concatenate(a, axis=1), jnp.concatenate([b[0], b[0]], axis=axis), dims)
    return wide + mm(a[0], b[1], dims)


def fused_kernel(
    lengths_ref, rate_ref, slot_hbm, src_hbm, hidden_hbm, wqkv_hbm, wdown_hbm, wbeta_hbm,
    conv_hbm, up_hbm, bias_hbm, gain_hbm,
    out_ref,
    slot_buf, src_buf, hidden_buf, w_qkv, w_down, wbeta_buf, conv_ref, up_ref, bias_ref, gain_ref,
    send_a, send_b, send_c, landed_a, landed_b, landed_c, shards, acc, acc_low, ext_ref,
    stack, local, lift, maps, total, others, state, entry_out, entry,
    in_sem, s_sem, r_sem, hs_sem, hr_sem, rim_sem,
    xs_sem, xr_sem, zs_sem, zr_sem, bs_sem, br_sem,
):
    n_ctx = lax.axis_size("ctx")
    n_z = n_ctx // X_SIZE
    n_head = lax.axis_size("head")
    n_y = n_head // CORES
    n_groups = n_ctx // GROUP
    me = lax.axis_index("ctx")
    head = lax.axis_index("head")
    z, own_x = me // X_SIZE, lax.rem(me, X_SIZE)
    y, core = head // CORES, lax.rem(head, CORES)
    sibling = y * CORES + (1 - core)
    member = lax.rem(me, GROUP)
    group = me // GROUP
    x, side = lax.rem(member, X_SIZE), member // X_SIZE
    width, rows = hidden_buf.shape
    slots = send_a.shape[0]
    cap = slots // n_ctx
    heads, _, channels = local.shape
    columns = heads * channels
    half = channels // 2
    blocks = rows // SPAN
    base = me * rows

    def at(ctx):
        return {"ctx": ctx, "head": head}

    def mate(index):
        return at(group * GROUP + index)

    operands = [
        (slot_hbm, slot_buf), (hidden_hbm, hidden_buf), (src_hbm, src_buf), (wbeta_hbm, wbeta_buf),
        (wqkv_hbm, w_qkv), (wdown_hbm, w_down),
        (up_hbm, up_ref), (bias_hbm, bias_ref), (conv_hbm, conv_ref), (gain_hbm, gain_ref),
    ]
    loads = [pltpu.make_async_copy(a, b, in_sem.at[i]) for i, (a, b) in enumerate(operands)]
    for copy in loads[:4]:
        copy.start()

    far = sorted(
        ((dz, dx) for dz in range(n_z) for dx in range(X_SIZE) if dz or dx),
        key=lambda d: -(min(d[0], n_z - d[0]) * 2 + min(d[1], X_SIZE - d[1])),
    )
    peers = [lax.rem(z + dz, n_z) * X_SIZE + lax.rem(own_x + dx, X_SIZE) for dz, dx in far]
    ring = {dy: lax.rem(y + dy, n_y) for dy in range(n_y)}

    barrier = pltpu.get_barrier_semaphore()
    for to in peers:
        pl.semaphore_signal(barrier, inc=1, device_id=at(to), device_id_type=MESH)
    here = [ring[dy] * CORES + core for dy in range(n_y)]
    there = [ring[dy] * CORES + (1 - core) for dy in range(n_y)]
    for to in here[1:] + there:
        pl.semaphore_signal(barrier, inc=1, device_id={"ctx": me, "head": to}, device_id_type=MESH)

    for copy in loads[:4]:
        copy.wait()
    slot_ids = lax.broadcasted_iota(jnp.int32, (slots, rows), 0)
    place = (slot_ids == slot_buf[...]).astype(F32).astype(BF16)
    spans, start = [], 0
    while start < width:
        spans.append((start, min(LANES, width - start)))
        start += LANES
    sent, landed = (send_a, send_b, send_c), (landed_a, landed_b, landed_c)

    def fill(c):
        start, size = spans[c]
        sent[c][...] = mm(place, hidden_buf[start : start + size, :], NT).astype(BF16)

    fill(0)

    pl.semaphore_wait(barrier, n_ctx - 1 + n_head - 1)

    def slots_of(index):
        return pl.ds(pl.multiple_of(index * cap, cap), cap)

    def slot_copy(c, to, frm):
        return pltpu.make_async_remote_copy(
            src_ref=sent[c].at[slots_of(to), :], dst_ref=landed[c].at[slots_of(frm), :],
            send_sem=s_sem.at[c * n_ctx + to], recv_sem=r_sem.at[c * n_ctx + frm],
            device_id=at(to), device_id_type=MESH,
        )

    for c in range(len(spans)):
        if c:
            fill(c)
        for to in peers:
            slot_copy(c, to, me).start()
    for copy in loads[4:]:
        copy.start()
    pick = (slot_ids == src_buf[...]).astype(F32).astype(BF16)
    for c in range(len(spans)):
        landed[c][slots_of(me), :] = sent[c][slots_of(me), :]

    passed = []
    last_chunk = len(spans) - 1

    def shard_copy(c, index, to, send, recv):
        start, size = spans[c]
        rows_at = pl.ds(pl.multiple_of(index * width + start, 16), size)
        return pltpu.make_async_remote_copy(
            src_ref=shards.at[rows_at, :], dst_ref=shards.at[rows_at, :],
            send_sem=hs_sem.at[send], recv_sem=hr_sem.at[recv],
            device_id={"ctx": me, "head": to}, device_id_type=MESH,
        )

    def push(c, index, to, recv):
        copy = shard_copy(c, index, to, len(passed), recv)
        copy.start()
        passed.append(copy)

    def mine(c, dy):
        return c * 2 * n_y + dy

    def other(c, dy):
        return c * 2 * n_y + n_y + dy

    def collect(c):
        start, size = spans[c]
        for frm in reversed(peers):
            slot_copy(c, frm, frm).wait_recv()
        own_at = pl.ds(pl.multiple_of(head * width + start, 16), size)
        shards[own_at, :] = mm(landed[c][...], pick, TN).astype(BF16)
        for dy in (2, 1, 3) if c else (1, 3):
            push(c, head, here[dy], mine(c, n_y - dy))
        push(c, head, sibling, other(c, 0))
        if c == last_chunk:
            for dy in (2, 1, 3):
                push(c, head, there[dy], other(c, n_y - dy))

    def hand_over(c, dy):
        shard_copy(c, here[dy], sibling, 0, mine(c, dy)).wait_recv()
        push(c, here[dy], sibling, other(c, dy))

    def products(c):
        start, size = spans[c]
        if c == last_chunk:
            for dy in range(1, n_y):
                shard_copy(c, here[dy], sibling, 0, mine(c, dy)).wait_recv()
        for dy in range(n_y):
            shard_copy(c, there[dy], sibling, 0, other(c, dy)).wait_recv()
        at_rows = [slice(i * width + start, i * width + start + size) for i in range(n_head)]
        part = jnp.concatenate([shards[r, :] for r in at_rows], axis=0).T

        def chunk(ref):
            return jnp.concatenate([ref[r, :] for r in at_rows], axis=0)

        return [mm(part, chunk(w_qkv.at[j])) for j in range(3)] + [mm(part, chunk(w_down))]

    collect(0)
    collect(1)
    hand_over(0, 1)
    push(0, here[1], here[n_y - 1], mine(0, 2))
    hand_over(0, 3)
    collect(2)
    hand_over(0, 2)
    hand_over(1, 1)
    hand_over(1, 3)
    for copy in loads[4:6]:
        copy.wait()
    sums = [acc.at[0], acc.at[1], acc.at[2], acc_low]
    for ref, value in zip(sums, products(0)):
        ref[...] = value
    hand_over(1, 2)
    for ref, value in zip(sums, products(1)):
        ref[...] = ref[...] + value
    last = [ref[...] + value for ref, value in zip(sums, products(2))]
    for j in range(3):
        ext_ref[RIM:, j * columns : (j + 1) * columns] = last[j].astype(BF16).astype(F32)
    low_rank = last[3].astype(BF16)
    rim = pltpu.make_async_remote_copy(
        src_ref=ext_ref.at[pl.ds(rows, RIM), :], dst_ref=ext_ref.at[pl.ds(0, RIM), :],
        send_sem=rim_sem.at[0], recv_sem=rim_sem.at[1],
        device_id=at(lax.rem(me + 1, n_ctx)), device_id_type=MESH,
    )
    rim.start()
    for copy in loads[6:]:
        copy.wait()

    ends, total_len = [], 0
    for i in range(lengths_ref.shape[0]):
        total_len = total_len + lengths_ref[i]
        ends.append(total_len)

    def doc_of(positions):
        ended = sum((positions >= end).astype(jnp.int32) for end in ends)
        return jnp.where(positions < 0, -1, ended)

    pos = base + lax.broadcasted_iota(jnp.int32, (rows, channels), 0)
    doc = doc_of(pos)
    valid = [None] + [(doc_of(pos - shift) == doc).astype(F32) for shift in range(1, CONV)]
    before = doc_of(jnp.zeros((1, channels), jnp.int32) + (base - 1))
    final = doc_of(jnp.zeros((1, channels), jnp.int32) + (base + rows - 1))
    first_doc = (doc == before).astype(F32)
    last_doc = (doc == final).astype(F32)
    carry = (final == before).astype(F32)
    row = lax.broadcasted_iota(jnp.int32, (rows, rows), 0)
    col = lax.broadcasted_iota(jnp.int32, (rows, rows), 1)
    col_doc = doc_of(base + lax.broadcasted_iota(jnp.int32, (1, rows), 1))
    same = jnp.concatenate([doc, doc], axis=1) == col_doc
    strict = (row > col) & same
    inclusive = (row >= col) & same
    apart = row ^ col
    running = ((row >= col) & (apart < SPAN)).astype(F32).astype(BF16)
    small_row = lax.broadcasted_iota(jnp.int32, (SPAN, rows), 0)
    small_col = lax.broadcasted_iota(jnp.int32, (SPAN, rows), 1)
    small_apart = small_row ^ (small_col & (SPAN - 1))
    small_block = small_col // SPAN
    small_eye = (small_apart == 0).astype(F32)

    every = range(heads)
    nothing = jnp.zeros((1, channels), F32)

    def of_head(v, h):
        return v[:, h * channels : (h + 1) * channels]

    def block(v, b):
        return v[b * SPAN : (b + 1) * SPAN]

    def activated(j, first, size):
        lanes = slice(j * columns, (j + 1) * columns)
        out = None
        for tap in range(CONV):
            shift = CONV - 1 - tap
            part = conv_ref[j, tap : tap + 1, :] * ext_ref[pl.ds(RIM - shift + first, size), lanes]
            if shift:
                part = part * jnp.concatenate([valid[shift][first : first + size]] * heads, axis=1)
            out = part if out is None else out + part
        grown = 1.0 + jnp.exp(jnp.minimum(-out, 80.0))
        inverted = pl.reciprocal(grown, approx=True)
        return out * (inverted * (2.0 - grown * inverted))

    def unit(v):
        return v * lax.rsqrt(jnp.sum(v * v, axis=-1, keepdims=True) + 1e-06)

    def activations(first, size):
        query, key, value = [activated(j, first, size) for j in range(3)]
        return (
            [unit(of_head(query, h)) * channels ** (-0.5) for h in every],
            [unit(of_head(key, h)) for h in every],
            [of_head(value, h) for h in every],
        )

    drive = mm(low_rank, up_ref[...]) + bias_ref[...]
    soft = jnp.maximum(drive, 0.0) + jnp.log(1.0 + jnp.exp(-jnp.abs(drive)))
    rates = jnp.concatenate([jnp.exp(jnp.full((1, channels), rate_ref[h], F32)) for h in every], axis=1)
    decay = -rates * soft
    d_high, d_mid = split(decay)
    d_low = (decay - d_high.astype(F32) - d_mid.astype(F32)).astype(BF16)
    cum_all = mm(running, d_high) + (mm(running, d_mid) + mm(running, d_low))
    logits = mm(wbeta_buf[...], shards[...])
    logits = jnp.concatenate([logits, jnp.zeros((8 - heads, rows), F32)], axis=0).T
    betas = 1.0 / (1.0 + jnp.exp(-logits))
    cums = [of_head(cum_all, h) for h in every]
    strengths = [jnp.broadcast_to(betas[:, h : h + 1], (rows, channels)) for h in every]
    lasts = [[cums[h][(b + 1) * SPAN - 1 : (b + 1) * SPAN] for b in range(blocks)] for h in every]
    grows = [jnp.exp(c) for c in cums]
    shrinks = [jnp.exp(-c) for c in cums]
    fades = [
        jnp.concatenate([jnp.exp(lasts[h][b] - block(cums[h], b)) for b in range(blocks)], axis=0)
        for h in every
    ]
    later_rows = activations(SPAN, rows - SPAN)
    rim.wait_recv()
    first_rows = activations(0, SPAN)
    queries, keys, values = [
        [jnp.concatenate([a, b], axis=0) for a, b in zip(f, l)] for f, l in zip(first_rows, later_rows)
    ]
    values = [strengths[h] * values[h] for h in every]

    lower, score, solved = [], [], []
    bk_ups, q_ups, tails = [], [], []
    for h in every:
        bk_ups.append(strengths[h] * keys[h] * grows[h])
        q_ups.append(queries[h] * grows[h])
        key_down = keys[h] * shrinks[h]
        tail = keys[h] * fades[h]
        tails.append([block(tail, b) for b in range(blocks)])
        mixes, reads = [], []
        for i in range(blocks):
            cols = []
            for b in range(blocks):
                if b < i - 1:
                    cols.append(tails[h][b] * jnp.exp(sum(lasts[h][b + 1 : i], nothing)))
                elif b == i - 1:
                    cols.append(tails[h][b])
                elif b == i:
                    cols.append(block(key_down, b))
                else:
                    cols.append(jnp.zeros((SPAN, channels), F32))
            left = split(jnp.concatenate([block(bk_ups[h], i), block(q_ups[h], i)], axis=0))
            product = mm3_narrow(left, split(jnp.concatenate(cols, axis=0)), NT)
            mixes.append(jnp.where(block(strict, i), product[:SPAN], 0.0))
            reads.append(jnp.where(block(inclusive, i), product[SPAN:], 0.0))
        lower.append(mixes)
        score.append(reads)

    def spread(v):
        return tuple(
            jnp.concatenate([jnp.where(small_block == b, part, 0.0).astype(BF16) for b in range(blocks)], axis=0)
            for part in split(v)
        )

    def times(lefts, rights):
        return [mm3(split(a), spread(b)) for a, b in zip(lefts, rights)]

    diagonal = []
    for h in every:
        picked = jnp.zeros((SPAN, rows), F32)
        for b in range(blocks):
            picked = jnp.where(small_block == b, lower[h][b], picked)
        diagonal.append(picked)
    power = [jnp.where(small_apart < 8, d, 0.0) for d in diagonal]
    inverse = [small_eye - p for p in power]
    power = times(power, power)
    inverse = [i + t for i, t in zip(inverse, times(inverse, power))]
    power = times(power, power)
    inverse = [i + t for i, t in zip(inverse, times(inverse, power))]
    size = 8
    while size < SPAN:
        off = [jnp.where((small_apart >= size) & (small_apart < 2 * size), d, 0.0) for d in diagonal]
        inverse = [i - t for i, t in zip(inverse, times(inverse, times(off, inverse)))]
        size *= 2

    full_keys, full_queries, ends_k, keeps = [], [], [], []
    for h in every:
        prefix = nothing
        k_rows, q_rows, t_rows = [], [], []
        for b in range(blocks):
            scale = jnp.exp(prefix)
            k_rows.append(block(bk_ups[h], b) * scale)
            q_rows.append(block(q_ups[h], b) * scale)
            prefix = prefix + lasts[h][b]
            t_rows.append(tails[h][b] * jnp.exp(sum(lasts[h][b + 1 :], nothing)))
        full_keys.append(jnp.concatenate(k_rows, axis=0) * first_doc)
        full_queries.append(jnp.concatenate(q_rows, axis=0) * first_doc)
        ends_k.append(split(jnp.concatenate(t_rows, axis=0) * last_doc))
        keeps.append(carry * jnp.exp(prefix))
    rights = [jnp.concatenate([full_keys[h], values[h]], axis=1) for h in every]
    done = [[] for _ in every]
    for i in range(blocks):
        rest = []
        for h in every:
            part = block(rights[h], i)
            if i:
                seen = tuple(jnp.concatenate([d[k] for d in done[h]], axis=0) for k in range(2))
                part = part - mm3(split(lower[h][i][:, : i * SPAN]), seen)
            rest.append(split(part))
        for h in every:
            own = split(inverse[h][:, i * SPAN : (i + 1) * SPAN])
            done[h].append(split(mm3(own, rest[h])))
    solved = [tuple(jnp.concatenate([d[k] for d in done[h]], axis=0) for k in range(2)) for h in every]

    eye_channels = (
        lax.broadcasted_iota(jnp.int32, (channels, channels), 0)
        == lax.broadcasted_iota(jnp.int32, (channels, channels), 1)
    ).astype(F32)
    keep_at, late_at = half + channels, half + channels + KEEP
    message = late_at

    def keep_rows(keep):
        high, middle = split(keep)
        low = (keep - high.astype(F32) - middle.astype(F32)).astype(BF16)
        return jnp.concatenate([high, middle, low, jnp.zeros((KEEP - 3, channels), BF16)], axis=0)

    def keep_of(rows3):
        wide = rows3.astype(F32)
        return wide[0:1] + (wide[1:2] + wide[2:3])

    for h in every:
        summary = mm3(solved[h], ends_k[h], TN).astype(BF16)
        stack[h, :half, :] = summary[channels : channels + half]
        stack[h, half:keep_at, :] = -summary[:channels]
        stack[h, keep_at:late_at, :] = keep_rows(keeps[h])
        stack[h, late_at:, :] = summary[channels + half :]

    mates = [(1, 2), (1, 1), (1, 3), (0, 2), (1, 0), (0, 1), (0, 3)]
    mates = [lax.rem(side + ds, 2) * X_SIZE + lax.rem(x + dx, X_SIZE) for ds, dx in mates]

    def map_copy(k, to):
        start = pl.multiple_of((to // X_SIZE) * half, half)
        return pltpu.make_async_remote_copy(
            src_ref=stack.at[lax.rem(to, X_SIZE), pl.ds(start, message), :],
            dst_ref=maps.at[member],
            send_sem=xs_sem.at[k], recv_sem=xr_sem.at[member],
            device_id=mate(to), device_id_type=MESH,
        )

    sends = [map_copy(k, to) for k, to in enumerate(mates)]
    for copy in sends:
        copy.start()
    maps[member] = stack[x, pl.ds(pl.multiple_of(side * half, half), message), :]

    for h in every:
        combined = mm3(split(jnp.concatenate(score[h], axis=0)), solved[h])
        lift[h] = full_queries[h] - combined[:, :channels]
        local[h] = combined[:, channels:]

    for frm in mates:
        pltpu.make_async_remote_copy(
            src_ref=maps.at[frm], dst_ref=maps.at[frm],
            send_sem=xs_sem.at[0], recv_sem=xr_sem.at[frm],
            device_id=mate(frm), device_id_type=MESH,
        ).wait_recv()

    map_at = pl.ds(pl.multiple_of((1 - side) * half, half), channels)
    keeps_at = pl.ds(pl.multiple_of(channels + (1 - side) * half, 16), KEEP)
    feed_at = pl.ds(pl.multiple_of(side * (channels + KEEP), 16), half)

    def apply(v, keep, exact_map):
        parts = jnp.concatenate(split(v), axis=1)
        return v * keep + mm(parts, jnp.concatenate([exact_map, exact_map], axis=0))

    def follow(whole, j):
        moved = apply(whole, step_keeps[j], maps[j, map_at, :])
        return jnp.concatenate([moved[:channels], moved[channels:] + maps[j, feed_at, :].astype(F32)], axis=0)

    def single(j):
        return jnp.concatenate(
            [step_keeps[j] * eye_channels + maps[j, map_at, :].astype(F32), maps[j, feed_at, :].astype(F32)], axis=0
        )

    def join(first, second):
        moved = mm3_narrow(split(first), split(second[:channels]))
        return jnp.concatenate([moved[:channels], moved[channels:] + second[channels:]], axis=0)

    step_keeps = [keep_of(maps[j, keeps_at, :]) for j in range(GROUP)]
    prefixes = [single(0)]
    late = [single(X_SIZE)]
    for j in range(1, X_SIZE):
        prefixes.append(follow(prefixes[-1], j))
        late.append(follow(late[-1], X_SIZE + j))
    group_total = join(prefixes[-1], late[-1])
    group_keep = functools.reduce(lambda a, b: a * b, step_keeps)
    total[:channels, :] = (group_total[:channels] - group_keep * eye_channels).astype(BF16)
    total[channels : channels + KEEP, :] = keep_rows(group_keep)
    total[channels + KEEP :, :] = group_total[channels:].astype(BF16)
    whole_span, feed_span = pl.ds(0, message), pl.ds(channels + KEEP, half)

    def total_copy(k, only_feed):
        span = feed_span if only_feed else whole_span
        return pltpu.make_async_remote_copy(
            src_ref=total.at[span, :], dst_ref=others.at[group, span, :],
            send_sem=zs_sem.at[k], recv_sem=zr_sem.at[group],
            device_id=at(lax.rem(me + k * GROUP, n_ctx)), device_id_type=MESH,
        )

    def for_later_groups(act):
        for k in sorted(range(1, n_groups), key=lambda k: -min(k, n_groups - k)):
            @pl.when((group > 0) & (group + k < n_groups))
            def _():
                act(total_copy(k, False))

        @pl.when(group == 0)
        def _():
            for k in range(1, n_groups):
                act(total_copy(k, True))

    for_later_groups(lambda copy: copy.start())
    for j in range(X_SIZE - 1):
        prefixes.append(join(prefixes[X_SIZE - 1], late[j]))
    into = split(jnp.concatenate([p[:channels] for p in prefixes], axis=1))

    state[...] = jnp.zeros_like(state)
    for frm in range(n_groups - 1):
        @pl.when(group > frm)
        def _():
            span = whole_span if frm else feed_span
            pltpu.make_async_remote_copy(
                src_ref=total.at[span, :], dst_ref=others.at[frm, span, :],
                send_sem=zs_sem.at[0], recv_sem=zr_sem.at[frm],
                device_id=at(lax.rem(me + GROUP, n_ctx)), device_id_type=MESH,
            ).wait_recv()
            feed = others[frm, feed_span, :].astype(F32)
            if frm:
                keep = keep_of(others[frm, pl.ds(channels, KEEP), :])
                feed = feed + apply(state[...], keep, others[frm, pl.ds(0, channels), :])
            state[...] = feed

    start_state = state[...]
    moved = mm3_narrow(split(start_state), into)
    entry_out[0] = start_state.astype(BF16)
    for j in range(1, GROUP):
        there_state = moved[:, (j - 1) * channels : j * channels] + prefixes[j - 1][channels:]
        entry_out[j] = there_state.astype(BF16)

    def entry_copy(k, to):
        return pltpu.make_async_remote_copy(
            src_ref=entry_out.at[to], dst_ref=entry.at[member],
            send_sem=bs_sem.at[k], recv_sem=br_sem.at[member],
            device_id=mate(to), device_id_type=MESH,
        )

    returns = [entry_copy(k, to) for k, to in enumerate(mates)]
    for copy in returns:
        copy.start()
    entry[member] = entry_out[member]
    for frm in mates:
        pltpu.make_async_remote_copy(
            src_ref=entry_out.at[frm], dst_ref=entry.at[frm],
            send_sem=bs_sem.at[0], recv_sem=br_sem.at[frm],
            device_id=mate(frm), device_id_type=MESH,
        ).wait_recv()

    for h in every:
        incoming = jnp.concatenate([entry[h], entry[X_SIZE + h]], axis=0)
        parts = jnp.concatenate(split(lift[h]), axis=1)
        result = local[h] + mm(parts, jnp.concatenate([incoming, incoming], axis=1), NT)
        mean = jnp.mean(result * result, axis=-1, keepdims=True)
        scaled = result * lax.rsqrt(mean + 1e-05) * gain_ref[...]
        out_ref[:, h * channels : (h + 1) * channels] = scaled.astype(BF16)

    for c in range(len(spans)):
        for to in peers:
            slot_copy(c, to, me).wait_send()
    for copy in passed + sends + returns:
        copy.wait_send()
    rim.wait_send()
    for_later_groups(lambda copy: copy.wait_send())


def on_device(
    hidden, qkv_weight, conv_weight, w_beta, gate_down, gate_up,
    a_log, dt_bias, norm_gain, prompt_lengths, send_slot, gather_src,
):
    rows, width = hidden.shape
    _, features, columns = qkv_weight.shape
    n_ctx, n_head = lax.axis_size("ctx"), lax.axis_size("head")
    n_y, n_groups = n_head // CORES, n_ctx // GROUP
    heads, channels = a_log.shape[0], norm_gain.shape[0]
    rank = gate_down.shape[1]
    half = channels // 2
    message = channels + KEEP + half
    slots = 2 * rows
    pieces = [pltpu.VMEM((slots, min(LANES, width - start)), BF16) for start in range(0, width, LANES)]
    dma = pltpu.SemaphoreType.DMA
    call = pl.pallas_call(
        fused_kernel,
        out_shape=jax.ShapeDtypeStruct((rows, columns), BF16),
        in_specs=[SMEM, SMEM] + [HBM] * 10,
        out_specs=VMEM,
        scratch_shapes=[
            pltpu.VMEM((1, rows), jnp.int32),
            pltpu.VMEM((1, rows), jnp.int32),
            pltpu.VMEM((width, rows), BF16),
            pltpu.VMEM((3, features, columns), BF16),
            pltpu.VMEM((features, rank), BF16),
            pltpu.VMEM((heads, features), BF16),
            pltpu.VMEM((3, CONV, columns), F32),
            pltpu.VMEM((rank, columns), BF16),
            pltpu.VMEM((1, columns), F32),
            pltpu.VMEM((1, channels), F32),
            *pieces,
            *pieces,
            pltpu.VMEM((features, rows), BF16),
            pltpu.VMEM((3, rows, columns), F32),
            pltpu.VMEM((rows, rank), F32),
            pltpu.VMEM((RIM + rows, 3 * columns), F32),
            pltpu.VMEM((heads, 2 * channels + KEEP, channels), BF16),
            pltpu.VMEM((heads, rows, channels), F32),
            pltpu.VMEM((heads, rows, channels), F32),
            pltpu.VMEM((GROUP, message, channels), BF16),
            pltpu.VMEM((message, channels), BF16),
            pltpu.VMEM((n_groups, message, channels), BF16),
            pltpu.VMEM((half, channels), F32),
            pltpu.VMEM((GROUP, half, channels), BF16),
            pltpu.VMEM((GROUP, half, channels), BF16),
            dma((10,)), dma((3 * n_ctx,)), dma((3 * n_ctx,)), dma((21,)), dma((6 * n_y,)), dma((2,)),
            dma((GROUP,)), dma((GROUP,)), dma((n_groups,)), dma((n_groups,)), dma((GROUP,)), dma((GROUP,)),
        ],
        compiler_params=pltpu.CompilerParams(
            collective_id=0, has_side_effects=True, vmem_limit_bytes=48 * 1024 * 1024
        ),
        name="delta_prefill",
    )
    operands = (
        prompt_lengths, a_log, send_slot.reshape(1, rows), gather_src.reshape(1, rows), hidden.T,
        qkv_weight, gate_down, w_beta.T, conv_weight.transpose(1, 0, 2), gate_up,
        dt_bias.reshape(1, columns), norm_gain.reshape(1, channels),
    )
    return call(*[pltpu.with_memory_space_constraint(v, pltpu.HBM) for v in operands])


def solution(mesh):
    placed = (
        P("ctx", "head"),
        P(None, None, "head"),
        P(None, None, "head"),
        P(None, "head"),
        P(),
        P(None, "head"),
        P("head"),
        P("head"),
        P(),
        P(),
        P("ctx"),
        P("ctx"),
    )
    return jax.shard_map(
        on_device, mesh=mesh, in_specs=placed, out_specs=P("ctx", "head"), check_vma=False
    )
```

```python
import functools

import jax
import jax.numpy as jnp
from jax import lax
from jax.experimental import pallas as pl
from jax.experimental.pallas import tpu as pltpu
from jax.sharding import PartitionSpec as P

CONV = 4
SPAN = 64
RIM = 8
X_SIZE = 4
CORES = 2
GROUP = 8
KEEP = 16
LANES = 128
MESH = pl.DeviceIdType.MESH
F32 = jnp.float32
BF16 = jnp.bfloat16
VMEM = pl.BlockSpec(memory_space=pltpu.VMEM)
SMEM = pl.BlockSpec(memory_space=pltpu.SMEM)
HBM = pl.BlockSpec(memory_space=pltpu.HBM)

NN = (((1,), (0,)), ((), ()))
NT = (((1,), (1,)), ((), ()))
TN = (((0,), (0,)), ((), ()))


def mm(a, b, dims=NN):
    return lax.dot_general(a, b, dims, preferred_element_type=F32)


def split(v):
    high = v.astype(BF16)
    return high, (v - high.astype(F32)).astype(BF16)


def mm3(a, b, dims=NN):
    axis = 1 - dims[0][0][0]
    count = a[0].shape[axis]
    both = mm(jnp.concatenate(a, axis=axis), b[0], dims)
    return both[:count] + (both[count:] + mm(a[0], b[1], dims))


def mm3_narrow(a, b, dims=NN):
    axis = dims[0][1][0]
    wide = mm(jnp.concatenate(a, axis=1), jnp.concatenate([b[0], b[0]], axis=axis), dims)
    return wide + mm(a[0], b[1], dims)


def fused_kernel(
    lengths_ref, rate_ref, slot_hbm, src_hbm, hidden_hbm, wqkv_hbm, wdown_hbm, wbeta_hbm,
    conv_hbm, up_hbm, bias_hbm, gain_hbm,
    out_ref,
    slot_buf, src_buf, hidden_buf, w_qkv, w_down, wbeta_buf, conv_ref, up_ref, bias_ref, gain_ref,
    send_a, send_b, send_c, landed_a, landed_b, landed_c, shards, acc, acc_low, ext_ref,
    stack, local, lift, maps, total, others, state, entry_out, entry,
    in_sem, s_sem, r_sem, hs_sem, hr_sem, rim_sem,
    xs_sem, xr_sem, zs_sem, zr_sem, bs_sem, br_sem,
):
    n_ctx = lax.axis_size("ctx")
    n_z = n_ctx // X_SIZE
    n_head = lax.axis_size("head")
    n_y = n_head // CORES
    n_groups = n_ctx // GROUP
    me = lax.axis_index("ctx")
    head = lax.axis_index("head")
    z, own_x = me // X_SIZE, lax.rem(me, X_SIZE)
    y, core = head // CORES, lax.rem(head, CORES)
    sibling = y * CORES + (1 - core)
    member = lax.rem(me, GROUP)
    group = me // GROUP
    x, side = lax.rem(member, X_SIZE), member // X_SIZE
    width, rows = hidden_buf.shape
    slots = send_a.shape[0]
    cap = slots // n_ctx
    heads, _, channels = local.shape
    columns = heads * channels
    half = channels // 2
    blocks = rows // SPAN
    base = me * rows

    def at(ctx):
        return {"ctx": ctx, "head": head}

    def mate(index):
        return at(group * GROUP + index)

    operands = [
        (slot_hbm, slot_buf), (hidden_hbm, hidden_buf), (src_hbm, src_buf), (wbeta_hbm, wbeta_buf),
        (wqkv_hbm, w_qkv), (wdown_hbm, w_down),
        (up_hbm, up_ref), (bias_hbm, bias_ref), (conv_hbm, conv_ref), (gain_hbm, gain_ref),
    ]
    loads = [pltpu.make_async_copy(a, b, in_sem.at[i]) for i, (a, b) in enumerate(operands)]
    for copy in loads[:4]:
        copy.start()

    far = sorted(
        ((dz, dx) for dz in range(n_z) for dx in range(X_SIZE) if dz or dx),
        key=lambda d: -(min(d[0], n_z - d[0]) * 2 + min(d[1], X_SIZE - d[1])),
    )
    peers = [lax.rem(z + dz, n_z) * X_SIZE + lax.rem(own_x + dx, X_SIZE) for dz, dx in far]
    ring = {dy: lax.rem(y + dy, n_y) for dy in range(n_y)}

    barrier = pltpu.get_barrier_semaphore()
    for to in peers:
        pl.semaphore_signal(barrier, inc=1, device_id=at(to), device_id_type=MESH)
    here = [ring[dy] * CORES + core for dy in range(n_y)]
    there = [ring[dy] * CORES + (1 - core) for dy in range(n_y)]
    for to in here[1:] + there:
        pl.semaphore_signal(barrier, inc=1, device_id={"ctx": me, "head": to}, device_id_type=MESH)

    for copy in loads[:4]:
        copy.wait()
    slot_ids = lax.broadcasted_iota(jnp.int32, (slots, rows), 0)
    place = (slot_ids == slot_buf[...]).astype(F32).astype(BF16)
    spans, start = [], 0
    while start < width:
        spans.append((start, min(LANES, width - start)))
        start += LANES
    sent, landed = (send_a, send_b, send_c), (landed_a, landed_b, landed_c)

    def fill(c):
        start, size = spans[c]
        sent[c][...] = mm(place, hidden_buf[start : start + size, :], NT).astype(BF16)

    fill(0)

    pl.semaphore_wait(barrier, n_ctx - 1 + n_head - 1)

    def slots_of(index):
        return pl.ds(pl.multiple_of(index * cap, cap), cap)

    def slot_copy(c, to, frm):
        return pltpu.make_async_remote_copy(
            src_ref=sent[c].at[slots_of(to), :], dst_ref=landed[c].at[slots_of(frm), :],
            send_sem=s_sem.at[c * n_ctx + to], recv_sem=r_sem.at[c * n_ctx + frm],
            device_id=at(to), device_id_type=MESH,
        )

    for c in range(len(spans)):
        if c:
            fill(c)
        for to in peers:
            slot_copy(c, to, me).start()
    for copy in loads[4:]:
        copy.start()
    pick = (slot_ids == src_buf[...]).astype(F32).astype(BF16)
    for c in range(len(spans)):
        landed[c][slots_of(me), :] = sent[c][slots_of(me), :]

    passed = []
    last_chunk = len(spans) - 1

    def shard_copy(c, index, to, send, recv):
        start, size = spans[c]
        rows_at = pl.ds(pl.multiple_of(index * width + start, 16), size)
        return pltpu.make_async_remote_copy(
            src_ref=shards.at[rows_at, :], dst_ref=shards.at[rows_at, :],
            send_sem=hs_sem.at[send], recv_sem=hr_sem.at[recv],
            device_id={"ctx": me, "head": to}, device_id_type=MESH,
        )

    def push(c, index, to, recv):
        copy = shard_copy(c, index, to, len(passed), recv)
        copy.start()
        passed.append(copy)

    def mine(c, dy):
        return c * 2 * n_y + dy

    def other(c, dy):
        return c * 2 * n_y + n_y + dy

    def collect(c):
        start, size = spans[c]
        for frm in reversed(peers):
            slot_copy(c, frm, frm).wait_recv()
        own_at = pl.ds(pl.multiple_of(head * width + start, 16), size)
        shards[own_at, :] = mm(landed[c][...], pick, TN).astype(BF16)
        for dy in (2, 1, 3) if c else (1, 3):
            push(c, head, here[dy], mine(c, n_y - dy))
        push(c, head, sibling, other(c, 0))
        if c == last_chunk:
            for dy in (2, 1, 3):
                push(c, head, there[dy], other(c, n_y - dy))

    def hand_over(c, dy):
        shard_copy(c, here[dy], sibling, 0, mine(c, dy)).wait_recv()
        push(c, here[dy], sibling, other(c, dy))

    def products(c):
        start, size = spans[c]
        if c == last_chunk:
            for dy in range(1, n_y):
                shard_copy(c, here[dy], sibling, 0, mine(c, dy)).wait_recv()
        for dy in range(n_y):
            shard_copy(c, there[dy], sibling, 0, other(c, dy)).wait_recv()
        at_rows = [slice(i * width + start, i * width + start + size) for i in range(n_head)]
        part = jnp.concatenate([shards[r, :] for r in at_rows], axis=0).T

        def chunk(ref):
            return jnp.concatenate([ref[r, :] for r in at_rows], axis=0)

        return [mm(part, chunk(w_qkv.at[j])) for j in range(3)] + [mm(part, chunk(w_down))]

    collect(0)
    collect(1)
    hand_over(0, 1)
    push(0, here[1], here[n_y - 1], mine(0, 2))
    hand_over(0, 3)
    collect(2)
    hand_over(0, 2)
    hand_over(1, 1)
    hand_over(1, 3)
    for copy in loads[4:6]:
        copy.wait()
    sums = [acc.at[0], acc.at[1], acc.at[2], acc_low]
    for ref, value in zip(sums, products(0)):
        ref[...] = value
    hand_over(1, 2)
    for ref, value in zip(sums, products(1)):
        ref[...] = ref[...] + value
    last = [ref[...] + value for ref, value in zip(sums, products(2))]
    for j in range(3):
        ext_ref[RIM:, j * columns : (j + 1) * columns] = last[j].astype(BF16).astype(F32)
    low_rank = last[3].astype(BF16)
    rim = pltpu.make_async_remote_copy(
        src_ref=ext_ref.at[pl.ds(rows, RIM), :], dst_ref=ext_ref.at[pl.ds(0, RIM), :],
        send_sem=rim_sem.at[0], recv_sem=rim_sem.at[1],
        device_id=at(lax.rem(me + 1, n_ctx)), device_id_type=MESH,
    )
    rim.start()
    for copy in loads[6:]:
        copy.wait()

    ends, total_len = [], 0
    for i in range(lengths_ref.shape[0]):
        total_len = total_len + lengths_ref[i]
        ends.append(total_len)

    def doc_of(positions):
        ended = sum((positions >= end).astype(jnp.int32) for end in ends)
        return jnp.where(positions < 0, -1, ended)

    pos = base + lax.broadcasted_iota(jnp.int32, (rows, channels), 0)
    doc = doc_of(pos)
    valid = [None] + [(doc_of(pos - shift) == doc).astype(F32) for shift in range(1, CONV)]
    before = doc_of(jnp.zeros((1, channels), jnp.int32) + (base - 1))
    final = doc_of(jnp.zeros((1, channels), jnp.int32) + (base + rows - 1))
    first_doc = (doc == before).astype(F32)
    last_doc = (doc == final).astype(F32)
    carry = (final == before).astype(F32)
    row = lax.broadcasted_iota(jnp.int32, (rows, rows), 0)
    col = lax.broadcasted_iota(jnp.int32, (rows, rows), 1)
    col_doc = doc_of(base + lax.broadcasted_iota(jnp.int32, (1, rows), 1))
    same = jnp.concatenate([doc, doc], axis=1) == col_doc
    strict = (row > col) & same
    inclusive = (row >= col) & same
    apart = row ^ col
    running = ((row >= col) & (apart < SPAN)).astype(F32).astype(BF16)
    small_row = lax.broadcasted_iota(jnp.int32, (SPAN, rows), 0)
    small_col = lax.broadcasted_iota(jnp.int32, (SPAN, rows), 1)
    small_apart = small_row ^ (small_col & (SPAN - 1))
    small_block = small_col // SPAN
    small_eye = (small_apart == 0).astype(F32)

    every = range(heads)
    nothing = jnp.zeros((1, channels), F32)

    def of_head(v, h):
        return v[:, h * channels : (h + 1) * channels]

    def block(v, b):
        return v[b * SPAN : (b + 1) * SPAN]

    def activated(j, first, size):
        lanes = slice(j * columns, (j + 1) * columns)
        out = None
        for tap in range(CONV):
            shift = CONV - 1 - tap
            part = conv_ref[j, tap : tap + 1, :] * ext_ref[pl.ds(RIM - shift + first, size), lanes]
            if shift:
                part = part * jnp.concatenate([valid[shift][first : first + size]] * heads, axis=1)
            out = part if out is None else out + part
        grown = 1.0 + jnp.exp(jnp.minimum(-out, 80.0))
        inverted = pl.reciprocal(grown, approx=True)
        return out * (inverted * (2.0 - grown * inverted))

    def unit(v):
        return v * lax.rsqrt(jnp.sum(v * v, axis=-1, keepdims=True) + 1e-06)

    def activations(first, size):
        query, key, value = [activated(j, first, size) for j in range(3)]
        return (
            [unit(of_head(query, h)) * channels ** (-0.5) for h in every],
            [unit(of_head(key, h)) for h in every],
            [of_head(value, h) for h in every],
        )

    drive = mm(low_rank, up_ref[...]) + bias_ref[...]
    soft = jnp.maximum(drive, 0.0) + jnp.log(1.0 + jnp.exp(-jnp.abs(drive)))
    rates = jnp.concatenate([jnp.exp(jnp.full((1, channels), rate_ref[h], F32)) for h in every], axis=1)
    decay = -rates * soft
    d_high, d_mid = split(decay)
    d_low = (decay - d_high.astype(F32) - d_mid.astype(F32)).astype(BF16)
    cum_all = mm(running, d_high) + (mm(running, d_mid) + mm(running, d_low))
    logits = mm(wbeta_buf[...], shards[...])
    logits = jnp.concatenate([logits, jnp.zeros((8 - heads, rows), F32)], axis=0).T
    betas = 1.0 / (1.0 + jnp.exp(-logits))
    cums = [of_head(cum_all, h) for h in every]
    strengths = [jnp.broadcast_to(betas[:, h : h + 1], (rows, channels)) for h in every]
    lasts = [[cums[h][(b + 1) * SPAN - 1 : (b + 1) * SPAN] for b in range(blocks)] for h in every]
    grows = [jnp.exp(c) for c in cums]
    shrinks = [jnp.exp(-c) for c in cums]
    fades = [
        jnp.concatenate([jnp.exp(lasts[h][b] - block(cums[h], b)) for b in range(blocks)], axis=0)
        for h in every
    ]
    later_rows = activations(SPAN, rows - SPAN)
    rim.wait_recv()
    first_rows = activations(0, SPAN)
    queries, keys, values = [
        [jnp.concatenate([a, b], axis=0) for a, b in zip(f, l)] for f, l in zip(first_rows, later_rows)
    ]
    values = [strengths[h] * values[h] for h in every]

    lower, score, solved = [], [], []
    bk_ups, q_ups, tails = [], [], []
    for h in every:
        bk_ups.append(strengths[h] * keys[h] * grows[h])
        q_ups.append(queries[h] * grows[h])
        key_down = keys[h] * shrinks[h]
        tail = keys[h] * fades[h]
        tails.append([block(tail, b) for b in range(blocks)])
        mixes, reads = [], []
        for i in range(blocks):
            cols = []
            for b in range(blocks):
                if b < i - 1:
                    cols.append(tails[h][b] * jnp.exp(sum(lasts[h][b + 1 : i], nothing)))
                elif b == i - 1:
                    cols.append(tails[h][b])
                elif b == i:
                    cols.append(block(key_down, b))
                else:
                    cols.append(jnp.zeros((SPAN, channels), F32))
            left = split(jnp.concatenate([block(bk_ups[h], i), block(q_ups[h], i)], axis=0))
            product = mm3_narrow(left, split(jnp.concatenate(cols, axis=0)), NT)
            mixes.append(jnp.where(block(strict, i), product[:SPAN], 0.0))
            reads.append(jnp.where(block(inclusive, i), product[SPAN:], 0.0))
        lower.append(mixes)
        score.append(reads)

    def spread(v):
        return tuple(
            jnp.concatenate([jnp.where(small_block == b, part, 0.0).astype(BF16) for b in range(blocks)], axis=0)
            for part in split(v)
        )

    def times(lefts, rights):
        return [mm3(split(a), spread(b)) for a, b in zip(lefts, rights)]

    diagonal = []
    for h in every:
        picked = jnp.zeros((SPAN, rows), F32)
        for b in range(blocks):
            picked = jnp.where(small_block == b, lower[h][b], picked)
        diagonal.append(picked)
    power = [jnp.where(small_apart < 8, d, 0.0) for d in diagonal]
    inverse = [small_eye - p for p in power]
    power = times(power, power)
    inverse = [i + t for i, t in zip(inverse, times(inverse, power))]
    power = times(power, power)
    inverse = [i + t for i, t in zip(inverse, times(inverse, power))]
    size = 8
    while size < SPAN:
        off = [jnp.where((small_apart >= size) & (small_apart < 2 * size), d, 0.0) for d in diagonal]
        inverse = [i - t for i, t in zip(inverse, times(inverse, times(off, inverse)))]
        size *= 2

    full_keys, full_queries, ends_k, keeps = [], [], [], []
    for h in every:
        prefix = nothing
        k_rows, q_rows, t_rows = [], [], []
        for b in range(blocks):
            scale = jnp.exp(prefix)
            k_rows.append(block(bk_ups[h], b) * scale)
            q_rows.append(block(q_ups[h], b) * scale)
            prefix = prefix + lasts[h][b]
            t_rows.append(tails[h][b] * jnp.exp(sum(lasts[h][b + 1 :], nothing)))
        full_keys.append(jnp.concatenate(k_rows, axis=0) * first_doc)
        full_queries.append(jnp.concatenate(q_rows, axis=0) * first_doc)
        ends_k.append(split(jnp.concatenate(t_rows, axis=0) * last_doc))
        keeps.append(carry * jnp.exp(prefix))
    rights = [jnp.concatenate([full_keys[h], values[h]], axis=1) for h in every]
    done = [[] for _ in every]
    for i in range(blocks):
        rest = []
        for h in every:
            part = block(rights[h], i)
            if i:
                seen = tuple(jnp.concatenate([d[k] for d in done[h]], axis=0) for k in range(2))
                part = part - mm3(split(lower[h][i][:, : i * SPAN]), seen)
            rest.append(split(part))
        for h in every:
            own = split(inverse[h][:, i * SPAN : (i + 1) * SPAN])
            done[h].append(split(mm3(own, rest[h])))
    solved = [tuple(jnp.concatenate([d[k] for d in done[h]], axis=0) for k in range(2)) for h in every]

    eye_channels = (
        lax.broadcasted_iota(jnp.int32, (channels, channels), 0)
        == lax.broadcasted_iota(jnp.int32, (channels, channels), 1)
    ).astype(F32)
    keep_at, late_at = half + channels, half + channels + KEEP
    message = late_at

    def keep_rows(keep):
        high, middle = split(keep)
        low = (keep - high.astype(F32) - middle.astype(F32)).astype(BF16)
        return jnp.concatenate([high, middle, low, jnp.zeros((KEEP - 3, channels), BF16)], axis=0)

    def keep_of(rows3):
        wide = rows3.astype(F32)
        return wide[0:1] + (wide[1:2] + wide[2:3])

    for h in every:
        summary = mm3(solved[h], ends_k[h], TN).astype(BF16)
        stack[h, :half, :] = summary[channels : channels + half]
        stack[h, half:keep_at, :] = -summary[:channels]
        stack[h, keep_at:late_at, :] = keep_rows(keeps[h])
        stack[h, late_at:, :] = summary[channels + half :]

    mates = [(1, 2), (1, 1), (1, 3), (0, 2), (1, 0), (0, 1), (0, 3)]
    mates = [lax.rem(side + ds, 2) * X_SIZE + lax.rem(x + dx, X_SIZE) for ds, dx in mates]

    def map_copy(k, to):
        start = pl.multiple_of((to // X_SIZE) * half, half)
        return pltpu.make_async_remote_copy(
            src_ref=stack.at[lax.rem(to, X_SIZE), pl.ds(start, message), :],
            dst_ref=maps.at[member],
            send_sem=xs_sem.at[k], recv_sem=xr_sem.at[member],
            device_id=mate(to), device_id_type=MESH,
        )

    sends = [map_copy(k, to) for k, to in enumerate(mates)]
    for copy in sends:
        copy.start()
    maps[member] = stack[x, pl.ds(pl.multiple_of(side * half, half), message), :]

    for h in every:
        combined = mm3(split(jnp.concatenate(score[h], axis=0)), solved[h])
        lift[h] = jnp.concatenate(split(full_queries[h] - combined[:, :channels]), axis=1)
        local[h] = combined[:, channels:]

    for c in range(len(spans)):
        for to in peers:
            slot_copy(c, to, me).wait_send()
    for copy in passed:
        copy.wait_send()
    rim.wait_send()

    for frm in mates:
        pltpu.make_async_remote_copy(
            src_ref=maps.at[frm], dst_ref=maps.at[frm],
            send_sem=xs_sem.at[0], recv_sem=xr_sem.at[frm],
            device_id=mate(frm), device_id_type=MESH,
        ).wait_recv()

    map_at = pl.ds(pl.multiple_of((1 - side) * half, half), channels)
    keeps_at = pl.ds(pl.multiple_of(channels + (1 - side) * half, 16), KEEP)
    feed_at = pl.ds(pl.multiple_of(side * (channels + KEEP), 16), half)

    def apply(v, keep, exact_map):
        parts = jnp.concatenate(split(v), axis=1)
        return v * keep + mm(parts, jnp.concatenate([exact_map, exact_map], axis=0))

    def follow(whole, j):
        moved = apply(whole, step_keeps[j], maps[j, map_at, :])
        return jnp.concatenate([moved[:channels], moved[channels:] + maps[j, feed_at, :].astype(F32)], axis=0)

    def single(j):
        return jnp.concatenate(
            [step_keeps[j] * eye_channels + maps[j, map_at, :].astype(F32), maps[j, feed_at, :].astype(F32)], axis=0
        )

    def join(first, second):
        moved = mm3_narrow(split(first), split(second[:channels]))
        return jnp.concatenate([moved[:channels], moved[channels:] + second[channels:]], axis=0)

    step_keeps = [keep_of(maps[j, keeps_at, :]) for j in range(GROUP)]
    prefixes = [single(0)]
    late = [single(X_SIZE)]
    for j in range(1, X_SIZE):
        prefixes.append(follow(prefixes[-1], j))
        late.append(follow(late[-1], X_SIZE + j))
    group_total = join(prefixes[-1], late[-1])
    group_keep = functools.reduce(lambda a, b: a * b, step_keeps)
    total[:channels, :] = (group_total[:channels] - group_keep * eye_channels).astype(BF16)
    total[channels : channels + KEEP, :] = keep_rows(group_keep)
    total[channels + KEEP :, :] = group_total[channels:].astype(BF16)
    whole_span, feed_span = pl.ds(0, message), pl.ds(channels + KEEP, half)

    def total_copy(k, only_feed):
        span = feed_span if only_feed else whole_span
        return pltpu.make_async_remote_copy(
            src_ref=total.at[span, :], dst_ref=others.at[group, span, :],
            send_sem=zs_sem.at[k], recv_sem=zr_sem.at[group],
            device_id=at(lax.rem(me + k * GROUP, n_ctx)), device_id_type=MESH,
        )

    def for_later_groups(act):
        for k in sorted(range(1, n_groups), key=lambda k: -min(k, n_groups - k)):
            @pl.when((group > 0) & (group + k < n_groups))
            def _():
                act(total_copy(k, False))

        @pl.when(group == 0)
        def _():
            for k in range(1, n_groups):
                act(total_copy(k, True))

    for_later_groups(lambda copy: copy.start())
    for j in range(X_SIZE - 1):
        prefixes.append(join(prefixes[X_SIZE - 1], late[j]))
    into = split(jnp.concatenate([p[:channels] for p in prefixes], axis=1))

    state[...] = jnp.zeros_like(state)
    for frm in range(n_groups - 1):
        @pl.when(group > frm)
        def _():
            span = whole_span if frm else feed_span
            pltpu.make_async_remote_copy(
                src_ref=total.at[span, :], dst_ref=others.at[frm, span, :],
                send_sem=zs_sem.at[0], recv_sem=zr_sem.at[frm],
                device_id=at(lax.rem(me + GROUP, n_ctx)), device_id_type=MESH,
            ).wait_recv()
            feed = others[frm, feed_span, :].astype(F32)
            if frm:
                keep = keep_of(others[frm, pl.ds(channels, KEEP), :])
                feed = feed + apply(state[...], keep, others[frm, pl.ds(0, channels), :])
            state[...] = feed

    start_state = state[...]
    moved = mm3_narrow(split(start_state), into)
    entry_out[0] = start_state.astype(BF16)
    for j in range(1, GROUP):
        there_state = moved[:, (j - 1) * channels : j * channels] + prefixes[j - 1][channels:]
        entry_out[j] = there_state.astype(BF16)

    def entry_copy(k, to):
        return pltpu.make_async_remote_copy(
            src_ref=entry_out.at[to], dst_ref=entry.at[member],
            send_sem=bs_sem.at[k], recv_sem=br_sem.at[member],
            device_id=mate(to), device_id_type=MESH,
        )

    returns = [entry_copy(k, to) for k, to in enumerate(mates)]
    for copy in returns:
        copy.start()
    entry[member] = entry_out[member]
    for copy in sends:
        copy.wait_send()
    for_later_groups(lambda copy: copy.wait_send())
    for frm in mates:
        pltpu.make_async_remote_copy(
            src_ref=entry_out.at[frm], dst_ref=entry.at[frm],
            send_sem=bs_sem.at[0], recv_sem=br_sem.at[frm],
            device_id=mate(frm), device_id_type=MESH,
        ).wait_recv()

    for h in every:
        incoming = jnp.concatenate([entry[h], entry[X_SIZE + h]], axis=0)
        result = local[h] + mm(lift[h], jnp.concatenate([incoming, incoming], axis=1), NT)
        mean = jnp.mean(result * result, axis=-1, keepdims=True)
        scaled = result * lax.rsqrt(mean + 1e-05) * gain_ref[...]
        out_ref[:, h * channels : (h + 1) * channels] = scaled.astype(BF16)

    for copy in returns:
        copy.wait_send()


def on_device(
    hidden, qkv_weight, conv_weight, w_beta, gate_down, gate_up,
    a_log, dt_bias, norm_gain, prompt_lengths, send_slot, gather_src,
):
    rows, width = hidden.shape
    _, features, columns = qkv_weight.shape
    n_ctx, n_head = lax.axis_size("ctx"), lax.axis_size("head")
    n_y, n_groups = n_head // CORES, n_ctx // GROUP
    heads, channels = a_log.shape[0], norm_gain.shape[0]
    rank = gate_down.shape[1]
    half = channels // 2
    message = channels + KEEP + half
    slots = 2 * rows
    pieces = [pltpu.VMEM((slots, min(LANES, width - start)), BF16) for start in range(0, width, LANES)]
    dma = pltpu.SemaphoreType.DMA
    call = pl.pallas_call(
        fused_kernel,
        out_shape=jax.ShapeDtypeStruct((rows, columns), BF16),
        in_specs=[SMEM, SMEM] + [HBM] * 10,
        out_specs=VMEM,
        scratch_shapes=[
            pltpu.VMEM((1, rows), jnp.int32),
            pltpu.VMEM((1, rows), jnp.int32),
            pltpu.VMEM((width, rows), BF16),
            pltpu.VMEM((3, features, columns), BF16),
            pltpu.VMEM((features, rank), BF16),
            pltpu.VMEM((heads, features), BF16),
            pltpu.VMEM((3, CONV, columns), F32),
            pltpu.VMEM((rank, columns), BF16),
            pltpu.VMEM((1, columns), F32),
            pltpu.VMEM((1, channels), F32),
            *pieces,
            *pieces,
            pltpu.VMEM((features, rows), BF16),
            pltpu.VMEM((3, rows, columns), F32),
            pltpu.VMEM((rows, rank), F32),
            pltpu.VMEM((RIM + rows, 3 * columns), F32),
            pltpu.VMEM((heads, 2 * channels + KEEP, channels), BF16),
            pltpu.VMEM((heads, rows, channels), F32),
            pltpu.VMEM((heads, rows, 2 * channels), BF16),
            pltpu.VMEM((GROUP, message, channels), BF16),
            pltpu.VMEM((message, channels), BF16),
            pltpu.VMEM((n_groups, message, channels), BF16),
            pltpu.VMEM((half, channels), F32),
            pltpu.VMEM((GROUP, half, channels), BF16),
            pltpu.VMEM((GROUP, half, channels), BF16),
            dma((10,)), dma((3 * n_ctx,)), dma((3 * n_ctx,)), dma((21,)), dma((6 * n_y,)), dma((2,)),
            dma((GROUP,)), dma((GROUP,)), dma((n_groups,)), dma((n_groups,)), dma((GROUP,)), dma((GROUP,)),
        ],
        compiler_params=pltpu.CompilerParams(
            collective_id=0, has_side_effects=True, vmem_limit_bytes=48 * 1024 * 1024
        ),
        name="delta_prefill",
    )
    operands = (
        prompt_lengths, a_log, send_slot.reshape(1, rows), gather_src.reshape(1, rows), hidden.T,
        qkv_weight, gate_down, w_beta.T, conv_weight.transpose(1, 0, 2), gate_up,
        dt_bias.reshape(1, columns), norm_gain.reshape(1, channels),
    )
    return call(*[pltpu.with_memory_space_constraint(v, pltpu.HBM) for v in operands])


def solution(mesh):
    placed = (
        P("ctx", "head"),
        P(None, None, "head"),
        P(None, None, "head"),
        P(None, "head"),
        P(),
        P(None, "head"),
        P("head"),
        P("head"),
        P(),
        P(),
        P("ctx"),
        P("ctx"),
    )
    return jax.shard_map(
        on_device, mesh=mesh, in_specs=placed, out_specs=P("ctx", "head"), check_vma=False
    )
```

```python
import functools

import jax
import jax.numpy as jnp
from jax import lax
from jax.experimental import pallas as pl
from jax.experimental.pallas import tpu as pltpu
from jax.sharding import PartitionSpec as P

CONV = 4
SPAN = 64
RIM = 8
X_SIZE = 4
CORES = 2
GROUP = 8
KEEP = 16
LANES = 128
MESH = pl.DeviceIdType.MESH
F32 = jnp.float32
BF16 = jnp.bfloat16
VMEM = pl.BlockSpec(memory_space=pltpu.VMEM)
SMEM = pl.BlockSpec(memory_space=pltpu.SMEM)
HBM = pl.BlockSpec(memory_space=pltpu.HBM)

NN = (((1,), (0,)), ((), ()))
NT = (((1,), (1,)), ((), ()))
TN = (((0,), (0,)), ((), ()))


def mm(a, b, dims=NN):
    return lax.dot_general(a, b, dims, preferred_element_type=F32)


def split(v):
    high = v.astype(BF16)
    return high, (v - high.astype(F32)).astype(BF16)


def mm3(a, b, dims=NN):
    axis = 1 - dims[0][0][0]
    count = a[0].shape[axis]
    both = mm(jnp.concatenate(a, axis=axis), b[0], dims)
    return both[:count] + (both[count:] + mm(a[0], b[1], dims))


def mm3_narrow(a, b, dims=NN):
    axis = dims[0][1][0]
    wide = mm(jnp.concatenate(a, axis=1), jnp.concatenate([b[0], b[0]], axis=axis), dims)
    return wide + mm(a[0], b[1], dims)


def fused_kernel(
    lengths_ref, rate_ref, slot_hbm, src_hbm, hidden_hbm, wqkv_hbm, wdown_hbm, wbeta_hbm,
    conv_hbm, up_hbm, bias_hbm, gain_hbm,
    out_ref,
    slot_buf, src_buf, hidden_buf, w_qkv, w_down, wbeta_buf, conv_ref, up_ref, bias_ref, gain_ref,
    send_a, send_b, send_c, landed_a, landed_b, landed_c, shards, acc, acc_low, ext_ref,
    stack, local, lift, maps, total, others, state, entry_out, entry,
    in_sem, s_sem, r_sem, hs_sem, hr_sem, rim_sem,
    xs_sem, xr_sem, zs_sem, zr_sem, bs_sem, br_sem,
):
    n_ctx = lax.axis_size("ctx")
    n_z = n_ctx // X_SIZE
    n_head = lax.axis_size("head")
    n_y = n_head // CORES
    n_groups = n_ctx // GROUP
    me = lax.axis_index("ctx")
    head = lax.axis_index("head")
    z, own_x = me // X_SIZE, lax.rem(me, X_SIZE)
    y, core = head // CORES, lax.rem(head, CORES)
    sibling = y * CORES + (1 - core)
    member = lax.rem(me, GROUP)
    group = me // GROUP
    x, side = lax.rem(member, X_SIZE), member // X_SIZE
    width, rows = hidden_buf.shape
    slots = send_a.shape[0]
    cap = slots // n_ctx
    heads, _, channels = local.shape
    columns = heads * channels
    half = channels // 2
    blocks = rows // SPAN
    base = me * rows

    def at(ctx):
        return {"ctx": ctx, "head": head}

    def mate(index):
        return at(group * GROUP + index)

    operands = [
        (slot_hbm, slot_buf), (hidden_hbm, hidden_buf), (src_hbm, src_buf), (wbeta_hbm, wbeta_buf),
        (wqkv_hbm, w_qkv), (wdown_hbm, w_down),
        (up_hbm, up_ref), (bias_hbm, bias_ref), (conv_hbm, conv_ref), (gain_hbm, gain_ref),
    ]
    loads = [pltpu.make_async_copy(a, b, in_sem.at[i]) for i, (a, b) in enumerate(operands)]
    for copy in loads[:4]:
        copy.start()

    far = sorted(
        ((dz, dx) for dz in range(n_z) for dx in range(X_SIZE) if dz or dx),
        key=lambda d: -(min(d[0], n_z - d[0]) * 2 + min(d[1], X_SIZE - d[1])),
    )
    peers = [lax.rem(z + dz, n_z) * X_SIZE + lax.rem(own_x + dx, X_SIZE) for dz, dx in far]
    ring = {dy: lax.rem(y + dy, n_y) for dy in range(n_y)}

    barrier = pltpu.get_barrier_semaphore()
    for to in peers:
        pl.semaphore_signal(barrier, inc=1, device_id=at(to), device_id_type=MESH)
    here = [ring[dy] * CORES + core for dy in range(n_y)]
    there = [ring[dy] * CORES + (1 - core) for dy in range(n_y)]
    for to in here[1:] + there:
        pl.semaphore_signal(barrier, inc=1, device_id={"ctx": me, "head": to}, device_id_type=MESH)

    for copy in loads[:4]:
        copy.wait()
    slot_ids = lax.broadcasted_iota(jnp.int32, (slots, rows), 0)
    place = (slot_ids == slot_buf[...]).astype(F32).astype(BF16)
    spans, start = [], 0
    while start < width:
        spans.append((start, min(LANES, width - start)))
        start += LANES
    sent, landed = (send_a, send_b, send_c), (landed_a, landed_b, landed_c)

    def fill(c):
        start, size = spans[c]
        sent[c][...] = mm(place, hidden_buf[start : start + size, :], NT).astype(BF16)

    fill(0)

    pl.semaphore_wait(barrier, n_ctx - 1 + n_head - 1)

    def slots_of(index):
        return pl.ds(pl.multiple_of(index * cap, cap), cap)

    def slot_copy(c, to, frm):
        return pltpu.make_async_remote_copy(
            src_ref=sent[c].at[slots_of(to), :], dst_ref=landed[c].at[slots_of(frm), :],
            send_sem=s_sem.at[c * n_ctx + to], recv_sem=r_sem.at[c * n_ctx + frm],
            device_id=at(to), device_id_type=MESH,
        )

    for c in range(len(spans)):
        if c:
            fill(c)
        for to in peers:
            slot_copy(c, to, me).start()
    for copy in loads[4:]:
        copy.start()
    pick = (slot_ids == src_buf[...]).astype(F32).astype(BF16)
    for c in range(len(spans)):
        landed[c][slots_of(me), :] = sent[c][slots_of(me), :]

    passed = []
    last_chunk = len(spans) - 1

    def shard_copy(c, index, to, send, recv):
        start, size = spans[c]
        rows_at = pl.ds(pl.multiple_of(index * width + start, 16), size)
        return pltpu.make_async_remote_copy(
            src_ref=shards.at[rows_at, :], dst_ref=shards.at[rows_at, :],
            send_sem=hs_sem.at[send], recv_sem=hr_sem.at[recv],
            device_id={"ctx": me, "head": to}, device_id_type=MESH,
        )

    def push(c, index, to, recv):
        copy = shard_copy(c, index, to, len(passed), recv)
        copy.start()
        passed.append(copy)

    def mine(c, dy):
        return c * 2 * n_y + dy

    def other(c, dy):
        return c * 2 * n_y + n_y + dy

    def collect(c):
        start, size = spans[c]
        for frm in reversed(peers):
            slot_copy(c, frm, frm).wait_recv()
        own_at = pl.ds(pl.multiple_of(head * width + start, 16), size)
        shards[own_at, :] = mm(landed[c][...], pick, TN).astype(BF16)
        for dy in (2, 1, 3) if c else (1, 3):
            push(c, head, here[dy], mine(c, n_y - dy))
        push(c, head, sibling, other(c, 0))
        if c == last_chunk:
            for dy in (2, 1, 3):
                push(c, head, there[dy], other(c, n_y - dy))

    def hand_over(c, dy):
        shard_copy(c, here[dy], sibling, 0, mine(c, dy)).wait_recv()
        push(c, here[dy], sibling, other(c, dy))

    def products(c):
        start, size = spans[c]
        if c == last_chunk:
            for dy in range(1, n_y):
                shard_copy(c, here[dy], sibling, 0, mine(c, dy)).wait_recv()
        for dy in range(n_y):
            shard_copy(c, there[dy], sibling, 0, other(c, dy)).wait_recv()
        at_rows = [slice(i * width + start, i * width + start + size) for i in range(n_head)]
        part = jnp.concatenate([shards[r, :] for r in at_rows], axis=0).T

        def chunk(ref):
            return jnp.concatenate([ref[r, :] for r in at_rows], axis=0)

        return [mm(part, chunk(w_qkv.at[j])) for j in range(3)] + [mm(part, chunk(w_down))]

    collect(0)
    collect(1)
    hand_over(0, 1)
    push(0, here[1], here[n_y - 1], mine(0, 2))
    hand_over(0, 3)
    collect(2)
    hand_over(0, 2)
    hand_over(1, 1)
    hand_over(1, 3)
    for copy in loads[4:6]:
        copy.wait()
    sums = [acc.at[0], acc.at[1], acc.at[2], acc_low]
    for ref, value in zip(sums, products(0)):
        ref[...] = value
    hand_over(1, 2)
    for ref, value in zip(sums, products(1)):
        ref[...] = ref[...] + value
    last = [ref[...] + value for ref, value in zip(sums, products(2))]
    for j in range(3):
        ext_ref[RIM:, j * columns : (j + 1) * columns] = last[j].astype(BF16).astype(F32)
    low_rank = last[3].astype(BF16)
    rim = pltpu.make_async_remote_copy(
        src_ref=ext_ref.at[pl.ds(rows, RIM), :], dst_ref=ext_ref.at[pl.ds(0, RIM), :],
        send_sem=rim_sem.at[0], recv_sem=rim_sem.at[1],
        device_id=at(lax.rem(me + 1, n_ctx)), device_id_type=MESH,
    )
    rim.start()
    for copy in loads[6:]:
        copy.wait()

    ends, total_len = [], 0
    for i in range(lengths_ref.shape[0]):
        total_len = total_len + lengths_ref[i]
        ends.append(total_len)

    def doc_of(positions):
        ended = sum((positions >= end).astype(jnp.int32) for end in ends)
        return jnp.where(positions < 0, -1, ended)

    pos = base + lax.broadcasted_iota(jnp.int32, (rows, channels), 0)
    doc = doc_of(pos)
    valid = [None] + [(doc_of(pos - shift) == doc).astype(F32) for shift in range(1, CONV)]
    before = doc_of(jnp.zeros((1, channels), jnp.int32) + (base - 1))
    final = doc_of(jnp.zeros((1, channels), jnp.int32) + (base + rows - 1))
    first_doc = (doc == before).astype(F32)
    last_doc = (doc == final).astype(F32)
    carry = (final == before).astype(F32)
    row = lax.broadcasted_iota(jnp.int32, (rows, rows), 0)
    col = lax.broadcasted_iota(jnp.int32, (rows, rows), 1)
    col_doc = doc_of(base + lax.broadcasted_iota(jnp.int32, (1, rows), 1))
    same = jnp.concatenate([doc, doc], axis=1) == col_doc
    strict = (row > col) & same
    inclusive = (row >= col) & same
    apart = row ^ col
    running = ((row >= col) & (apart < SPAN)).astype(F32).astype(BF16)
    small_row = lax.broadcasted_iota(jnp.int32, (SPAN, rows), 0)
    small_col = lax.broadcasted_iota(jnp.int32, (SPAN, rows), 1)
    small_apart = small_row ^ (small_col & (SPAN - 1))
    small_block = small_col // SPAN
    small_eye = (small_apart == 0).astype(F32)

    every = range(heads)
    nothing = jnp.zeros((1, channels), F32)

    def of_head(v, h):
        return v[:, h * channels : (h + 1) * channels]

    def block(v, b):
        return v[b * SPAN : (b + 1) * SPAN]

    def activated(j, first, size):
        lanes = slice(j * columns, (j + 1) * columns)
        out = None
        for tap in range(CONV):
            shift = CONV - 1 - tap
            part = conv_ref[j, tap : tap + 1, :] * ext_ref[pl.ds(RIM - shift + first, size), lanes]
            if shift:
                part = part * jnp.concatenate([valid[shift][first : first + size]] * heads, axis=1)
            out = part if out is None else out + part
        grown = 1.0 + jnp.exp(jnp.minimum(-out, 80.0))
        inverted = pl.reciprocal(grown, approx=True)
        return out * (inverted * (2.0 - grown * inverted))

    def unit(v):
        return v * lax.rsqrt(jnp.sum(v * v, axis=-1, keepdims=True) + 1e-06)

    def activations(first, size):
        query, key, value = [activated(j, first, size) for j in range(3)]
        return (
            [unit(of_head(query, h)) * channels ** (-0.5) for h in every],
            [unit(of_head(key, h)) for h in every],
            [of_head(value, h) for h in every],
        )

    drive = mm(low_rank, up_ref[...]) + bias_ref[...]
    soft = jnp.maximum(drive, 0.0) + jnp.log(1.0 + jnp.exp(-jnp.abs(drive)))
    rates = jnp.concatenate([jnp.exp(jnp.full((1, channels), rate_ref[h], F32)) for h in every], axis=1)
    decay = -rates * soft
    d_high, d_mid = split(decay)
    d_low = (decay - d_high.astype(F32) - d_mid.astype(F32)).astype(BF16)
    cum_all = mm(running, d_high) + (mm(running, d_mid) + mm(running, d_low))
    logits = mm(wbeta_buf[...], shards[...])[:8].T
    betas = 1.0 / (1.0 + jnp.exp(-logits))
    cums = [of_head(cum_all, h) for h in every]
    strengths = [jnp.broadcast_to(betas[:, h : h + 1], (rows, channels)) for h in every]
    lasts = [[cums[h][(b + 1) * SPAN - 1 : (b + 1) * SPAN] for b in range(blocks)] for h in every]
    grows = [jnp.exp(c) for c in cums]
    shrinks = [jnp.exp(-c) for c in cums]
    fades = [
        jnp.concatenate([jnp.exp(lasts[h][b] - block(cums[h], b)) for b in range(blocks)], axis=0)
        for h in every
    ]
    later_rows = activations(SPAN, rows - SPAN)
    rim.wait_recv()
    first_rows = activations(0, SPAN)
    queries, keys, values = [
        [jnp.concatenate([a, b], axis=0) for a, b in zip(f, l)] for f, l in zip(first_rows, later_rows)
    ]
    values = [strengths[h] * values[h] for h in every]

    lower, score, solved = [], [], []
    bk_ups, q_ups, tails = [], [], []
    for h in every:
        bk_ups.append(strengths[h] * keys[h] * grows[h])
        q_ups.append(queries[h] * grows[h])
        key_down = keys[h] * shrinks[h]
        tail = keys[h] * fades[h]
        tails.append([block(tail, b) for b in range(blocks)])
        mixes, reads = [], []
        for i in range(blocks):
            cols = []
            for b in range(blocks):
                if b < i - 1:
                    cols.append(tails[h][b] * jnp.exp(sum(lasts[h][b + 1 : i], nothing)))
                elif b == i - 1:
                    cols.append(tails[h][b])
                elif b == i:
                    cols.append(block(key_down, b))
                else:
                    cols.append(jnp.zeros((SPAN, channels), F32))
            left = split(jnp.concatenate([block(bk_ups[h], i), block(q_ups[h], i)], axis=0))
            product = mm3_narrow(left, split(jnp.concatenate(cols, axis=0)), NT)
            mixes.append(jnp.where(block(strict, i), product[:SPAN], 0.0))
            reads.append(jnp.where(block(inclusive, i), product[SPAN:], 0.0))
        lower.append(mixes)
        score.append(reads)

    def spread(v):
        return tuple(
            jnp.concatenate([jnp.where(small_block == b, part, 0.0).astype(BF16) for b in range(blocks)], axis=0)
            for part in split(v)
        )

    def times(lefts, rights):
        return [mm3(split(a), spread(b)) for a, b in zip(lefts, rights)]

    diagonal = []
    for h in every:
        picked = jnp.zeros((SPAN, rows), F32)
        for b in range(blocks):
            picked = jnp.where(small_block == b, lower[h][b], picked)
        diagonal.append(picked)
    power = [jnp.where(small_apart < 8, d, 0.0) for d in diagonal]
    inverse = [small_eye - p for p in power]
    power = times(power, power)
    inverse = [i + t for i, t in zip(inverse, times(inverse, power))]
    power = times(power, power)
    inverse = [i + t for i, t in zip(inverse, times(inverse, power))]
    size = 8
    while size < SPAN:
        off = [jnp.where((small_apart >= size) & (small_apart < 2 * size), d, 0.0) for d in diagonal]
        inverse = [i - t for i, t in zip(inverse, times(inverse, times(off, inverse)))]
        size *= 2

    full_keys, full_queries, ends_k, keeps = [], [], [], []
    for h in every:
        prefix = nothing
        k_rows, q_rows, t_rows = [], [], []
        for b in range(blocks):
            scale = jnp.exp(prefix)
            k_rows.append(block(bk_ups[h], b) * scale)
            q_rows.append(block(q_ups[h], b) * scale)
            prefix = prefix + lasts[h][b]
            t_rows.append(tails[h][b] * jnp.exp(sum(lasts[h][b + 1 :], nothing)))
        full_keys.append(jnp.concatenate(k_rows, axis=0) * first_doc)
        full_queries.append(jnp.concatenate(q_rows, axis=0) * first_doc)
        ends_k.append(split(jnp.concatenate(t_rows, axis=0) * last_doc))
        keeps.append(carry * jnp.exp(prefix))
    rights = [jnp.concatenate([full_keys[h], values[h]], axis=1) for h in every]
    done = [[] for _ in every]
    for i in range(blocks):
        rest = []
        for h in every:
            part = block(rights[h], i)
            if i:
                seen = tuple(jnp.concatenate([d[k] for d in done[h]], axis=0) for k in range(2))
                part = part - mm3(split(lower[h][i][:, : i * SPAN]), seen)
            rest.append(split(part))
        for h in every:
            own = split(inverse[h][:, i * SPAN : (i + 1) * SPAN])
            done[h].append(split(mm3(own, rest[h])))
    solved = [tuple(jnp.concatenate([d[k] for d in done[h]], axis=0) for k in range(2)) for h in every]

    eye_channels = (
        lax.broadcasted_iota(jnp.int32, (channels, channels), 0)
        == lax.broadcasted_iota(jnp.int32, (channels, channels), 1)
    ).astype(F32)
    keep_at, late_at = half + channels, half + channels + KEEP
    message = late_at

    def keep_rows(keep):
        high, middle = split(keep)
        low = (keep - high.astype(F32) - middle.astype(F32)).astype(BF16)
        return jnp.concatenate([high, middle, low, jnp.zeros((KEEP - 3, channels), BF16)], axis=0)

    def keep_of(rows3):
        wide = rows3.astype(F32)
        return wide[0:1] + (wide[1:2] + wide[2:3])

    for h in every:
        summary = mm3(solved[h], ends_k[h], TN).astype(BF16)
        stack[h, :half, :] = summary[channels : channels + half]
        stack[h, half:keep_at, :] = -summary[:channels]
        stack[h, keep_at:late_at, :] = keep_rows(keeps[h])
        stack[h, late_at:, :] = summary[channels + half :]

    mates = [(1, 2), (1, 1), (1, 3), (0, 2), (1, 0), (0, 1), (0, 3)]
    mates = [lax.rem(side + ds, 2) * X_SIZE + lax.rem(x + dx, X_SIZE) for ds, dx in mates]

    def map_copy(k, to):
        start = pl.multiple_of((to // X_SIZE) * half, half)
        return pltpu.make_async_remote_copy(
            src_ref=stack.at[lax.rem(to, X_SIZE), pl.ds(start, message), :],
            dst_ref=maps.at[member],
            send_sem=xs_sem.at[k], recv_sem=xr_sem.at[member],
            device_id=mate(to), device_id_type=MESH,
        )

    sends = [map_copy(k, to) for k, to in enumerate(mates)]
    for copy in sends:
        copy.start()
    maps[member] = stack[x, pl.ds(pl.multiple_of(side * half, half), message), :]

    for h in every:
        combined = mm3(split(jnp.concatenate(score[h], axis=0)), solved[h])
        lift[h] = jnp.concatenate(split(full_queries[h] - combined[:, :channels]), axis=1)
        local[h] = combined[:, channels:]

    for c in range(len(spans)):
        for to in peers:
            slot_copy(c, to, me).wait_send()
    for copy in passed:
        copy.wait_send()
    rim.wait_send()

    for frm in mates:
        pltpu.make_async_remote_copy(
            src_ref=maps.at[frm], dst_ref=maps.at[frm],
            send_sem=xs_sem.at[0], recv_sem=xr_sem.at[frm],
            device_id=mate(frm), device_id_type=MESH,
        ).wait_recv()

    map_at = pl.ds(pl.multiple_of((1 - side) * half, half), channels)
    keeps_at = pl.ds(pl.multiple_of(channels + (1 - side) * half, 16), KEEP)
    feed_at = pl.ds(pl.multiple_of(side * (channels + KEEP), 16), half)

    def apply(v, keep, exact_map):
        parts = jnp.concatenate(split(v), axis=1)
        return v * keep + mm(parts, jnp.concatenate([exact_map, exact_map], axis=0))

    def follow(whole, j):
        moved = apply(whole, step_keeps[j], maps[j, map_at, :])
        return jnp.concatenate([moved[:channels], moved[channels:] + maps[j, feed_at, :].astype(F32)], axis=0)

    def single(j):
        return jnp.concatenate(
            [step_keeps[j] * eye_channels + maps[j, map_at, :].astype(F32), maps[j, feed_at, :].astype(F32)], axis=0
        )

    def join(first, second):
        moved = mm3_narrow(split(first), split(second[:channels]))
        return jnp.concatenate([moved[:channels], moved[channels:] + second[channels:]], axis=0)

    step_keeps = [keep_of(maps[j, keeps_at, :]) for j in range(GROUP)]
    prefixes = [single(0)]
    late = [single(X_SIZE)]
    for j in range(1, X_SIZE):
        prefixes.append(follow(prefixes[-1], j))
        late.append(follow(late[-1], X_SIZE + j))
    group_total = join(prefixes[-1], late[-1])
    group_keep = functools.reduce(lambda a, b: a * b, step_keeps)
    total[:channels, :] = (group_total[:channels] - group_keep * eye_channels).astype(BF16)
    total[channels : channels + KEEP, :] = keep_rows(group_keep)
    total[channels + KEEP :, :] = group_total[channels:].astype(BF16)
    whole_span, feed_span = pl.ds(0, message), pl.ds(channels + KEEP, half)

    def total_copy(k, only_feed):
        span = feed_span if only_feed else whole_span
        return pltpu.make_async_remote_copy(
            src_ref=total.at[span, :], dst_ref=others.at[group, span, :],
            send_sem=zs_sem.at[k], recv_sem=zr_sem.at[group],
            device_id=at(lax.rem(me + k * GROUP, n_ctx)), device_id_type=MESH,
        )

    def for_later_groups(act):
        for k in sorted(range(1, n_groups), key=lambda k: -min(k, n_groups - k)):
            @pl.when((group > 0) & (group + k < n_groups))
            def _():
                act(total_copy(k, False))

        @pl.when(group == 0)
        def _():
            for k in range(1, n_groups):
                act(total_copy(k, True))

    for_later_groups(lambda copy: copy.start())
    for j in range(X_SIZE - 1):
        prefixes.append(join(prefixes[X_SIZE - 1], late[j]))
    into = split(jnp.concatenate([p[:channels] for p in prefixes], axis=1))

    state[...] = jnp.zeros_like(state)
    for frm in range(n_groups - 1):
        @pl.when(group > frm)
        def _():
            span = whole_span if frm else feed_span
            pltpu.make_async_remote_copy(
                src_ref=total.at[span, :], dst_ref=others.at[frm, span, :],
                send_sem=zs_sem.at[0], recv_sem=zr_sem.at[frm],
                device_id=at(lax.rem(me + GROUP, n_ctx)), device_id_type=MESH,
            ).wait_recv()
            feed = others[frm, feed_span, :].astype(F32)
            if frm:
                keep = keep_of(others[frm, pl.ds(channels, KEEP), :])
                feed = feed + apply(state[...], keep, others[frm, pl.ds(0, channels), :])
            state[...] = feed

    start_state = state[...]
    moved = mm3_narrow(split(start_state), into)
    entry_out[0] = start_state.astype(BF16)
    for j in range(1, GROUP):
        there_state = moved[:, (j - 1) * channels : j * channels] + prefixes[j - 1][channels:]
        entry_out[j] = there_state.astype(BF16)

    def entry_copy(k, to):
        return pltpu.make_async_remote_copy(
            src_ref=entry_out.at[to], dst_ref=entry.at[member],
            send_sem=bs_sem.at[k], recv_sem=br_sem.at[member],
            device_id=mate(to), device_id_type=MESH,
        )

    returns = [entry_copy(k, to) for k, to in enumerate(mates)]
    for copy in returns:
        copy.start()
    entry[member] = entry_out[member]
    for copy in sends:
        copy.wait_send()
    for_later_groups(lambda copy: copy.wait_send())
    for frm in mates:
        pltpu.make_async_remote_copy(
            src_ref=entry_out.at[frm], dst_ref=entry.at[frm],
            send_sem=bs_sem.at[0], recv_sem=br_sem.at[frm],
            device_id=mate(frm), device_id_type=MESH,
        ).wait_recv()

    for h in every:
        incoming = jnp.concatenate([entry[h], entry[X_SIZE + h]], axis=0)
        result = local[h] + mm(lift[h], jnp.concatenate([incoming, incoming], axis=1), NT)
        mean = jnp.mean(result * result, axis=-1, keepdims=True)
        scaled = result * lax.rsqrt(mean + 1e-05) * gain_ref[...]
        out_ref[:, h * channels : (h + 1) * channels] = scaled.astype(BF16)

    for copy in returns:
        copy.wait_send()


def on_device(
    hidden, qkv_weight, conv_weight, w_beta, gate_down, gate_up,
    a_log, dt_bias, norm_gain, prompt_lengths, send_slot, gather_src,
):
    rows, width = hidden.shape
    _, features, columns = qkv_weight.shape
    n_ctx, n_head = lax.axis_size("ctx"), lax.axis_size("head")
    n_y, n_groups = n_head // CORES, n_ctx // GROUP
    heads, channels = a_log.shape[0], norm_gain.shape[0]
    rank = gate_down.shape[1]
    half = channels // 2
    message = channels + KEEP + half
    slots = 2 * rows
    pieces = [pltpu.VMEM((slots, min(LANES, width - start)), BF16) for start in range(0, width, LANES)]
    dma = pltpu.SemaphoreType.DMA
    call = pl.pallas_call(
        fused_kernel,
        out_shape=jax.ShapeDtypeStruct((rows, columns), BF16),
        in_specs=[SMEM, SMEM] + [HBM] * 10,
        out_specs=VMEM,
        scratch_shapes=[
            pltpu.VMEM((1, rows), jnp.int32),
            pltpu.VMEM((1, rows), jnp.int32),
            pltpu.VMEM((width, rows), BF16),
            pltpu.VMEM((3, features, columns), BF16),
            pltpu.VMEM((features, rank), BF16),
            pltpu.VMEM((16, features), BF16),
            pltpu.VMEM((3, CONV, columns), F32),
            pltpu.VMEM((rank, columns), BF16),
            pltpu.VMEM((1, columns), F32),
            pltpu.VMEM((1, channels), F32),
            *pieces,
            *pieces,
            pltpu.VMEM((features, rows), BF16),
            pltpu.VMEM((3, rows, columns), F32),
            pltpu.VMEM((rows, rank), F32),
            pltpu.VMEM((RIM + rows, 3 * columns), F32),
            pltpu.VMEM((heads, 2 * channels + KEEP, channels), BF16),
            pltpu.VMEM((heads, rows, channels), F32),
            pltpu.VMEM((heads, rows, 2 * channels), BF16),
            pltpu.VMEM((GROUP, message, channels), BF16),
            pltpu.VMEM((message, channels), BF16),
            pltpu.VMEM((n_groups, message, channels), BF16),
            pltpu.VMEM((half, channels), F32),
            pltpu.VMEM((GROUP, half, channels), BF16),
            pltpu.VMEM((GROUP, half, channels), BF16),
            dma((10,)), dma((3 * n_ctx,)), dma((3 * n_ctx,)), dma((21,)), dma((6 * n_y,)), dma((2,)),
            dma((GROUP,)), dma((GROUP,)), dma((n_groups,)), dma((n_groups,)), dma((GROUP,)), dma((GROUP,)),
        ],
        compiler_params=pltpu.CompilerParams(
            collective_id=0, has_side_effects=True, vmem_limit_bytes=48 * 1024 * 1024
        ),
        name="delta_prefill",
    )
    operands = (
        prompt_lengths, a_log, send_slot.reshape(1, rows), gather_src.reshape(1, rows), hidden.T,
        qkv_weight, gate_down, jnp.pad(w_beta.T, ((0, 16 - heads), (0, 0))), conv_weight.transpose(1, 0, 2), gate_up,
        dt_bias.reshape(1, columns), norm_gain.reshape(1, channels),
    )
    return call(*[pltpu.with_memory_space_constraint(v, pltpu.HBM) for v in operands])


def solution(mesh):
    placed = (
        P("ctx", "head"),
        P(None, None, "head"),
        P(None, None, "head"),
        P(None, "head"),
        P(),
        P(None, "head"),
        P("head"),
        P("head"),
        P(),
        P(),
        P("ctx"),
        P("ctx"),
    )
    return jax.shard_map(
        on_device, mesh=mesh, in_specs=placed, out_specs=P("ctx", "head"), check_vma=False
    )
```
